32 devices in a mesh: dp: 4 (over y, core), blk: 8 (over z, x).
Axes of the slice: x: 2, y: 2, z: 4, core: 2. Of those that a mesh axis runs over, the one named last changes fastest.
Arguments:
- inputs: bfloat16 [4, 4, 1024, 768], P(None, 'dp', 'blk'), may hold values from -6 to 6
- segment_ids: int32 [4, 4, 1024], P(None, 'dp', 'blk'), may hold values from 0 to 1023, as said below
- query_weight: bfloat16 [768, 768], P('dp', 'blk'), may hold values from -0.21875 to 0.21875
- query_bias: bfloat16 [768], P('blk'), may hold values from -3 to 3
- key_weight: bfloat16 [768, 768], P('dp', 'blk'), may hold values from -0.21875 to 0.21875
- value_weight: bfloat16 [768, 768], P('dp', 'blk'), may hold values from -0.21875 to 0.21875
- value_bias: bfloat16 [768], P('blk'), may hold values from -3 to 3
- output_weight: bfloat16 [768, 768], P('dp', 'blk'), may hold values from -1.25 to 1.25
- output_bias: bfloat16 [768], P('blk'), may hold values from -3 to 3
- first_gain: bfloat16 [768], P('blk'), may hold values from 0.5 to 1.5
- first_shift: bfloat16 [768], P('blk'), may hold values from -3 to 3
- up_weight: bfloat16 [768, 3072], P('dp', 'blk'), may hold values from -0.21875 to 0.21875
- up_bias: bfloat16 [3072], P('blk'), may hold values from -3 to 3
- down_weight: bfloat16 [3072, 768], P('dp', 'blk'), may hold values from -0.109375 to 0.109375
- down_bias: bfloat16 [768], P('blk'), may hold values from -3 to 3
- second_gain: bfloat16 [768], P('blk'), may hold values from 0.5 to 1.5
- second_shift: bfloat16 [768], P('blk'), may hold values from -3 to 3
- cotangent: bfloat16 [4, 4, 1024, 768], P(None, 'dp', 'blk'), may hold values from -6 to 6
Outputs:
- layer_output: bfloat16 [4, 4, 1024, 768], P(None, 'dp', 'blk')
- input_grad: bfloat16 [4, 4, 1024, 768], P(None, 'dp', 'blk')
- grad_query_weight: float32 [768, 768], P('dp', 'blk')
- grad_query_bias: float32 [768], P('blk')
- grad_key_weight: float32 [768, 768], P('dp', 'blk')
- grad_value_weight: float32 [768, 768], P('dp', 'blk')
- grad_value_bias: float32 [768], P('blk')
- grad_output_weight: float32 [768, 768], P('dp', 'blk')
- grad_output_bias: float32 [768], P('blk')
- grad_first_gain: float32 [768], P('blk')
- grad_first_shift: float32 [768], P('blk')
- grad_up_weight: float32 [768, 3072], P('dp', 'blk')
- grad_up_bias: float32 [3072], P('blk')
- grad_down_weight: float32 [3072, 768], P('dp', 'blk')
- grad_down_bias: float32 [768], P('blk')
- grad_second_gain: float32 [768], P('blk')
- grad_second_shift: float32 [768], P('blk')
The draws below stay inside these ranges and needn't reach their ends.
Inputs may be any that keep to these rules, and one draw needn't show every extreme that they name: `segment_ids`: along each row the ids never fall, and a passage is a run of equal ids. The last passage of every row has id 1024 - 1, and every other passage has a smaller id. Among the rows of one index of dp (all micro-batches), one row holds a passage that begins among the first 128 positions and ends among the last 128.
All inputs are finite; a program needn't handle non-finite values.
Results may differ from the reference program's by a relative error of at most 0.019.
Values may be sent and summed in bfloat16 or wider, within the bound.
A program may use at most 256 MiB of HBM per device.

```python
import jax
import jax.numpy as jnp
from jax import lax

D = 768
HEADS = 12
HD = 64
FF = 3072
SEQ_DEV = 128
MICRO = 4
ROWS_MB = 1
SEQ_LEN = 1024
ROWS = 4


def draw_segment_ids(key, part):
    key = jax.random.fold_in(key, 11)
    streams = jax.random.split(key, 5)
    draw_shape = (MICRO, ROWS, SEQ_LEN)
    positions = jnp.arange(SEQ_LEN, dtype=jnp.int32)
    free_starts = jax.random.randint(streams[0], draw_shape, 0, 256) == 0
    head_cut = jax.random.randint(streams[1], (MICRO, ROWS, 1), 1, SEQ_DEV)
    tail_cut = jax.random.randint(streams[2], (MICRO, ROWS, 1), 1, SEQ_DEV)
    edge_flags = jax.random.randint(streams[3], draw_shape, 0, 32) == 0
    outer_part = (positions < head_cut) | (positions >= SEQ_LEN - tail_cut)
    spanning = outer_part & edge_flags | (positions == head_cut) | (positions == SEQ_LEN - tail_cut)
    group_count = ROWS // ROWS_MB
    picked = jax.random.randint(streams[4], (group_count,), 0, MICRO * ROWS_MB)
    micro_index = jnp.arange(MICRO, dtype=jnp.int32)[:, None]
    row_index = jnp.arange(ROWS, dtype=jnp.int32)[None, :]
    slot_index = micro_index * ROWS_MB + row_index % ROWS_MB
    chosen = slot_index == picked[row_index // ROWS_MB]
    starts = jnp.where(chosen[:, :, None], spanning, free_starts)
    starts = starts & (positions > 0)
    counted = jnp.cumsum(starts.astype(jnp.int32), axis=-1).astype(jnp.int32)
    final_id = counted[:, :, -1:]
    return jnp.where(counted == final_id, SEQ_LEN - 1, counted).astype(jnp.int32)


def shard_levels(stream_key, extent, cuts, least, high):
    loudness, own = 1.0, jax.random.fold_in(stream_key, 6)
    for dim, parts in cuts:
        steps = jnp.exp(jax.random.uniform(jax.random.fold_in(own, dim), (parts,), jnp.float32, least / len(cuts), high / len(cuts)))
        loudness = loudness * jnp.repeat(steps, extent[dim] // parts).reshape([-1 if axis == dim else 1 for axis in range(len(extent))])
    return loudness


def scatter_about(rng, dims, deviation, most, pieces=(), kind=jnp.bfloat16):
    factor_of = shard_levels(rng, dims, pieces, -0.22, 0.18) if pieces else 1.0
    drawn = jax.random.normal(rng, dims, jnp.float32) * deviation * factor_of
    return jnp.minimum(jnp.maximum(drawn, -most), most).astype(kind)


def setup_inputs(seed: int = 0) -> dict:
    streams_of = jax.random.split(jax.random.key(seed), 19)
    return {
        "inputs": scatter_about(streams_of[0], (MICRO, ROWS, SEQ_LEN, D), 1.0, 6.0, ((1, 4), (2, 8))),
        "segment_ids": draw_segment_ids(jax.random.fold_in(streams_of[18], 71), 0),
        "query_weight": scatter_about(streams_of[2], (D, D), D ** -0.5, 0.21875, ((0, 4), (1, 8))),
        "query_bias": scatter_about(streams_of[3], (D,), 0.5, 3.0, ((0, 8),)),
        "key_weight": scatter_about(streams_of[4], (D, D), D ** -0.5, 0.21875, ((0, 4), (1, 8))),
        "value_weight": scatter_about(streams_of[5], (D, D), D ** -0.5, 0.21875, ((0, 4), (1, 8))),
        "value_bias": scatter_about(streams_of[6], (D,), 0.5, 3.0, ((0, 8),)),
        "output_weight": scatter_about(streams_of[7], (D, D), (D // 32) ** -0.5, 1.25, ((0, 4), (1, 8))),
        "output_bias": scatter_about(streams_of[8], (D,), 0.5, 3.0, ((0, 8),)),
        "first_gain": jnp.clip(1.0 + 0.1 * jax.random.normal(streams_of[9], (D,), jnp.float32), 0.5, 1.5).astype(jnp.bfloat16),
        "first_shift": scatter_about(streams_of[10], (D,), 0.5, 3.0, ((0, 8),)),
        "up_weight": scatter_about(streams_of[11], (D, FF), D ** -0.5, 0.21875, ((0, 4), (1, 8))),
        "up_bias": scatter_about(streams_of[12], (FF,), 0.5, 3.0, ((0, 8),)),
        "down_weight": scatter_about(streams_of[13], (FF, D), FF ** -0.5, 0.109375, ((0, 4), (1, 8))),
        "down_bias": scatter_about(streams_of[14], (D,), 0.5, 3.0, ((0, 8),)),
        "second_gain": jnp.clip(1.0 + 0.1 * jax.random.normal(streams_of[15], (D,), jnp.float32), 0.5, 1.5).astype(jnp.bfloat16),
        "second_shift": scatter_about(streams_of[16], (D,), 0.5, 3.0, ((0, 8),)),
        "cotangent": scatter_about(streams_of[17], (MICRO, ROWS, SEQ_LEN, D), 1.0, 6.0, ((1, 4), (2, 8))),
    }


EPSILON = 1e-12
NEGATIVE = -1e+30

@jax.custom_vjp
def low(v):
    return lax.optimization_barrier(v.astype(jnp.bfloat16)).astype(jnp.float32)

@jax.custom_vjp
def low_back(v):
    return v

def low_keep(v):
    return (low(v), None)

def low_pass(kept, grad):
    return (grad,)

def back_keep(v):
    return (v, None)

def back_low(kept, grad):
    return (low(grad),)
low.defvjp(low_keep, low_pass)
low_back.defvjp(back_keep, back_low)

def rounded(value):
    return low(low_back(value))

def matmul(left, right):
    return jnp.dot(left, right, precision=lax.Precision.HIGHEST, preferred_element_type=jnp.float32)

def norm_rows(hidden, gain, shift):
    centred = hidden - lax.optimization_barrier(jnp.mean(hidden, axis=-1, keepdims=True))
    normed = centred * lax.rsqrt(lax.optimization_barrier(jnp.mean(centred * centred, axis=-1, keepdims=True)) + EPSILON)
    return normed * gain + shift

def attend(queries, keys, values, passage):
    length = queries.shape[0]
    block = min(512, length)
    count = length // block
    query_blocks = queries.reshape(count, block, HEADS, HD)
    passage_blocks = passage.reshape(count, block)
    key_heads = keys.reshape(length, HEADS, HD)
    value_heads = values.reshape(length, HEADS, HD)

    def one_block(items):
        query_block, passage_block = items
        scores = jnp.einsum('qhd,khd->hqk', query_block, key_heads, precision=lax.Precision.HIGHEST) * HD ** (-0.5)
        scores = low_back(scores)
        allowed = (passage_block[:, None] == passage[None, :])[None]
        scores = jnp.where(allowed, scores, NEGATIVE)
        highest = lax.optimization_barrier(jnp.max(scores, axis=-1, keepdims=True))
        expo = jnp.exp(scores - highest)
        probs = low(expo / lax.optimization_barrier(jnp.sum(expo, axis=-1, keepdims=True)))
        return jnp.einsum('hqk,khd->qhd', probs, value_heads, precision=lax.Precision.HIGHEST)
    mixed = lax.map(jax.checkpoint(one_block), (query_blocks, passage_blocks))
    return mixed.reshape(length, HEADS * HD)

def layer_row(params, tokens_row, passage):
    query_weight, query_bias, key_weight, value_weight, value_bias, output_weight, output_bias, first_gain, first_shift, up_weight, up_bias, down_weight, down_bias, second_gain, second_shift = params
    queries = rounded(matmul(tokens_row, query_weight) + query_bias)
    keys = rounded(matmul(tokens_row, key_weight))
    values = rounded(matmul(tokens_row, value_weight) + value_bias)
    context = rounded(attend(queries, keys, values, passage))
    branch = low_back(matmul(context, output_weight) + output_bias)
    first = norm_rows(tokens_row + branch, first_gain, first_shift)
    inner = low_back(matmul(low(first), up_weight) + up_bias)
    hidden = low(jax.nn.gelu(inner, approximate=False))
    second = low_back(matmul(hidden, down_weight) + down_bias)
    return norm_rows(first + second, second_gain, second_shift)

def reference(inputs, segment_ids, query_weight, query_bias, key_weight, value_weight, value_bias, output_weight, output_bias, first_gain, first_shift, up_weight, up_bias, down_weight, down_bias, second_gain, second_shift, cotangent):
    params = tuple((member.astype(jnp.float32) for member in (query_weight, query_bias, key_weight, value_weight, value_bias, output_weight, output_bias, first_gain, first_shift, up_weight, up_bias, down_weight, down_bias, second_gain, second_shift)))
    token_rows = inputs.reshape(-1, SEQ_LEN, D).astype(jnp.float32)
    passages = segment_ids.reshape(-1, SEQ_LEN).astype(jnp.int32)
    upstream = cotangent.reshape(-1, SEQ_LEN, D).astype(jnp.float32)
    start_totals = jax.tree.map(jnp.zeros_like, params)

    def step(totals, items):
        tokens_row, passage, upstream_row = items
        result, pull = jax.vjp(lambda weights, values_row: layer_row(weights, values_row, passage), params, tokens_row)
        grad_params, grad_row = pull(upstream_row)
        totals = jax.tree.map(lambda earlier, latest: earlier + latest, totals, grad_params)
        return (totals, (result.astype(jnp.bfloat16), grad_row.astype(jnp.bfloat16)))
    totals, (results, row_grads) = lax.scan(step, start_totals, (token_rows, passages, upstream))
    return (results.reshape(inputs.shape), row_grads.reshape(inputs.shape), totals[0], totals[1], totals[2], totals[3], totals[4], totals[5], totals[6], totals[7], totals[8], totals[9], totals[10], totals[11], totals[12], totals[13], totals[14])
```

```python
from functools import partial

import jax
import jax.numpy as jnp
from jax import lax
from jax.experimental import pallas as pl
from jax.experimental.pallas import tpu as pltpu
from jax.sharding import PartitionSpec as P

MESH = pl.DeviceIdType.MESH
BF = jnp.bfloat16
F32 = jnp.float32


def place():
    dp = lax.axis_index("dp")
    blk = lax.axis_index("blk")
    return dp // 2, dp % 2, blk // 2, blk % 2


def device(y, c, z, x):
    return (y * 2 + c, z * 2 + x)


def greet_all():
    y, c, z, x = place()
    me = (y * 2 + c) * 8 + z * 2 + x
    barrier = pltpu.get_barrier_semaphore()

    def greet(i, carry):
        other = (me + i) % 32
        pl.semaphore_signal(barrier, inc=1, device_id=(other // 8, other % 8), device_id_type=MESH)
        return carry

    lax.fori_loop(1, 32, greet, 0)
    pl.semaphore_wait(barrier, 31)


XY, YX = "abxyc", "abyxc"
CHUNKS = [("t", 0, XY), ("t", 1, YX), ("t", 2, XY), ("t", 3, YX)]
for _i in range(4):
    CHUNKS += [("u", _i, XY), ("d", _i, YX)]
OFF = (1, 2, 4, 6, 7)
XT = 5


def coords():
    y, c, z, x = place()
    return {"a": z // 2, "b": z % 2, "x": x, "y": y, "c": c}


def to_device(at):
    return device(at["y"], at["c"], 2 * at["a"] + at["b"], at["x"])


def flip(at, dim):
    return {**at, dim: 1 - at[dim]}


def whole(at, dims):
    return {k: (None if k in dims else v) for k, v in at.items()}


def span(v):
    return slice(None) if v is None else v


def each(v):
    return (0, 1) if v is None else (v,)


def lanes(start, size):
    return pl.ds(start if isinstance(start, int) else pl.multiple_of(start, 128), size)


def region(refs, chunk, at):
    wt, wu, wd = refs
    kind, i, _ = chunk
    a, b, x, y, c = (at[k] for k in "abxyc")
    if kind == "t":
        cols = slice(None) if y is None else lanes(384 * y, 384)
        return [wt.at[i, span(a), span(b), span(x), span(c), :, cols]]
    if kind == "u":
        if a is None and b is None and x is None:
            return [wu.at[span(y), span(c), i]]
        return [wu.at[span(y), span(c), i, :, lanes(384 * (4 * p + 2 * q + r), 384)] for p in each(a) for q in each(b) for r in each(x)]
    return [wd.at[span(a), span(b), span(x), i // 2, :, lanes(768 * (2 * p + q) + 384 * (i % 2), 384)] for p in each(y) for q in each(c)]


def gather_kernel(
    xs, cot, seg, w4, wup, wdt, vec,
    X, C, SEG, WT, WUP, WDT, VEC,
    pair, stage,
    ps, pr, zs, zr, ls, xsnd, xrcv, xfs, xfr, csnd, crcv, ssnd, srcv, vsnd, vrcv, lsem,
):
    y, c, z, x = place()
    j = 2 * z + x
    greet_all()
    sends = []

    def remote(src, dst, send, recv, to, start=True):
        cp = pltpu.make_async_remote_copy(src_ref=src, dst_ref=dst, send_sem=send, recv_sem=recv, device_id=to, device_id_type=MESH)
        if start is True:
            cp.start()
        else:
            pl.when(start)(cp.start)
        sends.append((start, cp))
        return cp

    def arrive(dst, recv):
        pltpu.make_async_remote_copy(src_ref=dst, dst_ref=dst, send_sem=recv, recv_sem=recv, device_id=device(y, c, z, x), device_id_type=MESH).wait_recv()

    partner = device(y, 1 - c, z, x)
    first = remote(w4.at[:, pl.ds(48 * (1 - c), 48)], pair, ps, pr, partner)

    def tokens(src, dst, i, send, recv, loc):
        m = (z + i) % 4
        to = device(y, z // 2, m, c)
        mine = (z == m) & (x == c) & (z // 2 == c)
        cp = pltpu.make_async_remote_copy(src_ref=src.at[m], dst_ref=dst, send_sem=send, recv_sem=recv, device_id=to, device_id_type=MESH)
        lc = pltpu.make_async_copy(src.at[m], dst, loc)
        pl.when(jnp.logical_not(mine))(cp.start)
        pl.when(mine)(lc.start)
        return mine, cp, lc

    conds = []
    for m in range(4):
        conds.append(tokens(xs, X.at[j], m, xsnd.at[m], xrcv.at[j % 4], lsem.at[0]))
    for m in range(4):
        for k in range(2):
            to = device(y, k, m, c)
            mine = (z == m) & (x == c) & (k == c)
            cp = pltpu.make_async_remote_copy(src_ref=seg.at[m], dst_ref=SEG.at[j], send_sem=ssnd.at[2 * m + k], recv_sem=srcv.at[j], device_id=to, device_id_type=MESH)
            lc = pltpu.make_async_copy(seg.at[m], SEG.at[j], lsem.at[1])
            pl.when(jnp.logical_not(mine))(cp.start)
            pl.when(mine)(lc.start)
            conds.append((mine, cp, lc))
    own_vec = pltpu.make_async_copy(vec, VEC.at[j], lsem.at[2])
    own_vec.start()
    for d in range(1, 8):
        o = (j + d) % 8
        remote(vec, VEC.at[j], vsnd.at[d], vrcv.at[d], device(y, c, o // 2, o % 2))

    first.wait_recv()
    own = w4[:, pl.ds(pl.multiple_of(48 * c, 16), 48), :]
    got = pair[...]
    lo = jnp.where(c == 0, own, got)
    hi = jnp.where(c == 0, got, own)
    stage[...] = jnp.concatenate([lo, hi], axis=-1)

    def source(ch):
        kind, i, _ = ch
        if kind == "t":
            return stage.at[i]
        if kind == "u":
            return wup.at[i]
        return wdt.at[i // 2, :, pl.ds(384 * (i % 2), 384)]

    at = coords()
    refs = (WT, WUP, WDT)
    n = len(CHUNKS)
    locals_ = []
    for t in range(n + OFF[4]):
        if t < n:
            ch = CHUNKS[t]
            here = region(refs, ch, at)[0]
            lc = pltpu.make_async_copy(source(ch), here, ls.at[t])
            lc.start()
            locals_.append(lc)
            remote(source(ch), here, zs.at[t, 0, 0], zr.at[t, 0, 0], to_device(flip(at, ch[2][0])))
        if t == XT:
            for i in range(4):
                b = 4 * c + i
                is_mine = (b // 2 == z) & (b % 2 == x) & (c == x)

                @pl.when(jnp.logical_not(is_mine))
                def _(b=b, i=i):
                    arrive(X.at[b], xrcv.at[i])

                @pl.when(is_mine)
                def _(b=b):
                    pltpu.make_async_copy(X.at[b], X.at[b], lsem.at[0]).wait()

                remote(X.at[b], X.at[b], xfs.at[i], xfr.at[i], partner)
        if t in (4, 6, 8, 10):
            m = (t - 4) // 2
            conds.append(tokens(cot, C.at[j % 4], m, csnd.at[m], crcv.at[j % 4], lsem.at[3]))
        for s in range(5):
            u = t - OFF[s]
            if not 0 <= u < n:
                continue
            ch = CHUNKS[u]
            order = ch[2]
            if s == 0:
                locals_[u].wait()
            for k, part in enumerate(region(refs, ch, whole(flip(at, order[s]), order[:s]))):
                arrive(part, zr.at[u, s, k])
            if s < 4:
                for k, part in enumerate(region(refs, ch, whole(at, order[: s + 1]))):
                    remote(part, part, zs.at[u, s + 1, k], zr.at[u, s + 1, k], to_device(flip(at, order[s + 1])))
    for i in range(4):
        b = 4 * (1 - c) + i
        arrive(X.at[b], xfr.at[i])
        b = 4 * c + i
        is_mine = (b // 2 == z) & (b % 2 == x) & (c == x)

        @pl.when(jnp.logical_not(is_mine))
        def _(i=i):
            arrive(C.at[i], crcv.at[i])

        @pl.when(is_mine)
        def _(i=i):
            pltpu.make_async_copy(C.at[i], C.at[i], lsem.at[3]).wait()
    for b in range(8):
        is_mine = (b // 2 == z) & (b % 2 == x) & (c == x)

        @pl.when(jnp.logical_not(is_mine))
        def _(b=b):
            arrive(SEG.at[b], srcv.at[b])

        @pl.when(is_mine)
        def _(b=b):
            pltpu.make_async_copy(SEG.at[b], SEG.at[b], lsem.at[1]).wait()
    own_vec.wait()
    for d in range(1, 8):
        arrive(VEC.at[(j - d) % 8], vrcv.at[d])
    for cond, cp in sends:
        if cond is True:
            cp.wait_send()
        else:
            pl.when(cond)(cp.wait_send)
    for mine, cp, lc in conds:
        pl.when(jnp.logical_not(mine))(cp.wait_send)


def gather_call(xs, cot, seg, w4, wup, wdt, vec):
    any_ = pl.BlockSpec(memory_space=pl.ANY)
    vm = pl.BlockSpec(memory_space=pltpu.VMEM)
    n = len(CHUNKS)
    S = pltpu.SemaphoreType.DMA
    return pl.pallas_call(
        gather_kernel,
        out_shape=[
            jax.ShapeDtypeStruct((8, 128, 768), BF),
            jax.ShapeDtypeStruct((4, 128, 768), BF),
            jax.ShapeDtypeStruct((8, 1, 128), jnp.int32),
            jax.ShapeDtypeStruct((4, 2, 2, 2, 2, 48, 768), BF),
            jax.ShapeDtypeStruct((2, 2, 4, 48, 3072), BF),
            jax.ShapeDtypeStruct((2, 2, 2, 2, 48, 3072), BF),
            jax.ShapeDtypeStruct((8, 16, 384), BF),
        ],
        in_specs=[any_, any_, vm, vm, vm, vm, vm],
        out_specs=[any_] * 7,
        scratch_shapes=[
            pltpu.VMEM((4, 48, 192), BF),
            pltpu.VMEM((4, 48, 384), BF),
            S, S, S((n, 5, 4)), S((n, 5, 4)), S((n,)),
            S((4,)), S((4,)), S((4,)), S((4,)), S((4,)), S((4,)), S((8,)), S((8,)), S((8,)), S((8,)), S((4,)),
        ],
        name="gather",
        compiler_params=pltpu.CompilerParams(collective_id=1, has_side_effects=True, vmem_limit_bytes=48 * 2**20),
    )(xs, cot, seg, w4, wup, wdt, vec)


def prepare(a):
    (inputs, segment_ids, query_weight, query_bias, key_weight, value_weight, value_bias, output_weight, output_bias,
     first_gain, first_shift, up_weight, up_bias, down_weight, down_bias, second_gain, second_shift, cotangent) = a
    w4 = jnp.stack([query_weight, key_weight, value_weight, output_weight]).swapaxes(1, 2)
    wup = up_weight.reshape(4, 48, 384)
    wdt = down_weight.T.reshape(2, 48, 768)
    small = jnp.stack([query_bias, value_bias, output_bias, first_gain, first_shift, down_bias, second_gain, second_shift])
    small = jnp.pad(small, ((0, 0), (0, 288)))
    vec = jnp.concatenate([small, up_bias[None], jnp.zeros((7, 384), BF)])
    return inputs.reshape(4, 128, 768), cotangent.reshape(4, 128, 768), segment_ids.reshape(4, 1, 128), w4, wup, wdt, vec


HEADS, HD = 12, 64
NT = (((1,), (1,)), ((), ()))
NN = (((1,), (0,)), ((), ()))


def dot(l, r, dims=NN):
    return lax.dot_general(l, r, dims, preferred_element_type=F32)


def vector(VEC, i):
    return jnp.concatenate([VEC[j, pl.ds(i, 1), :][:, :96] for j in range(8)], axis=-1).astype(F32)


def attend_kernel(X, WT, SEG, VEC, Q, KT, V, E, CT, RS, kbuf, vtbuf, mask, sbuf, ebuf, esem):
    _, c, _, _ = place()
    own = X[pl.ds(pl.multiple_of(512 * c, 128), 512), :]
    q = dot(own, WT[0], NT) + vector(VEC, 0)
    Q[...] = (q.astype(BF).astype(F32) * 0.125).astype(BF)
    k = dot(X[...], WT[1], NT)
    kbuf[...] = k.astype(BF)
    KT[...] = k.T.astype(BF)
    v = dot(X[...], WT[2], NT) + vector(VEC, 1)
    V[...] = v.astype(BF)
    vtbuf[...] = v.T.astype(BF)
    row = jnp.concatenate([SEG[j] for j in range(8)], axis=-1).astype(F32)
    mine = jnp.concatenate([SEG[4 * c + j] for j in range(4)], axis=-1).astype(F32)
    col = jnp.broadcast_to(row, (8, 1024)).T[:, :1]
    mask[...] = jnp.where(col == mine, 0.0, -1e30)

    def pair(p, carry):
        lanes = pl.ds(pl.multiple_of(128 * p, 128), 128)
        kp = kbuf[:, lanes]
        qp = Q[:, lanes]
        half = lax.broadcasted_iota(jnp.int32, (512, 128), 1) // 64
        for i in range(2):
            h = 2 * p + i
            qm = jnp.where(half == i, qp, jnp.zeros_like(qp))
            s = dot(kp, qm, NT) + mask[...]
            m = jnp.max(s, axis=0, keepdims=True)
            e = jnp.exp(s - m)
            r = 1.0 / jnp.sum(e, axis=0, keepdims=True)

            @pl.when(p > 0)
            def _():
                pltpu.make_async_copy(ebuf.at[i], E.at[h], esem.at[i]).wait()

            ebuf[i] = e.astype(BF)
            pltpu.make_async_copy(ebuf.at[i], E.at[h], esem.at[i]).start()
            RS[pl.ds(h, 1), :] = r
            rows = pl.ds(pl.multiple_of(64 * h, 64), 64)
            CT[rows, :] = (dot(vtbuf[rows, :], ebuf[i]) * r).astype(BF)
        return carry

    lax.fori_loop(0, 6, pair, 0)
    for i in range(2):
        pltpu.make_async_copy(ebuf.at[i], E.at[10 + i], esem.at[i]).wait()


VM = pl.BlockSpec(memory_space=pltpu.VMEM)
ANY = pl.BlockSpec(memory_space=pl.ANY)


def sds(shape, dt=BF):
    return jax.ShapeDtypeStruct(shape, dt)


def attend_call(X, WT, SEG, VEC):
    return pl.pallas_call(
        attend_kernel,
        out_shape=[sds((512, 768)), sds((768, 1024)), sds((1024, 768)), sds((12, 1024, 512)), sds((768, 512)), sds((16, 512), F32)],
        in_specs=[VM] * 4,
        out_specs=[VM, VM, VM, ANY, VM, VM],
        scratch_shapes=[pltpu.VMEM((1024, 768), BF), pltpu.VMEM((768, 1024), BF), pltpu.VMEM((1024, 512), F32), pltpu.VMEM((8, 128), F32), pltpu.VMEM((2, 1024, 512), BF), pltpu.SemaphoreType.DMA((2,))],
        name="attend",
        compiler_params=pltpu.CompilerParams(vmem_limit_bytes=56 * 2**20),
    )(X, WT, SEG, VEC)


def norm(h):
    centred = h - jnp.mean(h, axis=-1, keepdims=True)
    inv = lax.rsqrt(jnp.mean(centred * centred, axis=-1, keepdims=True) + 1e-12)
    return centred * inv, inv


def norm_back(g, normed, inv):
    return inv * (g - jnp.mean(g, axis=-1, keepdims=True) - normed * jnp.mean(g * normed, axis=-1, keepdims=True))


FC = 768


def feed_kernel(X, CT, WO, WU, WD, VEC, COT, OUT, GF, GC, GO, GU, GD, VS, hid, dge, acc, acc2):
    _, c, _, _ = place()
    x = X[pl.ds(pl.multiple_of(512 * c, 128), 512), :].astype(F32)
    ctx = CT[...].astype(F32).T.astype(BF)
    h = x + dot(ctx, WO[...], NT) + vector(VEC, 2)
    normed1, inv1 = norm(h)
    gain1 = vector(VEC, 3)
    first = normed1 * gain1 + vector(VEC, 4)
    low = first.astype(BF)
    upb = jnp.concatenate([VEC[j, pl.ds(8, 1), :] for j in range(8)], axis=-1).astype(F32)
    for f in range(3072 // FC):
        cols = slice(FC * f, FC * (f + 1))
        inner = dot(low, WU[:, cols]) + upb[:, cols]
        cdf = 0.5 * (1.0 + lax.erf(inner * 0.7071067811865476))
        pdf = jnp.exp(-0.5 * inner * inner) * 0.3989422804014327
        hid[:, cols] = (inner * cdf).astype(BF)
        dge[:, cols] = (cdf + inner * pdf).astype(BF)
        part = dot(hid[:, cols], WD[:, cols], NT)
        if f == 0:
            acc[...] = part
        else:
            acc[...] += part
    normed2, inv2 = norm(first + acc[...] + vector(VEC, 5))
    gain2 = vector(VEC, 6)
    OUT[...] = (normed2 * gain2 + vector(VEC, 7)).astype(BF)
    up = COT[...].astype(F32)

    def total(v):
        return jnp.sum(v, axis=0, keepdims=True)

    VS[...] = jnp.zeros_like(VS)
    VS[6:7, :768] = total(up * normed2)
    VS[7:8, :768] = total(up)
    gss = norm_back(up * gain2, normed2, inv2)
    gs = gss.astype(BF)
    VS[5:6, :768] = total(gs.astype(F32))
    gst = gss.T.astype(BF)
    lowt = first.T.astype(BF)
    acc2[...] = gss
    for f in range(3072 // FC):
        cols = slice(FC * f, FC * (f + 1))
        gi = (dot(gs, WD[:, cols]) * dge[:, cols].astype(F32)).astype(BF)
        VS[8:9, cols] = total(gi.astype(F32))
        GD[:, cols] = dot(gst, hid[:, cols]).astype(BF)
        GU[:, cols] = dot(lowt, gi).astype(BF)
        acc2[...] += dot(gi, WU[:, cols], NT)
    gf = acc2[...]
    VS[3:4, :768] = total(gf * normed1)
    VS[4:5, :768] = total(gf)
    gsf = norm_back(gf * gain1, normed1, inv1)
    GF[...] = gsf
    gb = gsf.astype(BF)
    VS[2:3, :768] = total(gb.astype(F32))
    GC[...] = dot(gb, WO[...]).astype(BF)
    GO[...] = dot(gsf.T.astype(BF), ctx).astype(BF)


def feed_call(X, CT, WO, WU, WD, VEC, COT):
    return pl.pallas_call(
        feed_kernel,
        out_shape=[sds((512, 768)), sds((512, 768), F32), sds((512, 768)), sds((768, 768)), sds((768, 3072)), sds((768, 3072)), sds((16, 3072), F32)],
        in_specs=[VM] * 7,
        out_specs=[VM] * 7,
        scratch_shapes=[pltpu.VMEM((512, 3072), BF), pltpu.VMEM((512, 3072), BF), pltpu.VMEM((512, 768), F32), pltpu.VMEM((512, 768), F32)],
        name="feed",
        compiler_params=pltpu.CompilerParams(vmem_limit_bytes=60 * 2**20),
    )(X, CT, WO, WU, WD, VEC, COT)


def attend_back_kernel(E, Q, KT, V, CT, RS, GC, DQT, DK, DV, ebuf, gct, rcol, esem):
    gct[...] = GC[...].astype(F32).T.astype(BF)
    rcol[...] = RS[...].T
    for i in range(2):
        pltpu.make_async_copy(E.at[i], ebuf.at[i], esem.at[i]).start()

    def pair(p, carry):
        lanes = pl.ds(pl.multiple_of(128 * p, 128), 128)
        vp = V[:, lanes]
        qp = Q[:, lanes]
        gp = GC[:, lanes].astype(F32)
        half = lax.broadcasted_iota(jnp.int32, (512, 128), 1) // 64
        dk = dv = None
        for i in range(2):
            h = 2 * p + i
            rows = pl.ds(pl.multiple_of(64 * h, 64), 64)
            rc = rcol[...]
            sel = lax.broadcasted_iota(jnp.int32, rc.shape, 1) == h
            r = jnp.sum(jnp.where(sel, rc, 0.0), axis=1, keepdims=True)
            gm = jnp.where(half == i, gp * r, 0.0).astype(BF)
            qm = jnp.where(half == i, qp, jnp.zeros_like(qp))
            delta = jnp.sum(CT[rows, :].astype(F32) * gct[rows, :].astype(F32), axis=0, keepdims=True) * RS[pl.ds(h, 1), :]
            pltpu.make_async_copy(E.at[h], ebuf.at[i], esem.at[i]).wait()
            e = ebuf[i]
            ds = (e.astype(F32) * (dot(vp, gm, NT) - delta)).astype(BF)
            dvi = dot(e, gm)
            dki = dot(ds, qm)
            dv = dvi if i == 0 else dv + dvi
            dk = dki if i == 0 else dk + dki
            DQT[rows, :] = (dot(KT[rows, :], ds) * 0.125).astype(BF)

            @pl.when(p < 5)
            def _():
                pltpu.make_async_copy(E.at[h + 2], ebuf.at[i], esem.at[i]).start()

        DK[:, lanes] = dk.astype(BF)
        DV[:, lanes] = dv.astype(BF)
        return carry

    lax.fori_loop(0, 6, pair, 0)


def attend_back_call(E, Q, KT, V, CT, RS, GC):
    return pl.pallas_call(
        attend_back_kernel,
        out_shape=[sds((768, 512)), sds((1024, 768)), sds((1024, 768))],
        in_specs=[ANY] + [VM] * 6,
        out_specs=[VM] * 3,
        scratch_shapes=[pltpu.VMEM((2, 1024, 512), BF), pltpu.VMEM((768, 512), BF), pltpu.VMEM((512, 16), F32), pltpu.SemaphoreType.DMA((2,))],
        name="attend_back",
        compiler_params=pltpu.CompilerParams(vmem_limit_bytes=56 * 2**20),
    )(E, Q, KT, V, CT, RS, GC)


ROFF = (1, 3, 4, 5, 6)
SUMS = []
for _i in range(4):
    SUMS += [("u", _i, XY), ("d", _i, YX)]
SUMS += [("t", 3, XY), ("t", 0, YX), ("t", 1, XY), ("t", 2, YX)]
GRADS_AT = 3


def scatter_kernel(
    X, DQT, DK, DV, GF, WT, GO, GU, GD, VS, OUT,
    LO, IG, D4, DU, DD, VO,
    gt, gu, gd, rt, ru, rd, dkr, dvr, igb, vpack, vrecv, vsum, vrecv2, pairs, pairr,
    lsem, ks, kr, os_, or_, gs, gr, cs, cr, vs_, vr, ws, wr, ps, pr,
):
    y, c, z, x = place()
    j = 2 * z + x
    at = coords()
    partner = device(y, 1 - c, z, x)
    G, R = (gt, gu, gd), (rt, ru, rd)
    loads = [
        pltpu.make_async_copy(GU, gu, lsem.at[0]),
        pltpu.make_async_copy(GD, gd, lsem.at[1]),
        pltpu.make_async_copy(GO, gt.at[3], lsem.at[2]),
    ]
    for cp in loads:
        cp.start()
    greet_all()
    sends = []

    def remote(src, dst, send, recv, to, cond=True):
        cp = pltpu.make_async_remote_copy(src_ref=src, dst_ref=dst, send_sem=send, recv_sem=recv, device_id=to, device_id_type=MESH)
        if cond is True:
            cp.start()
        else:
            pl.when(cond)(cp.start)
        sends.append((cond, cp))
        return cp

    def arrive(dst, recv):
        pltpu.make_async_remote_copy(src_ref=dst, dst_ref=dst, send_sem=recv, recv_sem=recv, device_id=partner, device_id_type=MESH).wait_recv()

    theirs = pl.ds(pl.multiple_of(512 * (1 - c), 128), 512)
    ours = pl.ds(pl.multiple_of(512 * c, 128), 512)
    remote(DK.at[theirs], dkr, ks.at[0], kr.at[0], partner)
    remote(DV.at[theirs], dvr, ks.at[1], kr.at[1], partner)

    def tokens(src, dst, k, send, recv, loc):
        b = 4 * c + k
        mine = (x == c) & (b // 2 == z) & (b % 2 == x)
        cp = pltpu.make_async_remote_copy(src_ref=src, dst_ref=dst, send_sem=send, recv_sem=recv, device_id=device(y, x, b // 2, b % 2), device_id_type=MESH)
        lc = pltpu.make_async_copy(src, dst, loc)
        pl.when(jnp.logical_not(mine))(cp.start)
        pl.when(mine)(lc.start)
        return mine, cp, lc

    conds = []
    for k in range(4):
        conds.append(tokens(OUT.at[pl.ds(128 * k, 128)], LO.at[z], k, os_.at[0, k], or_.at[0, z], lsem.at[3]))

    n = len(SUMS)

    def slot(order, s):
        def place_of(at):
            spot = dict(at)
            for d in order[s + 1 :]:
                spot[d] = 1 - at[d]
            return whole(spot, order[:s])
        return place_of

    def launch(u, s):
        ch = SUMS[u]
        order = ch[2]
        to = flip(at, order[s])
        src = region(G, ch, whole(to, order[:s]))
        dst = region(R, ch, slot(order, s)(to))
        for k in range(len(src)):
            remote(src[k], dst[k], gs.at[u, s, k], gr.at[u, s, k], to_device(to))

    def absorb(u, s):
        ch = SUMS[u]
        kind, i, order = ch
        got = region(R, ch, slot(order, s)(at))
        own = region(G, ch, whole(at, order[:s]))
        for k in range(len(got)):
            arrive(got[k], gr.at[u, s, k])
            if s > 0:
                own[k][...] = own[k][...] + got[k][...]
                continue
            done = own[k][...].astype(F32) + got[k][...].astype(F32)
            if kind == "u":
                DU[i] = done
            elif kind == "d":
                DD[i // 2, :, 384 * (i % 2) : 384 * (i % 2) + 384] = done
            else:
                lo, hi = done[:, :192], done[:, 192:]
                D4[i, pl.ds(pl.multiple_of(48 * c, 16), 48), :] = jnp.where(c == 0, lo, hi)
                pairs[i] = jnp.where(c == 0, hi, lo)
                remote(pairs.at[i], pairr.at[i], ps.at[i], pr.at[i], partner)

    def gradients():
        arrive(dkr, kr.at[0])
        arrive(dvr, kr.at[1])
        dk = (DK[ours].astype(F32) + dkr[...].astype(F32)).astype(BF)
        dv = (DV[ours].astype(F32) + dvr[...].astype(F32)).astype(BF)
        xo = X[ours]
        dqf = DQT[...].astype(F32).T
        dq = dqf.astype(BF)
        shape = (2, 2, 2, 2, 48, 768)
        gt[0] = dot(DQT[...], xo).astype(BF).reshape(shape)
        gt[1] = dot(dk.astype(F32).T.astype(BF), xo).astype(BF).reshape(shape)
        gt[2] = dot(dv.astype(F32).T.astype(BF), xo).astype(BF).reshape(shape)
        ig = GF[...] + dot(dq, WT[0]) + dot(dk, WT[1]) + dot(dv, WT[2])
        igb[...] = ig.astype(BF)
        for k in range(4):
            conds.append(tokens(igb.at[pl.ds(128 * k, 128)], IG.at[z], k, os_.at[1, k], or_.at[1, z], lsem.at[4]))
        qsum = jnp.sum(dqf, axis=0, keepdims=True)
        vsm = jnp.sum(dv.astype(F32), axis=0, keepdims=True)
        low = jnp.concatenate([qsum, vsm, VS[2:8, :768]], axis=0)
        for b in range(8):
            vpack[b] = jnp.zeros((16, 384), F32)
            vpack[b, 0:8, 0:96] = low[:, 96 * b : 96 * b + 96]
            vpack[b, 8:9, :] = VS[8:9, 384 * b : 384 * b + 384]
        for d in range(1, 8):
            o = (j + d) % 8
            remote(vpack.at[o], vrecv.at[d], vs_.at[d], vr.at[d], device(y, c, o // 2, o % 2))

    for t in range(n + ROFF[4]):
        if t == 0:
            loads[0].wait()
        if t == 1:
            loads[1].wait()
        if t == 8:
            loads[2].wait()
        if t < n:
            launch(t, 4)
        if t == GRADS_AT:
            gradients()
        for s in range(5):
            u = t - ROFF[s]
            if 0 <= u < n:
                absorb(u, 4 - s)
                if s < 4:
                    launch(u, 3 - s)
        if t == GRADS_AT + 2:
            total = vpack[j]
            for d in range(1, 8):
                arrive(vrecv.at[d], vr.at[d])
                total = total + vrecv[d]
            vsum[...] = total
            me = 2 * y + c
            for d in range(1, 4):
                o = (me + d) % 4
                remote(vsum, vrecv2.at[d], ws.at[d], wr.at[d], (o, j))
        if t == GRADS_AT + 4:
            total = vsum[...]
            for d in range(1, 4):
                arrive(vrecv2.at[d], wr.at[d])
                total = total + vrecv2[d]
            VO[...] = total
    for i in range(4):
        arrive(pairr.at[i], pr.at[i])
        D4[i, pl.ds(pl.multiple_of(48 * (1 - c), 16), 48), :] = pairr[i]
    for w, home in ((0, LO), (1, IG)):
        for m in range(4):
            mine = (m == z) & (x == c) & (z // 2 == c)

            @pl.when(jnp.logical_not(mine))
            def _(w=w, home=home, m=m):
                arrive(home.at[m], or_.at[w, m])

            @pl.when(mine)
            def _(w=w, home=home, m=m):
                pltpu.make_async_copy(home.at[m], home.at[m], lsem.at[3 + w]).wait()
    for cond, cp in sends:
        if cond is True:
            cp.wait_send()
        else:
            pl.when(cond)(cp.wait_send)
    for mine, cp, lc in conds:
        pl.when(jnp.logical_not(mine))(cp.wait_send)


def scatter_call(X, DQT, DK, DV, GF, WT, GO, GU, GD, VS, OUT):
    S = pltpu.SemaphoreType.DMA
    n = len(SUMS)
    sets = [pltpu.VMEM((4, 2, 2, 2, 2, 48, 768), BF), pltpu.VMEM((2, 2, 4, 48, 3072), BF), pltpu.VMEM((2, 2, 2, 2, 48, 3072), BF)]
    return pl.pallas_call(
        scatter_kernel,
        out_shape=[sds((4, 128, 768)), sds((4, 128, 768)), sds((4, 96, 192), F32), sds((4, 48, 384), F32), sds((2, 48, 768), F32), sds((16, 384), F32)],
        in_specs=[VM, VM, VM, VM, VM, VM, ANY, ANY, ANY, VM, VM],
        out_specs=[ANY, ANY, VM, VM, VM, VM],
        scratch_shapes=sets + sets + [
            pltpu.VMEM((512, 768), BF), pltpu.VMEM((512, 768), BF), pltpu.VMEM((512, 768), BF),
            pltpu.VMEM((8, 16, 384), F32), pltpu.VMEM((8, 16, 384), F32), pltpu.VMEM((16, 384), F32), pltpu.VMEM((4, 16, 384), F32),
            pltpu.VMEM((4, 48, 192), F32), pltpu.VMEM((4, 48, 192), F32),
            S((5,)), S((2,)), S((2,)), S((2, 4)), S((2, 4)), S((n, 5, 4)), S((n, 5, 4)), S((4,)), S((4,)), S((8,)), S((8,)), S((4,)), S((4,)), S((4,)), S((4,)),
        ],
        name="scatter",
        compiler_params=pltpu.CompilerParams(collective_id=2, has_side_effects=True, vmem_limit_bytes=60 * 2**20),
    )(X, DQT, DK, DV, GF, WT, GO.reshape(2, 2, 2, 2, 48, 768), GU.reshape(2, 2, 4, 48, 3072), GD.reshape(2, 2, 2, 2, 48, 3072), VS, OUT)


def rows_on_chips(*a):
    xs,cot,seg,w4,wup,wdt,vec=prepare(a)
    X,C,SEG,WT,WU,WD,VEC=gather_call(xs,cot,seg,w4,wup,wdt,vec)
    X=X.reshape(1024,768); C=C.reshape(512,768); W=WT.reshape(4,768,768); WU=WU.reshape(768,3072); WD=WD.reshape(768,3072)
    Q,KT,V,E,CT,RS=attend_call(X,W,SEG,VEC)
    OUT,GF,GC,GO,GU,GD,VS=feed_call(X,CT,W[3],WU,WD,VEC,C)
    DQT,DK,DV=attend_back_call(E,Q,KT,V,CT,RS,GC)
    LO,IG,D4,DU,DD,VO=scatter_call(X,DQT,DK,DV,GF,W,GO,GU,GD,VS,OUT)
    D4=D4.swapaxes(1,2)
    DU=DU.reshape(192,384); DD=DD.reshape(96,768).T
    v=VO[:8,:96]
    s=(4,1,128,768)
    return (LO.reshape(s),IG.reshape(s),D4[0],v[0],D4[1],D4[2],v[1],D4[3],v[2],v[3],v[4],DU,VO[8],DD,v[5],v[6],v[7])


EPSILON = 1e-12
NEGATIVE = -1e30


def product(left, right, form):
    return jnp.einsum(form, left, right, preferred_element_type=jnp.float32)


def normalize(hidden, gain, shift):
    centred = hidden - jnp.mean(hidden, axis=-1, keepdims=True)
    scale_inv = lax.rsqrt(jnp.mean(centred * centred, axis=-1, keepdims=True) + EPSILON)
    normed = centred * scale_inv
    return (normed * gain + shift, normed, scale_inv)


def normalize_back(grad_normed, normed, scale_inv):
    centred_grad = grad_normed - jnp.mean(grad_normed, axis=-1, keepdims=True)
    return scale_inv * (
        centred_grad - normed * jnp.mean(grad_normed * normed, axis=-1, keepdims=True)
    )


def same_passage(query_pair, key_pair):
    return jnp.all(query_pair[:, :, None, :] == key_pair[:, None, :, :], axis=-1)[:, None]


def micro_step(shared, tokens, passage_ids, cotan):
    (
        weight_query,
        weight_key,
        weight_value,
        weight_out,
        weight_up,
        weight_down,
        bias_query,
        bias_value,
        bias_out,
        gain_first,
        shift_first,
        bias_up,
        bias_down,
        gain_second,
        shift_second,
    ) = shared
    bias_query = bias_query.astype(jnp.float32)
    bias_value = bias_value.astype(jnp.float32)
    bias_out = bias_out.astype(jnp.float32)
    gain_first = gain_first.astype(jnp.float32)
    shift_first = shift_first.astype(jnp.float32)
    bias_up = bias_up.astype(jnp.float32)
    bias_down = bias_down.astype(jnp.float32)
    gain_second = gain_second.astype(jnp.float32)
    shift_second = shift_second.astype(jnp.float32)
    row_count, seq_count, width = tokens.shape
    token_count = row_count * seq_count
    scale = HD ** (-0.5)
    flat = tokens.reshape(token_count, width)
    queries = (product(flat, weight_query, "md,de->me") + bias_query).astype(jnp.bfloat16)
    keys = product(flat, weight_key, "md,de->me").astype(jnp.bfloat16)
    values = (product(flat, weight_value, "md,de->me") + bias_value).astype(jnp.bfloat16)
    query_four = queries.reshape(row_count, seq_count, HEADS, HD)
    pair_local = jnp.stack((passage_ids // 256, passage_ids % 256), axis=-1).astype(jnp.bfloat16)
    key_rows = keys.reshape(row_count, seq_count, width)
    value_rows = values.reshape(row_count, seq_count, width)
    key_local = key_rows.reshape(row_count, seq_count, HEADS, HD)
    value_local = value_rows.reshape(row_count, seq_count, HEADS, HD)
    running_max = jnp.full((row_count, HEADS, seq_count), NEGATIVE, jnp.float32)
    running_acc = jnp.zeros((row_count, seq_count, HEADS, HD), jnp.float32)
    key_piece = lax.all_gather(key_rows, "blk", axis=1, tiled=True)
    value_piece = lax.all_gather(value_rows, "blk", axis=1, tiled=True)
    pair_piece = lax.all_gather(pair_local, "blk", axis=1, tiled=True)
    count = key_piece.shape[1]
    key_four = key_piece.reshape(row_count, count, HEADS, HD)
    value_four = value_piece.reshape(row_count, count, HEADS, HD)
    allowed = same_passage(pair_local, pair_piece)
    scores = jnp.where(allowed, product(query_four, key_four, "rqhd,rkhd->rhqk") * scale, NEGATIVE)
    fresh_max = jnp.maximum(running_max, jnp.max(scores, axis=-1))
    weights = jnp.where(allowed, jnp.exp(scores - fresh_max[..., None]), 0.0)
    decay = jnp.exp(running_max - fresh_max)
    running_sum = jnp.sum(weights, axis=-1)
    mixed = product(weights.astype(jnp.bfloat16), value_four, "rhqk,rkhd->rqhd")
    running_acc = running_acc * jnp.swapaxes(decay, 1, 2)[..., None] + mixed
    running_max, running_sum, running_acc = (fresh_max, running_sum, running_acc)
    log_total = running_max + jnp.log(running_sum)
    attended = running_acc / jnp.swapaxes(running_sum, 1, 2)[..., None]
    context = attended.reshape(token_count, width).astype(jnp.bfloat16)
    branch = product(context, weight_out, "md,de->me") + bias_out
    first, normed_first, inv_first = normalize(
        flat.astype(jnp.float32) + branch, gain_first, shift_first
    )
    first_low = first.astype(jnp.bfloat16)
    inner = product(first_low, weight_up, "md,df->mf") + bias_up
    activation, gelu_pull = jax.vjp(partial(jax.nn.gelu, approximate=False), inner)
    hidden = activation.astype(jnp.bfloat16)
    second = product(hidden, weight_down, "mf,fd->md") + bias_down
    output, normed_second, inv_second = normalize(first + second, gain_second, shift_second)
    upstream = cotan.reshape(token_count, width).astype(jnp.float32)
    grad_gain_second = jnp.sum(upstream * normed_second, axis=0, keepdims=True)
    grad_shift_second = jnp.sum(upstream, axis=0, keepdims=True)
    grad_sum_second = normalize_back(upstream * gain_second, normed_second, inv_second)
    grad_second = grad_sum_second.astype(jnp.bfloat16)
    grad_weight_down = product(hidden, grad_second, "mf,md->fd")
    grad_bias_down = jnp.sum(grad_second.astype(jnp.float32), axis=0, keepdims=True)
    grad_inner = gelu_pull(product(grad_second, weight_down, "md,fd->mf"))[0].astype(jnp.bfloat16)
    grad_weight_up = product(first_low, grad_inner, "md,mf->df")
    grad_bias_up = jnp.sum(grad_inner.astype(jnp.float32), axis=0, keepdims=True)
    grad_first = grad_sum_second + product(grad_inner, weight_up, "mf,df->md")
    grad_gain_first = jnp.sum(grad_first * normed_first, axis=0, keepdims=True)
    grad_shift_first = jnp.sum(grad_first, axis=0, keepdims=True)
    grad_sum_first = normalize_back(grad_first * gain_first, normed_first, inv_first)
    grad_branch = grad_sum_first.astype(jnp.bfloat16)
    grad_weight_out = product(context, grad_branch, "md,me->de")
    grad_bias_out = jnp.sum(grad_branch.astype(jnp.float32), axis=0, keepdims=True)
    grad_context = product(grad_branch, weight_out, "me,de->md").astype(jnp.bfloat16)
    grad_context_four = grad_context.reshape(row_count, seq_count, HEADS, HD)
    delta = jnp.swapaxes(jnp.sum(grad_context_four.astype(jnp.float32) * attended, axis=-1), 1, 2)
    key_piece = lax.all_gather(key_rows, "blk", axis=1, tiled=True)
    value_piece = lax.all_gather(value_rows, "blk", axis=1, tiled=True)
    pair_piece = lax.all_gather(pair_local, "blk", axis=1, tiled=True)
    count = key_piece.shape[1]
    key_four = key_piece.reshape(row_count, count, HEADS, HD)
    value_four = value_piece.reshape(row_count, count, HEADS, HD)
    allowed = same_passage(pair_local, pair_piece)
    scores = jnp.where(allowed, product(query_four, key_four, "rqhd,rkhd->rhqk") * scale, NEGATIVE)
    probs = jnp.where(allowed, jnp.exp(scores - log_total[..., None]), 0.0)
    grad_probs = product(grad_context_four, value_four, "rqhd,rkhd->rhqk")
    grad_scores = (probs * (grad_probs - delta[..., None])).astype(jnp.bfloat16)
    grad_query_acc = product(grad_scores, key_four, "rhqk,rkhd->rqhd") * scale
    grad_queries = grad_query_acc.reshape(token_count, width).astype(jnp.bfloat16)
    pair_wide = pair_local.astype(jnp.float32)
    sent = (
        queries.reshape(row_count, seq_count, width).astype(jnp.float32),
        grad_context.reshape(row_count, seq_count, width).astype(jnp.float32),
        jnp.swapaxes(log_total, 1, 2),
        jnp.swapaxes(delta, 1, 2),
        pair_wide,
    )
    query_piece = lax.all_gather(sent[0], "blk", axis=1, tiled=True)
    context_piece = lax.all_gather(sent[1], "blk", axis=1, tiled=True)
    total_piece = lax.all_gather(sent[2], "blk", axis=1, tiled=True)
    delta_piece = lax.all_gather(sent[3], "blk", axis=1, tiled=True)
    pair_piece = lax.all_gather(sent[4], "blk", axis=1, tiled=True)
    count = query_piece.shape[1]
    query_part = query_piece.astype(jnp.bfloat16).reshape(row_count, count, HEADS, HD)
    context_part = context_piece.astype(jnp.bfloat16).reshape(row_count, count, HEADS, HD)
    total_part = jnp.swapaxes(total_piece, 1, 2)
    delta_part = jnp.swapaxes(delta_piece, 1, 2)
    allowed = same_passage(pair_piece, pair_wide)
    scores = jnp.where(allowed, product(query_part, key_local, "rqhd,rkhd->rhqk") * scale, NEGATIVE)
    probs = jnp.where(allowed, jnp.exp(scores - total_part[..., None]), 0.0)
    grad_value_acc = product(probs.astype(jnp.bfloat16), context_part, "rhqk,rqhd->rkhd")
    grad_probs = product(context_part, value_local, "rqhd,rkhd->rhqk")
    grad_scores = (probs * (grad_probs - delta_part[..., None])).astype(jnp.bfloat16)
    grad_key_acc = product(grad_scores, query_part, "rhqk,rqhd->rkhd") * scale
    grad_key_acc, grad_value_acc = (grad_key_acc, grad_value_acc)
    grad_keys = grad_key_acc.reshape(token_count, width).astype(jnp.bfloat16)
    grad_values = grad_value_acc.reshape(token_count, width).astype(jnp.bfloat16)
    grad_weight_query = product(flat, grad_queries, "md,me->de")
    grad_bias_query = jnp.sum(grad_queries.astype(jnp.float32), axis=0, keepdims=True)
    grad_weight_key = product(flat, grad_keys, "md,me->de")
    grad_weight_value = product(flat, grad_values, "md,me->de")
    grad_bias_value = jnp.sum(grad_values.astype(jnp.float32), axis=0, keepdims=True)
    grad_tokens = (
        grad_sum_first
        + product(grad_queries, weight_query, "me,de->md")
        + product(grad_keys, weight_key, "me,de->md")
        + product(grad_values, weight_value, "me,de->md")
    )
    contributions = (
        grad_weight_query,
        grad_weight_key,
        grad_weight_value,
        grad_weight_out,
        grad_weight_up,
        grad_weight_down,
        grad_bias_query,
        grad_bias_value,
        grad_bias_out,
        grad_gain_first,
        grad_shift_first,
        grad_bias_up,
        grad_bias_down,
        grad_gain_second,
        grad_shift_second,
    )
    return (
        output.astype(jnp.bfloat16).reshape(row_count, seq_count, width),
        grad_tokens.astype(jnp.bfloat16).reshape(row_count, seq_count, width),
        contributions,
    )


def general(
    inputs,
    segment_ids,
    query_weight,
    query_bias,
    key_weight,
    value_weight,
    value_bias,
    output_weight,
    output_bias,
    first_gain,
    first_shift,
    up_weight,
    up_bias,
    down_weight,
    down_bias,
    second_gain,
    second_shift,
    cotangent,
):
    outputs = []
    input_grads = []
    totals = None
    widened = (
        lax.all_gather(query_weight, "blk", axis=1, tiled=True),
        lax.all_gather(key_weight, "blk", axis=1, tiled=True),
        lax.all_gather(value_weight, "blk", axis=1, tiled=True),
        lax.all_gather(output_weight, "blk", axis=1, tiled=True),
        lax.all_gather(up_weight, "blk", axis=1, tiled=True),
        lax.all_gather(down_weight, "blk", axis=1, tiled=True),
        lax.all_gather(query_bias.reshape(1, -1), "blk", axis=1, tiled=True),
        lax.all_gather(value_bias.reshape(1, -1), "blk", axis=1, tiled=True),
        lax.all_gather(output_bias.reshape(1, -1), "blk", axis=1, tiled=True),
        lax.all_gather(first_gain.reshape(1, -1), "blk", axis=1, tiled=True),
        lax.all_gather(first_shift.reshape(1, -1), "blk", axis=1, tiled=True),
        lax.all_gather(up_bias.reshape(1, -1), "blk", axis=1, tiled=True),
        lax.all_gather(down_bias.reshape(1, -1), "blk", axis=1, tiled=True),
        lax.all_gather(second_gain.reshape(1, -1), "blk", axis=1, tiled=True),
        lax.all_gather(second_shift.reshape(1, -1), "blk", axis=1, tiled=True),
    )
    complete = (
        lax.all_gather(widened[0], "dp", axis=0, tiled=True),
        lax.all_gather(widened[1], "dp", axis=0, tiled=True),
        lax.all_gather(widened[2], "dp", axis=0, tiled=True),
        lax.all_gather(widened[3], "dp", axis=0, tiled=True),
        lax.all_gather(widened[4], "dp", axis=0, tiled=True),
        lax.all_gather(widened[5], "dp", axis=0, tiled=True),
    )
    shared = tuple(complete) + tuple(widened[6:])
    for batch_index in range(inputs.shape[0]):
        layer_out, layer_grad, contributions = micro_step(
            shared, inputs[batch_index], segment_ids[batch_index], cotangent[batch_index]
        )
        outputs.append(layer_out)
        input_grads.append(layer_grad)
        if totals is None:
            totals = contributions
        else:
            totals = tuple((earlier + latest for earlier, latest in zip(totals, contributions)))
    narrowed = (
        lax.psum_scatter(totals[0], "blk", scatter_dimension=1, tiled=True),
        lax.psum_scatter(totals[1], "blk", scatter_dimension=1, tiled=True),
        lax.psum_scatter(totals[2], "blk", scatter_dimension=1, tiled=True),
        lax.psum_scatter(totals[3], "blk", scatter_dimension=1, tiled=True),
        lax.psum_scatter(totals[4], "blk", scatter_dimension=1, tiled=True),
        lax.psum_scatter(totals[5], "blk", scatter_dimension=1, tiled=True),
        lax.psum_scatter(totals[6], "blk", scatter_dimension=1, tiled=True),
        lax.psum_scatter(totals[7], "blk", scatter_dimension=1, tiled=True),
        lax.psum_scatter(totals[8], "blk", scatter_dimension=1, tiled=True),
        lax.psum_scatter(totals[9], "blk", scatter_dimension=1, tiled=True),
        lax.psum_scatter(totals[10], "blk", scatter_dimension=1, tiled=True),
        lax.psum_scatter(totals[11], "blk", scatter_dimension=1, tiled=True),
        lax.psum_scatter(totals[12], "blk", scatter_dimension=1, tiled=True),
        lax.psum_scatter(totals[13], "blk", scatter_dimension=1, tiled=True),
        lax.psum_scatter(totals[14], "blk", scatter_dimension=1, tiled=True),
    )
    matrix_sums = (
        lax.psum_scatter(narrowed[0], "dp", scatter_dimension=0, tiled=True),
        lax.psum_scatter(narrowed[1], "dp", scatter_dimension=0, tiled=True),
        lax.psum_scatter(narrowed[2], "dp", scatter_dimension=0, tiled=True),
        lax.psum_scatter(narrowed[3], "dp", scatter_dimension=0, tiled=True),
        lax.psum_scatter(narrowed[4], "dp", scatter_dimension=0, tiled=True),
        lax.psum_scatter(narrowed[5], "dp", scatter_dimension=0, tiled=True),
    )
    vector_sums = lax.psum(
        (
            narrowed[6],
            narrowed[7],
            narrowed[8],
            narrowed[9],
            narrowed[10],
            narrowed[11],
            narrowed[12],
            narrowed[13],
            narrowed[14],
        ),
        "dp",
    )
    return (
        jnp.stack(outputs),
        jnp.stack(input_grads),
        matrix_sums[0],
        vector_sums[0].reshape(-1),
        matrix_sums[1],
        matrix_sums[2],
        vector_sums[1].reshape(-1),
        matrix_sums[3],
        vector_sums[2].reshape(-1),
        vector_sums[3].reshape(-1),
        vector_sums[4].reshape(-1),
        matrix_sums[4],
        vector_sums[5].reshape(-1),
        matrix_sums[5],
        vector_sums[6].reshape(-1),
        vector_sums[7].reshape(-1),
        vector_sums[8].reshape(-1),
    )


def solution(mesh):
    in_specs = (
        P(None, "dp", "blk", None),
        P(None, "dp", "blk"),
        P("dp", "blk"),
        P("blk"),
        P("dp", "blk"),
        P("dp", "blk"),
        P("blk"),
        P("dp", "blk"),
        P("blk"),
        P("blk"),
        P("blk"),
        P("dp", "blk"),
        P("blk"),
        P("dp", "blk"),
        P("blk"),
        P("blk"),
        P("blk"),
        P(None, "dp", "blk", None),
    )
    out_specs = (
        P(None, "dp", "blk", None),
        P(None, "dp", "blk", None),
        P("dp", "blk"),
        P("blk"),
        P("dp", "blk"),
        P("dp", "blk"),
        P("blk"),
        P("dp", "blk"),
        P("blk"),
        P("blk"),
        P("blk"),
        P("dp", "blk"),
        P("blk"),
        P("dp", "blk"),
        P("blk"),
        P("blk"),
        P("blk"),
    )
    small = mesh.shape["dp"] == 4 and mesh.shape["blk"] == 8

    def on_device(*arrays):
        if small and arrays[0].shape == (4, 1, 128, 768):
            return rows_on_chips(*arrays)
        return general(*arrays)

    return jax.shard_map(
        on_device, mesh=mesh, in_specs=in_specs, out_specs=out_specs, check_vma=False
    )
```

```python
from functools import partial

import jax
import jax.numpy as jnp
from jax import lax
from jax.experimental import pallas as pl
from jax.experimental.pallas import tpu as pltpu
from jax.sharding import PartitionSpec as P

MESH = pl.DeviceIdType.MESH
BF = jnp.bfloat16
F32 = jnp.float32


(BEGIN, RELAY, TOKENS, BLOCK, OTHER, COTANGENT, PAIR, QUERY, KEY, VALUE, HEAD, BRANCH, UP, DOWN) = range(14)
(LAUNCH, ABSORB, HOME, GRAD_U, GRAD_D, GRAD_T, HEAD_BACK, EXCHANGE, MERGE, INPUT_GRAD, VECTORS, VECTORS_LAST) = range(14, 26)


def place():
    dp = lax.axis_index("dp")
    blk = lax.axis_index("blk")
    return dp // 2, dp % 2, blk // 2, blk % 2


def device(y, c, z, x):
    return (y * 2 + c, z * 2 + x)


def greet_all():
    y, c, z, x = place()
    me = (y * 2 + c) * 8 + z * 2 + x
    barrier = pltpu.get_barrier_semaphore()

    def greet(i, carry):
        other = (me + i) % 32
        pl.semaphore_signal(barrier, inc=1, device_id=(other // 8, other % 8), device_id_type=MESH)
        return carry

    lax.fori_loop(1, 32, greet, 0)
    pl.semaphore_wait(barrier, 31)


def coords():
    y, c, z, x = place()
    return {"a": z // 2, "b": z % 2, "x": x, "y": y, "c": c}


def to_device(at):
    return device(at["y"], at["c"], 2 * at["a"] + at["b"], at["x"])


def flip(at, dim):
    return {**at, dim: 1 - at[dim]}


def whole(at, dims):
    return {k: (None if k in dims else v) for k, v in at.items()}


def span(v):
    return slice(None) if v is None else v


def each(v):
    return (0, 1) if v is None else (v,)


def lanes(start, size):
    return pl.ds(start if isinstance(start, int) else pl.multiple_of(start, 128), size)


def region(refs, chunk, at):
    wt, wu, wd = refs
    kind, i, _ = chunk
    a, b, x, y, c = (at[k] for k in "abxyc")
    if kind == "t":
        cols = slice(None) if y is None else lanes(384 * y, 384)
        return [wt.at[i, span(a), span(b), span(x), span(c), :, cols]]
    if kind == "u":
        if a is None and b is None and x is None:
            return [wu.at[span(y), span(c), i]]
        return [wu.at[span(y), span(c), i, :, lanes(384 * (4 * p + 2 * q + r), 384)] for p in each(a) for q in each(b) for r in each(x)]
    return [wd.at[span(a), span(b), span(x), i // 2, :, lanes(768 * (2 * p + q) + 384 * (i % 2), 384)] for p in each(y) for q in each(c)]


HEADS, HD = 12, 64
NT = (((1,), (1,)), ((), ()))
NN = (((1,), (0,)), ((), ()))


def dot(l, r, dims=NN):
    return lax.dot_general(l, r, dims, preferred_element_type=F32)


VM = pl.BlockSpec(memory_space=pltpu.VMEM)
ANY = pl.BlockSpec(memory_space=pl.ANY)


def sds(shape, dt=BF):
    return jax.ShapeDtypeStruct(shape, dt)


def norm(h):
    centred = h - jnp.mean(h, axis=-1, keepdims=True)
    inv = lax.rsqrt(jnp.mean(centred * centred, axis=-1, keepdims=True) + 1e-12)
    return centred * inv, inv


def norm_back(g, normed, inv):
    return inv * (g - jnp.mean(g, axis=-1, keepdims=True) - normed * jnp.mean(g * normed, axis=-1, keepdims=True))


FORWARD_CHUNKS = (
    ("t", 0, "abxyc"), ("t", 1, "abxyc"), ("t", 2, "abyxc"), ("t", 3, "abxyc"), ("u", 0, "abxyc"), ("u", 1, "abyxc"), ("u", 2, "abxyc"),
    ("u", 3, "axbyc"), ("d", 0, "abyxc"), ("d", 2, "abxyc"), ("d", 1, "abyxc"), ("d", 3, "abxyc"),
)
FORWARD_PLAN = (
    (TOKENS, 0), (PAIR,), (BEGIN, 0), (BEGIN, 1), (RELAY, 0, 0), (BEGIN, 2), (TOKENS, 1), (RELAY, 1, 0), (BEGIN, 3), (RELAY, 0, 1),
    (RELAY, 2, 0), (BEGIN, 4), (RELAY, 1, 1), (RELAY, 0, 2), (RELAY, 2, 1), (RELAY, 3, 0), (BEGIN, 5), (TOKENS, 2), (RELAY, 4, 0),
    (BEGIN, 6), (RELAY, 1, 2), (RELAY, 3, 1), (RELAY, 0, 3), (RELAY, 5, 0), (BEGIN, 7), (RELAY, 0, 4), (RELAY, 2, 2), (RELAY, 4, 1),
    (RELAY, 3, 2), (RELAY, 1, 3), (RELAY, 5, 1), (RELAY, 6, 0), (BEGIN, 8), (TOKENS, 3), (BLOCK, 0), (BLOCK, 1), (RELAY, 1, 4),
    (RELAY, 2, 3), (OTHER, 0), (BLOCK, 2), (RELAY, 7, 0), (BEGIN, 9), (OTHER, 1), (RELAY, 2, 4), (RELAY, 6, 1), (OTHER, 2), (RELAY, 4, 2),
    (RELAY, 8, 0), (BEGIN, 10), (RELAY, 3, 3), (RELAY, 3, 4), (RELAY, 5, 2), (RELAY, 7, 1), (RELAY, 8, 1), (RELAY, 9, 0), (RELAY, 6, 2),
    (BEGIN, 11), (COTANGENT, 0), (COTANGENT, 1), (COTANGENT, 2), (COTANGENT, 3), (RELAY, 10, 0), (BLOCK, 3), (QUERY,), (RELAY, 4, 3),
    (RELAY, 5, 3), (RELAY, 7, 2), (OTHER, 3), (KEY,), (RELAY, 4, 4), (RELAY, 5, 4), (RELAY, 9, 1), (VALUE,), (RELAY, 8, 2), (RELAY, 11, 0),
    (HEAD, 0), (HEAD, 1), (RELAY, 6, 3), (HEAD, 2), (HEAD, 3), (RELAY, 6, 4), (RELAY, 7, 3), (HEAD, 4), (HEAD, 5), (RELAY, 7, 4),
    (HEAD, 6), (HEAD, 7), (HEAD, 8), (HEAD, 9), (RELAY, 9, 2), (RELAY, 10, 1), (HEAD, 10), (RELAY, 11, 1), (HEAD, 11), (RELAY, 8, 3),
    (BRANCH,), (RELAY, 8, 4), (RELAY, 9, 3), (UP, 0), (RELAY, 9, 4), (UP, 1), (RELAY, 10, 2), (RELAY, 11, 2), (UP, 2), (UP, 3), (DOWN, 0),
    (RELAY, 10, 3), (RELAY, 11, 3), (RELAY, 10, 4), (RELAY, 11, 4), (DOWN, 1),
)
BACKWARD_CHUNKS = (
    ("d", 3, "bxayc"), ("d", 0, "axbyc"), ("u", 3, "axybc"), ("d", 1, "abyxc"), ("d", 2, "aybxc"), ("u", 1, "bxayc"), ("u", 2, "baxyc"),
    ("t", 3, "aybxc"), ("u", 0, "baxyc"), ("t", 0, "abxyc"), ("t", 1, "baxyc"), ("t", 2, "axbyc"),
)
BACKWARD_PLAN = (
    (GRAD_D, 3), (LAUNCH, 0), (GRAD_D, 0), (LAUNCH, 1), (HOME, 0), (HOME, 1), (HOME, 2), (HEAD_BACK, 0), (ABSORB, 0, 0), (GRAD_U, 3),
    (LAUNCH, 2), (ABSORB, 1, 0), (GRAD_D, 1), (LAUNCH, 3), (HOME, 3), (HEAD_BACK, 1), (ABSORB, 2, 0), (GRAD_D, 2), (LAUNCH, 4),
    (ABSORB, 0, 1), (ABSORB, 3, 0), (GRAD_U, 1), (LAUNCH, 5), (HEAD_BACK, 2), (ABSORB, 4, 0), (GRAD_U, 2), (LAUNCH, 6), (ABSORB, 1, 1),
    (ABSORB, 5, 0), (GRAD_T, 3), (LAUNCH, 7), (HEAD_BACK, 3), (ABSORB, 6, 0), (GRAD_U, 0), (LAUNCH, 8), (ABSORB, 3, 1), (ABSORB, 7, 0),
    (ABSORB, 2, 1), (ABSORB, 5, 1), (HEAD_BACK, 4), (ABSORB, 8, 0), (HEAD_BACK, 5), (HEAD_BACK, 6), (ABSORB, 4, 1), (ABSORB, 6, 1),
    (HEAD_BACK, 7), (HEAD_BACK, 8), (ABSORB, 0, 2), (ABSORB, 1, 2), (HEAD_BACK, 9), (ABSORB, 3, 2), (ABSORB, 7, 1), (HEAD_BACK, 10),
    (HEAD_BACK, 11), (EXCHANGE,), (ABSORB, 2, 2), (ABSORB, 4, 2), (ABSORB, 3, 3), (ABSORB, 5, 2), (ABSORB, 6, 2), (ABSORB, 8, 1),
    (ABSORB, 0, 3), (ABSORB, 7, 2), (ABSORB, 1, 3), (MERGE,), (GRAD_T, 0), (LAUNCH, 9), (ABSORB, 2, 3), (ABSORB, 3, 4), (GRAD_T, 1),
    (LAUNCH, 10), (ABSORB, 0, 4), (ABSORB, 4, 3), (ABSORB, 5, 3), (INPUT_GRAD,), (ABSORB, 6, 3), (ABSORB, 1, 4), (ABSORB, 7, 3),
    (ABSORB, 8, 2), (ABSORB, 9, 0), (ABSORB, 10, 0), (ABSORB, 2, 4), (GRAD_T, 2), (LAUNCH, 11), (ABSORB, 5, 4), (ABSORB, 4, 4),
    (ABSORB, 11, 0), (ABSORB, 9, 1), (ABSORB, 10, 1), (ABSORB, 6, 4), (ABSORB, 11, 1), (ABSORB, 9, 2), (ABSORB, 7, 4), (ABSORB, 10, 2),
    (ABSORB, 8, 3), (VECTORS,), (ABSORB, 11, 2), (ABSORB, 9, 3), (ABSORB, 8, 4), (ABSORB, 11, 3), (ABSORB, 10, 3), (ABSORB, 9, 4),
    (ABSORB, 10, 4), (ABSORB, 11, 4), (VECTORS_LAST,),
)
FORWARD = (FORWARD_PLAN, FORWARD_CHUNKS)
BACKWARD = (BACKWARD_PLAN, BACKWARD_CHUNKS)


S = pltpu.SemaphoreType.DMA
FC = 768


def total(v):
    return jnp.sum(v, axis=0, keepdims=True)


class Copies:
    def __init__(self):
        self.sent = []

    def start(self, src, dst, send, recv, to, cond=True):
        cp = pltpu.make_async_remote_copy(src_ref=src, dst_ref=dst, send_sem=send, recv_sem=recv, device_id=to, device_id_type=MESH)
        if cond is True:
            cp.start()
        else:
            pl.when(cond)(cp.start)
        self.sent.append((cond, cp))

    def start_or_keep(self, mine, src, dst, send, recv, to, local):
        self.start(src, dst, send, recv, to, jnp.logical_not(mine))
        pl.when(mine)(pltpu.make_async_copy(src, dst, local).start)

    def arrive_or_keep(self, mine, dst, recv, local):
        pl.when(jnp.logical_not(mine))(lambda: arrive(dst, recv))
        pl.when(mine)(pltpu.make_async_copy(dst, dst, local).wait)

    def finish(self):
        for cond, cp in self.sent:
            if cond is True:
                cp.wait_send()
            else:
                pl.when(cond)(cp.wait_send)


def arrive(dst, recv):
    y, c, z, x = place()
    pltpu.make_async_remote_copy(src_ref=dst, dst_ref=dst, send_sem=recv, recv_sem=recv, device_id=device(y, c, z, x), device_id_type=MESH).wait_recv()


def forward_kernel(
    plan, chunks,
    xs, cot, seg, qw, kw, vw, ow, wup, wdt, small, upb,
    OUT, GF, GC, GST, LOWT, CTX, HID, GI, XO, Q, KT, V, E, CT, RS, WQ, VS,
    wt, wu, wd, pair_src, pair_dst, stage, xbuf, cbuf, sbuf, vec, vbuf, vb, ub,
    qb, kb, ktb, vb_, vtb, mask, ebuf, ctb, rsb, vsb, hid, gib, ctxb, n1, first, acc, rowbuf, outb, gsb, lowb, gcb,
    ps, pr, ws, wr, ls, xsnd, xrcv, fsnd, frcv, csnd, crcv, ssnd, srcv, vsnd, vrcv, lsem, osem, esem,
):
    y, c, z, x = place()
    j = 2 * z + x
    at = coords()
    partner = device(y, 1 - c, z, x)
    refs = (wt, wu, wd)
    copies = Copies()
    outs = []

    def put(src, dst):
        cp = pltpu.make_async_copy(src, dst, osem.at[len(outs)])
        cp.start()
        outs.append(cp)

    for i, w in enumerate((qw, kw, vw, ow)):
        pair_src[i] = w[...].astype(F32).T.astype(BF)
    vec[...] = jnp.zeros_like(vec)
    vec[0:8, 0:96] = small[...].astype(F32)
    vec[8:11, :] = upb[...].astype(F32)
    greet_all()
    copies.start(pair_src.at[:, pl.ds(48 * (1 - c), 48)], pair_dst, ps, pr, partner)

    def home(b):
        return (b // 2 == z) & (b % 2 == x) & (c == x)

    def send_tokens(src, dst, i, send, recv, local):
        m = (z + i) % 4
        mine = (z == m) & (x == c) & (z // 2 == c)
        copies.start_or_keep(mine, src.at[m], dst, send, recv, device(y, z // 2, m, c), local)

    for i in range(4):
        for k in range(2):
            m = (z + i) % 4
            mine = (z == m) & (x == c) & (k == c)
            copies.start_or_keep(mine, seg.at[m], sbuf.at[j], ssnd.at[2 * i + k], srcv.at[j], device(y, k, m, c), lsem.at[1])
    pltpu.make_async_copy(vec, vbuf.at[j], lsem.at[2]).start()
    for d in range(1, 8):
        o = (j + d) % 8
        copies.start(vec, vbuf.at[j], vsnd.at[d], vrcv.at[d], device(y, c, o // 2, o % 2))

    def pair_up():
        arrive(pair_dst, pr)
        own = pair_src[:, pl.ds(pl.multiple_of(48 * c, 16), 48), :]
        got = pair_dst[...]
        stage[...] = jnp.concatenate([jnp.where(c == 0, own, got), jnp.where(c == 0, got, own)], axis=-1)

    def source(ch):
        kind, i, _ = ch
        if kind == "t":
            return stage.at[i]
        if kind == "u":
            return wup.at[i]
        return wdt.at[i // 2, :, pl.ds(384 * (i % 2), 384)]

    def begin(u):
        ch = chunks[u]
        here = region(refs, ch, at)[0]
        pltpu.make_async_copy(source(ch), here, ls.at[u]).start()
        copies.start(source(ch), here, ws.at[u, 0, 0], wr.at[u, 0, 0], to_device(flip(at, ch[2][0])))

    def relay(u, s):
        ch = chunks[u]
        order = ch[2]
        if s == 0:
            pltpu.make_async_copy(source(ch), region(refs, ch, at)[0], ls.at[u]).wait()

        def parts(at, s):
            if s < 3:
                return [region(refs, ch, whole(at, order[:s]))]
            return [region(refs, ch, whole(v, order[: s - 1])) for v in (at, flip(at, order[s - 1]))]

        def forward(s, h):
            for k, part in enumerate(parts(at, s)[h]):
                copies.start(part, part, ws.at[u, s, 4 * h + k], wr.at[u, s, 4 * h + k], to_device(flip(at, order[s])))

        for h, half in enumerate(parts(flip(at, order[s]), s)):
            for k, part in enumerate(half):
                arrive(part, wr.at[u, s, 4 * h + k])
        if s == 0:
            forward(1, 0)
        elif s == 1:
            forward(2, 0)
            forward(3, 0)
        elif s == 2:
            forward(3, 1)
            forward(4, 0)
        elif s == 3:
            forward(4, 1)

    def token_block(i):
        b = 4 * c + i
        copies.arrive_or_keep(home(b), xbuf.at[b], xrcv.at[i], lsem.at[0])
        copies.start(xbuf.at[b], xbuf.at[b], fsnd.at[i], frcv.at[i], partner)

    def weight(i):
        return wt[i].reshape(768, 768)

    ready = []

    def vectors():
        if ready:
            return
        ready.append(True)
        pltpu.make_async_copy(vec, vbuf.at[j], lsem.at[2]).wait()
        for d in range(1, 8):
            arrive(vbuf.at[(j - d) % 8], vrcv.at[d])
        for b in range(8):
            copies.arrive_or_keep(home(b), sbuf.at[b], srcv.at[b], lsem.at[1])
        pieces = [vbuf[b] for b in range(8)]
        vb[...] = jnp.concatenate([p[:8, :96] for p in pieces], axis=-1)
        ub[...] = jnp.concatenate([p[8 + k : 9 + k, :] for p in pieces for k in range(3)], axis=-1)
        row = jnp.concatenate([sbuf[b] for b in range(8)], axis=-1).astype(F32)
        mine = jnp.concatenate([sbuf[4 * c + b] for b in range(4)], axis=-1).astype(F32)
        col = jnp.broadcast_to(row, (8, 1024)).T[:, :1]
        mask[...] = jnp.where(col == mine, 0.0, -1e30)

    def own_rows():
        return xbuf[pl.ds(4 * c, 4)].reshape(512, 768)

    def queries():
        vectors()
        put(xbuf.at[pl.ds(4 * c, 4)], XO)
        q = dot(own_rows(), weight(0), NT) + vb[0:1]
        qb[...] = (q.astype(BF).astype(F32) * 0.125).astype(BF)
        put(qb, Q)

    def keys():
        k = dot(xbuf[...].reshape(1024, 768), weight(1), NT)
        kb[...] = k.astype(BF)
        ktb[...] = k.T.astype(BF)
        put(ktb, KT)

    def values():
        vectors()
        v = dot(xbuf[...].reshape(1024, 768), weight(2), NT) + vb[1:2]
        vb_[...] = v.astype(BF)
        vtb[...] = v.T.astype(BF)
        put(vb_, V)

    def head(h):
        p, i = h // 2, h % 2
        cols = slice(128 * p, 128 * p + 128)
        half = lax.broadcasted_iota(jnp.int32, (512, 128), 1) // 64
        qp = qb[:, cols]
        s = dot(kb[:, cols], jnp.where(half == i, qp, jnp.zeros_like(qp)), NT) + mask[...]
        e = jnp.exp(s - jnp.max(s, axis=0, keepdims=True))
        r = 1.0 / jnp.sum(e, axis=0, keepdims=True)
        if h >= 2:
            pltpu.make_async_copy(ebuf.at[i], E.at[h - 2], esem.at[i]).wait()
        ebuf[i] = e.astype(BF)
        pltpu.make_async_copy(ebuf.at[i], E.at[h], esem.at[i]).start()
        rsb[h : h + 1, :] = r
        rows = slice(64 * h, 64 * h + 64)
        ctb[rows, :] = (dot(vtb[rows, :], ebuf[i]) * r).astype(BF)

    def branch():
        put(wt.at[pl.ds(0, 3)], WQ)
        put(ctb, CT)
        put(rsb, RS)
        ctxb[...] = ctb[...].astype(F32).T.astype(BF)
        put(ctxb, CTX)
        normed, inv = norm(own_rows().astype(F32) + dot(ctxb[...], weight(3), NT) + vb[2:3])
        n1[...] = normed
        rowbuf[:, 0:1] = inv
        first[...] = normed * vb[3:4] + vb[4:5]
        lowb[...] = first[...].T.astype(BF)
        put(lowb, LOWT)

    def up(f):
        cols = slice(FC * f, FC * (f + 1))
        inner = dot(first[...].astype(BF), wu[:, :, :, :, cols].reshape(768, FC)) + ub[:, cols]
        cdf = 0.5 * (1.0 + lax.erf(inner * 0.7071067811865476))
        pdf = jnp.exp(-0.5 * inner * inner) * 0.3989422804014327
        hid[:, cols] = (inner * cdf).astype(BF)
        gib[:, cols] = (cdf + inner * pdf).astype(BF)
        if f == 3:
            put(hid, HID)

    downs = []

    def down(b):
        part = None
        for q in range(4):
            cols = slice(768 * q + 384 * b, 768 * q + 384 * b + 384)
            d = dot(hid[:, cols], wd[:, :, :, :, :, cols].reshape(768, 384), NT)
            part = d if part is None else part + d
        if downs:
            acc[...] += part
        else:
            acc[...] = part
        downs.append(b)

    def second_norm():
        normed, inv = norm(first[...] + acc[...] + vb[5:6])
        gain = vb[6:7]
        outb[...] = (normed * gain + vb[7:8]).astype(BF)
        put(outb, OUT)
        for b in range(4):
            copies.arrive_or_keep(home(4 * c + b), cbuf.at[b], crcv.at[b], lsem.at[3])
        g = cbuf[...].reshape(512, 768).astype(F32)
        vsb[...] = jnp.zeros_like(vsb)
        vsb[6:7, :768] = total(g * normed)
        vsb[7:8, :768] = total(g)
        gss = norm_back(g * gain, normed, inv)
        gs = gss.astype(BF)
        vsb[5:6, :768] = total(gs.astype(F32))
        acc[...] = gss
        gsb[...] = gss.T.astype(BF)
        put(gsb, GST)
        return gs

    def back(gs):
        for f in range(3072 // FC):
            cols = slice(FC * f, FC * (f + 1))
            gi = (dot(gs, wd[:, :, :, :, :, cols].reshape(768, FC)) * gib[:, cols].astype(F32)).astype(BF)
            gib[:, cols] = gi
            vsb[8:9, cols] = total(gi.astype(F32))
            put(gib.at[:, cols], GI.at[:, cols])
            acc[...] += dot(gi, wu[:, :, :, :, cols].reshape(768, FC), NT)
        gf = acc[...]
        vsb[3:4, :768] = total(gf * n1[...])
        vsb[4:5, :768] = total(gf)
        gsf = norm_back(gf * vb[3:4], n1[...], rowbuf[:, 0:1])
        first[...] = gsf
        put(first, GF)
        gb = gsf.astype(BF)
        vsb[2:3, :768] = total(gb.astype(F32))
        VS[...] = vsb[...]
        gcb[...] = dot(gb, weight(3)).astype(BF)
        put(gcb, GC)

    def tokens(i):
        send_tokens(xs, xbuf.at[j], i, xsnd.at[i], xrcv.at[j % 4], lsem.at[0])

    def cotangent(i):
        send_tokens(cot, cbuf.at[j % 4], i, csnd.at[i], crcv.at[j % 4], lsem.at[3])

    def other_block(i):
        arrive(xbuf.at[4 * (1 - c) + i], frcv.at[i])

    work = {
        BEGIN: begin, RELAY: relay, TOKENS: tokens, BLOCK: token_block, OTHER: other_block, COTANGENT: cotangent, PAIR: pair_up,
        QUERY: queries, KEY: keys, VALUE: values, HEAD: head, BRANCH: branch, UP: up, DOWN: down,
    }
    for step, *args in plan:
        work[step](*args)
    back(second_norm())
    for i in range(2):
        pltpu.make_async_copy(ebuf.at[i], E.at[10 + i], esem.at[i]).wait()
    for cp in outs:
        cp.wait()
    copies.finish()


def forward_call(plan, chunks, xs, cot, seg, qw, kw, vw, ow, wup, wdt, small, upb):
    n = len(chunks)
    V_ = pltpu.VMEM
    row = (512, 768)
    return pl.pallas_call(
        partial(forward_kernel, plan, chunks),
        out_shape=[
            sds(row), sds(row, F32), sds(row), sds((768, 512)), sds((768, 512)), sds(row), sds((512, 3072)), sds((512, 3072)),
            sds((4, 128, 768)), sds(row), sds((768, 1024)), sds((1024, 768)), sds((12, 1024, 512)), sds((768, 512)), sds((16, 512), F32),
            sds((3, 2, 2, 2, 2, 48, 768)), sds((16, 3072), F32),
        ],
        in_specs=[ANY, ANY] + [VM] * 9,
        out_specs=[ANY] * 16 + [VM],
        scratch_shapes=[
            V_((4, 2, 2, 2, 2, 48, 768), BF), V_((2, 2, 4, 48, 3072), BF), V_((2, 2, 2, 2, 48, 3072), BF),
            V_((4, 96, 192), BF), V_((4, 48, 192), BF), V_((4, 48, 384), BF), V_((8, 128, 768), BF), V_((4, 128, 768), BF),
            V_((8, 1, 128), jnp.int32), V_((16, 128), F32), V_((8, 16, 128), F32), V_((8, 768), F32), V_((1, 3072), F32),
            V_(row, BF), V_((1024, 768), BF), V_((768, 1024), BF), V_((1024, 768), BF), V_((768, 1024), BF), V_((1024, 512), F32),
            V_((2, 1024, 512), BF), V_((768, 512), BF), V_((16, 512), F32), V_((16, 3072), F32), V_((512, 3072), BF), V_((512, 3072), BF),
            V_(row, BF), V_(row, F32), V_(row, F32), V_(row, F32), V_((512, 128), F32), V_(row, BF), V_((768, 512), BF), V_((768, 512), BF), V_(row, BF),
            S, S, S((n, 5, 8)), S((n, 5, 8)), S((n,)), S((4,)), S((4,)), S((4,)), S((4,)), S((4,)), S((4,)), S((8,)), S((8,)), S((8,)), S((8,)),
            S((4,)), S((24,)), S((2,)),
        ],
        name="forward",
        compiler_params=pltpu.CompilerParams(collective_id=1, has_side_effects=True, vmem_limit_bytes=63 * 2**20),
    )(xs, cot, seg, qw, kw, vw, ow, wup, wdt, small, upb)


def landing(at, order, s):
    spot = dict(at)
    for d in order[s + 1 :]:
        spot[d] = 1 - at[d]
    return whole(spot, order[:s])


def backward_kernel(
    plan, chunks,
    OUT, GF, GC, GST, LOWT, CTX, HID, GI, XO, Q, KT, V, E, CT, RS, WQ, VS,
    LO, IG, D4, DU, DD, VO,
    gt, gu, gd, rt, ru, rd, hid, gib, gst, lowt, ctxb, xb, qb, ktb, vb, ctb, gcb, gct, gfb, wq, ebuf,
    dqt, dkb, dvb, dkr, dvr, igb, rcol, vpack, vrecv, vsum, vrecv2, pairs, pairr, fin,
    isem, esem, lsem, ks, kr, os_, or_, gs, gr, vs_, vr, ws, wr, ps, pr,
):
    y, c, z, x = place()
    j = 2 * z + x
    at = coords()
    partner = device(y, 1 - c, z, x)
    G, R = (gt, gu, gd), (rt, ru, rd)
    copies = Copies()
    loads = {}
    for src, dst, name in (
        (GST, gst, "gst"), (HID, hid, "hid"), (LOWT, lowt, "lowt"), (GI, gib, "gi"), (V, vb, "v"), (Q, qb, "q"), (GC, gcb, "gc"), (KT, ktb, "kt"),
        (CT, ctb, "ct"), (CTX, ctxb, "ctx"), (XO, xb, "x"), (WQ, wq, "wq"), (GF, gfb, "gf"),
    ):
        cp = pltpu.make_async_copy(src, dst, isem.at[len(loads)])
        cp.start()
        loads[name] = cp
    for i in range(2):
        pltpu.make_async_copy(E.at[i], ebuf.at[i], esem.at[i]).start()

    def need(*names):
        for n in names:
            if n in loads:
                loads.pop(n).wait()

    greet_all()

    def send_home(src, dst, k, send, recv, local):
        b = 4 * c + k
        mine = (x == c) & (b // 2 == z) & (b % 2 == x)
        copies.start_or_keep(mine, src, dst, send, recv, device(y, x, b // 2, b % 2), local)

    def send_out(k):
        send_home(OUT.at[pl.ds(128 * k, 128)], LO.at[z], k, os_.at[0, k], or_.at[0, z], lsem.at[0])

    def send_grad(k):
        send_home(igb.at[pl.ds(128 * k, 128)], IG.at[z], k, os_.at[1, k], or_.at[1, z], lsem.at[1])

    def halves(order, s, at):
        if s == 3:
            return [flip(at, order[2]), at]
        return [at]

    def stage(ch, s, at, h):
        order = ch[2]
        spot = landing(at, order, s)
        own = whole(at, order[:s])
        if s == 3:
            own[order[2]] = spot[order[2]] = halves(order, s, at)[h][order[2]]
        return region(G, ch, own), region(R, ch, spot)

    def launch(u, s):
        ch = chunks[u]
        to = flip(at, ch[2][s])
        for h in range(2 if s == 3 else 1):
            for k, (src, dst) in enumerate(zip(*stage(ch, s, to, h))):
                copies.start(src, dst, gs.at[u, s, 4 * h + k], gr.at[u, s, 4 * h + k], to_device(to))

    def take(u, s, h):
        for k, (own, got) in enumerate(zip(*stage(chunks[u], s, at, h))):
            arrive(got, gr.at[u, s, 4 * h + k])
            own[...] = own[...] + got[...]

    def absorb(u, s):
        kind, i, order = ch = chunks[u]
        if s > 0:
            if s == 2:
                take(u, 3, 1)
            take(u, s, 0)
            launch(u, s - 1)
            return
        (own,), (got,) = stage(ch, 0, at, 0)
        arrive(got, gr.at[u, 0, 0])
        done = own[...].astype(F32) + got[...].astype(F32)
        if kind == "u":
            DU[i] = done
        elif kind == "d":
            DD[i // 2, :, 384 * (i % 2) : 384 * (i % 2) + 384] = done
        else:
            lo, hi = done[:, :192], done[:, 192:]
            fin[i, pl.ds(pl.multiple_of(48 * c, 16), 48), :] = jnp.where(c == 0, lo, hi)
            pairs[i] = jnp.where(c == 0, hi, lo)
            copies.start(pairs.at[i], pairr.at[i], ps.at[i], pr.at[i], partner)

    def grad_u(i):
        need("lowt", "gi")
        rows = lowt[...].reshape(2, 2, 4, 48, 512)[:, :, i].reshape(192, 512)
        gu[:, :, i] = dot(rows, gib[...]).astype(BF).reshape(2, 2, 48, 3072)

    def grad_d(i):
        need("gst", "hid")
        rows = gst[...].reshape(2, 2, 2, 2, 48, 512)[:, :, :, i // 2].reshape(384, 512)
        for q in range(4):
            cols = slice(768 * q + 384 * (i % 2), 768 * q + 384 * (i % 2) + 384)
            gd[:, :, :, i // 2, :, cols] = dot(rows, hid[:, cols]).astype(BF).reshape(2, 2, 2, 48, 384)

    shape = (2, 2, 2, 2, 48, 768)

    def grad_t(i):
        if i == 3:
            need("gf", "ctx")
            gt[3] = dot(gfb[...].T.astype(BF), ctxb[...]).astype(BF).reshape(shape)
        elif i == 0:
            need("x")
            gt[0] = dot(dqt[...], xb[...].reshape(512, 768)).astype(BF).reshape(shape)
        else:
            src = dkr if i == 1 else dvr
            gt[i] = dot(src[...].astype(F32).T.astype(BF), xb[...].reshape(512, 768)).astype(BF).reshape(shape)

    def ready():
        need("gc", "v", "q", "kt", "ct")
        gct[...] = gcb[...].astype(F32).T.astype(BF)
        rcol[...] = RS[...].T

    def head(h):
        p, i = h // 2, h % 2
        if h == 0:
            ready()
        cols = slice(128 * p, 128 * p + 128)
        rows = slice(64 * h, 64 * h + 64)
        qp = qb[:, cols]
        half = lax.broadcasted_iota(jnp.int32, (512, 128), 1) // 64
        gm = jnp.where(half == i, gcb[:, cols].astype(F32) * rcol[:, h : h + 1], 0.0).astype(BF)
        qm = jnp.where(half == i, qp, jnp.zeros_like(qp))
        delta = total(ctb[rows, :].astype(F32) * gct[rows, :].astype(F32)) * RS[h : h + 1, :]
        pltpu.make_async_copy(E.at[h], ebuf.at[i], esem.at[i]).wait()
        ds = (ebuf[i].astype(F32) * (dot(vb[:, cols], gm, NT) - delta)).astype(BF)
        dv = dot(ebuf[i], gm)
        dk = dot(ds, qm)
        dqt[rows, :] = (dot(ktb[rows, :], ds) * 0.125).astype(BF)
        if h + 2 < 12:
            pltpu.make_async_copy(E.at[h + 2], ebuf.at[i], esem.at[i]).start()
        dkb[:, cols] = dk.astype(BF) if i == 0 else (dkb[:, cols].astype(F32) + dk).astype(BF)
        dvb[:, cols] = dv.astype(BF) if i == 0 else (dvb[:, cols].astype(F32) + dv).astype(BF)

    theirs = pl.ds(pl.multiple_of(512 * (1 - c), 128), 512)
    ours = pl.ds(pl.multiple_of(512 * c, 128), 512)

    def exchange():
        copies.start(dkb.at[theirs], dkr, ks.at[0], kr.at[0], partner)
        copies.start(dvb.at[theirs], dvr, ks.at[1], kr.at[1], partner)

    def merge():
        arrive(dkr, kr.at[0])
        arrive(dvr, kr.at[1])
        dkr[...] = (dkb[ours].astype(F32) + dkr[...].astype(F32)).astype(BF)
        dvr[...] = (dvb[ours].astype(F32) + dvr[...].astype(F32)).astype(BF)

    def token_grads():
        need("gf", "wq")
        dq = dqt[...].astype(F32).T
        ig = gfb[...] + dot(dq.astype(BF), wq[0].reshape(768, 768))
        ig = ig + dot(dkr[...], wq[1].reshape(768, 768)) + dot(dvr[...], wq[2].reshape(768, 768))
        low = jnp.concatenate([total(dq), total(dvr[...].astype(F32)), VS[2:8, :768]], axis=0)
        vpack[...] = jnp.zeros_like(vpack)
        for b in range(8):
            vpack[b, 0:8, 0:96] = low[:, 96 * b : 96 * b + 96]
            vpack[b, 8:9, :] = VS[8:9, 384 * b : 384 * b + 384]
        for d in range(1, 8):
            o = (j + d) % 8
            copies.start(vpack.at[o], vrecv.at[d], vs_.at[d], vr.at[d], device(y, c, o // 2, o % 2))
        igb[...] = ig.astype(BF)
        for k in range(4):
            send_grad(k)

    def vectors_first():
        acc = vpack[j]
        for d in range(1, 8):
            arrive(vrecv.at[d], vr.at[d])
            acc = acc + vrecv[d]
        vsum[...] = acc
        me = 2 * y + c
        for d in range(1, 4):
            copies.start(vsum, vrecv2.at[d], ws.at[d], wr.at[d], ((me + d) % 4, j))

    def vectors_last():
        acc = vsum[...]
        for d in range(1, 4):
            arrive(vrecv2.at[d], wr.at[d])
            acc = acc + vrecv2[d]
        VO[...] = acc

    work = {
        LAUNCH: lambda u: launch(u, 4), ABSORB: lambda u, s: absorb(u, 4 - s), HOME: send_out, GRAD_U: grad_u, GRAD_D: grad_d, GRAD_T: grad_t,
        HEAD_BACK: head, EXCHANGE: exchange, MERGE: merge, INPUT_GRAD: token_grads, VECTORS: vectors_first, VECTORS_LAST: vectors_last,
    }
    for step, *args in plan:
        work[step](*args)
    for i in range(4):
        arrive(pairr.at[i], pr.at[i])
        fin[i, pl.ds(pl.multiple_of(48 * (1 - c), 16), 48), :] = pairr[i]
        D4[i] = fin[i].T
    for w, out in ((0, LO), (1, IG)):
        for m in range(4):
            copies.arrive_or_keep((m == z) & (x == c) & (z // 2 == c), out.at[m], or_.at[w, m], lsem.at[w])
    copies.finish()


def backward_call(plan, chunks, OUT, GF, GC, GST, LOWT, CTX, HID, GI, XO, Q, KT, V, E, CT, RS, WQ, VS):
    n = len(chunks)
    V_ = pltpu.VMEM
    row = (512, 768)
    col = (768, 512)
    sets = [V_((4, 2, 2, 2, 2, 48, 768), BF), V_((2, 2, 4, 48, 3072), BF), V_((2, 2, 2, 2, 48, 3072), BF)]
    return pl.pallas_call(
        partial(backward_kernel, plan, chunks),
        out_shape=[sds((4, 128, 768)), sds((4, 128, 768))] + [sds((4, 192, 96), F32), sds((4, 48, 384), F32), sds((2, 48, 768), F32), sds((16, 384), F32)],
        in_specs=[ANY] * 14 + [VM, ANY, VM],
        out_specs=[ANY, ANY] + [VM] * 4,
        scratch_shapes=sets + sets + [
            V_((512, 3072), BF), V_((512, 3072), BF), V_(col, BF), V_(col, BF), V_(row, BF), V_((4, 128, 768), BF), V_(row, BF),
            V_((768, 1024), BF), V_((1024, 768), BF), V_(col, BF), V_(row, BF), V_(col, BF), V_(row, F32), V_((3, 2, 2, 2, 2, 48, 768), BF), V_((2, 1024, 512), BF),
            V_(col, BF), V_((1024, 768), BF), V_((1024, 768), BF), V_(row, BF), V_(row, BF), V_(row, BF), V_((512, 16), F32),
            V_((8, 16, 384), F32), V_((8, 16, 384), F32), V_((16, 384), F32), V_((4, 16, 384), F32), V_((4, 48, 192), F32), V_((4, 48, 192), F32), V_((4, 96, 192), F32),
            S((13,)), S((2,)), S((2,)), S((2,)), S((2,)), S((2, 4)), S((2, 4)), S((n, 5, 8)), S((n, 5, 8)), S((8,)), S((8,)), S((4,)), S((4,)), S((4,)), S((4,)),
        ],
        name="backward",
        compiler_params=pltpu.CompilerParams(collective_id=2, has_side_effects=True, vmem_limit_bytes=63 * 2**20),
    )(OUT, GF, GC, GST, LOWT, CTX, HID, GI, XO, Q, KT, V, E, CT, RS, WQ, VS)


def rows_on_chips(
    inputs, segment_ids, query_weight, query_bias, key_weight, value_weight, value_bias, output_weight, output_bias,
    first_gain, first_shift, up_weight, up_bias, down_weight, down_bias, second_gain, second_shift, cotangent,
):
    small = jnp.stack([query_bias, value_bias, output_bias, first_gain, first_shift, down_bias, second_gain, second_shift])
    kept = forward_call(
        *FORWARD, inputs.reshape(4, 128, 768), cotangent.reshape(4, 128, 768), segment_ids.reshape(4, 1, 128),
        query_weight, key_weight, value_weight, output_weight, up_weight.reshape(4, 48, 384), down_weight.T.reshape(2, 48, 768),
        small, up_bias.reshape(3, 128),
    )
    LO, IG, D4, DU, DD, VO = backward_call(*BACKWARD, *kept)
    v = VO[:8, :96]
    s = (4, 1, 128, 768)
    return (
        LO.reshape(s), IG.reshape(s), D4[0], v[0], D4[1], D4[2], v[1], D4[3], v[2], v[3], v[4], DU.reshape(192, 384), VO[8], DD.reshape(96, 768).T, v[5], v[6], v[7],
    )


EPSILON = 1e-12
NEGATIVE = -1e30


def product(left, right, form):
    return jnp.einsum(form, left, right, preferred_element_type=jnp.float32)


def normalize(hidden, gain, shift):
    centred = hidden - jnp.mean(hidden, axis=-1, keepdims=True)
    scale_inv = lax.rsqrt(jnp.mean(centred * centred, axis=-1, keepdims=True) + EPSILON)
    normed = centred * scale_inv
    return (normed * gain + shift, normed, scale_inv)


def normalize_back(grad_normed, normed, scale_inv):
    centred_grad = grad_normed - jnp.mean(grad_normed, axis=-1, keepdims=True)
    return scale_inv * (
        centred_grad - normed * jnp.mean(grad_normed * normed, axis=-1, keepdims=True)
    )


def same_passage(query_pair, key_pair):
    return jnp.all(query_pair[:, :, None, :] == key_pair[:, None, :, :], axis=-1)[:, None]


def micro_step(shared, tokens, passage_ids, cotan):
    (
        weight_query,
        weight_key,
        weight_value,
        weight_out,
        weight_up,
        weight_down,
        bias_query,
        bias_value,
        bias_out,
        gain_first,
        shift_first,
        bias_up,
        bias_down,
        gain_second,
        shift_second,
    ) = shared
    bias_query = bias_query.astype(jnp.float32)
    bias_value = bias_value.astype(jnp.float32)
    bias_out = bias_out.astype(jnp.float32)
    gain_first = gain_first.astype(jnp.float32)
    shift_first = shift_first.astype(jnp.float32)
    bias_up = bias_up.astype(jnp.float32)
    bias_down = bias_down.astype(jnp.float32)
    gain_second = gain_second.astype(jnp.float32)
    shift_second = shift_second.astype(jnp.float32)
    row_count, seq_count, width = tokens.shape
    token_count = row_count * seq_count
    scale = HD ** (-0.5)
    flat = tokens.reshape(token_count, width)
    queries = (product(flat, weight_query, "md,de->me") + bias_query).astype(jnp.bfloat16)
    keys = product(flat, weight_key, "md,de->me").astype(jnp.bfloat16)
    values = (product(flat, weight_value, "md,de->me") + bias_value).astype(jnp.bfloat16)
    query_four = queries.reshape(row_count, seq_count, HEADS, HD)
    pair_local = jnp.stack((passage_ids // 256, passage_ids % 256), axis=-1).astype(jnp.bfloat16)
    key_rows = keys.reshape(row_count, seq_count, width)
    value_rows = values.reshape(row_count, seq_count, width)
    key_local = key_rows.reshape(row_count, seq_count, HEADS, HD)
    value_local = value_rows.reshape(row_count, seq_count, HEADS, HD)
    running_max = jnp.full((row_count, HEADS, seq_count), NEGATIVE, jnp.float32)
    running_acc = jnp.zeros((row_count, seq_count, HEADS, HD), jnp.float32)
    key_piece = lax.all_gather(key_rows, "blk", axis=1, tiled=True)
    value_piece = lax.all_gather(value_rows, "blk", axis=1, tiled=True)
    pair_piece = lax.all_gather(pair_local, "blk", axis=1, tiled=True)
    count = key_piece.shape[1]
    key_four = key_piece.reshape(row_count, count, HEADS, HD)
    value_four = value_piece.reshape(row_count, count, HEADS, HD)
    allowed = same_passage(pair_local, pair_piece)
    scores = jnp.where(allowed, product(query_four, key_four, "rqhd,rkhd->rhqk") * scale, NEGATIVE)
    fresh_max = jnp.maximum(running_max, jnp.max(scores, axis=-1))
    weights = jnp.where(allowed, jnp.exp(scores - fresh_max[..., None]), 0.0)
    decay = jnp.exp(running_max - fresh_max)
    running_sum = jnp.sum(weights, axis=-1)
    mixed = product(weights.astype(jnp.bfloat16), value_four, "rhqk,rkhd->rqhd")
    running_acc = running_acc * jnp.swapaxes(decay, 1, 2)[..., None] + mixed
    running_max, running_sum, running_acc = (fresh_max, running_sum, running_acc)
    log_total = running_max + jnp.log(running_sum)
    attended = running_acc / jnp.swapaxes(running_sum, 1, 2)[..., None]
    context = attended.reshape(token_count, width).astype(jnp.bfloat16)
    branch = product(context, weight_out, "md,de->me") + bias_out
    first, normed_first, inv_first = normalize(
        flat.astype(jnp.float32) + branch, gain_first, shift_first
    )
    first_low = first.astype(jnp.bfloat16)
    inner = product(first_low, weight_up, "md,df->mf") + bias_up
    activation, gelu_pull = jax.vjp(partial(jax.nn.gelu, approximate=False), inner)
    hidden = activation.astype(jnp.bfloat16)
    second = product(hidden, weight_down, "mf,fd->md") + bias_down
    output, normed_second, inv_second = normalize(first + second, gain_second, shift_second)
    upstream = cotan.reshape(token_count, width).astype(jnp.float32)
    grad_gain_second = jnp.sum(upstream * normed_second, axis=0, keepdims=True)
    grad_shift_second = jnp.sum(upstream, axis=0, keepdims=True)
    grad_sum_second = normalize_back(upstream * gain_second, normed_second, inv_second)
    grad_second = grad_sum_second.astype(jnp.bfloat16)
    grad_weight_down = product(hidden, grad_second, "mf,md->fd")
    grad_bias_down = jnp.sum(grad_second.astype(jnp.float32), axis=0, keepdims=True)
    grad_inner = gelu_pull(product(grad_second, weight_down, "md,fd->mf"))[0].astype(jnp.bfloat16)
    grad_weight_up = product(first_low, grad_inner, "md,mf->df")
    grad_bias_up = jnp.sum(grad_inner.astype(jnp.float32), axis=0, keepdims=True)
    grad_first = grad_sum_second + product(grad_inner, weight_up, "mf,df->md")
    grad_gain_first = jnp.sum(grad_first * normed_first, axis=0, keepdims=True)
    grad_shift_first = jnp.sum(grad_first, axis=0, keepdims=True)
    grad_sum_first = normalize_back(grad_first * gain_first, normed_first, inv_first)
    grad_branch = grad_sum_first.astype(jnp.bfloat16)
    grad_weight_out = product(context, grad_branch, "md,me->de")
    grad_bias_out = jnp.sum(grad_branch.astype(jnp.float32), axis=0, keepdims=True)
    grad_context = product(grad_branch, weight_out, "me,de->md").astype(jnp.bfloat16)
    grad_context_four = grad_context.reshape(row_count, seq_count, HEADS, HD)
    delta = jnp.swapaxes(jnp.sum(grad_context_four.astype(jnp.float32) * attended, axis=-1), 1, 2)
    key_piece = lax.all_gather(key_rows, "blk", axis=1, tiled=True)
    value_piece = lax.all_gather(value_rows, "blk", axis=1, tiled=True)
    pair_piece = lax.all_gather(pair_local, "blk", axis=1, tiled=True)
    count = key_piece.shape[1]
    key_four = key_piece.reshape(row_count, count, HEADS, HD)
    value_four = value_piece.reshape(row_count, count, HEADS, HD)
    allowed = same_passage(pair_local, pair_piece)
    scores = jnp.where(allowed, product(query_four, key_four, "rqhd,rkhd->rhqk") * scale, NEGATIVE)
    probs = jnp.where(allowed, jnp.exp(scores - log_total[..., None]), 0.0)
    grad_probs = product(grad_context_four, value_four, "rqhd,rkhd->rhqk")
    grad_scores = (probs * (grad_probs - delta[..., None])).astype(jnp.bfloat16)
    grad_query_acc = product(grad_scores, key_four, "rhqk,rkhd->rqhd") * scale
    grad_queries = grad_query_acc.reshape(token_count, width).astype(jnp.bfloat16)
    pair_wide = pair_local.astype(jnp.float32)
    sent = (
        queries.reshape(row_count, seq_count, width).astype(jnp.float32),
        grad_context.reshape(row_count, seq_count, width).astype(jnp.float32),
        jnp.swapaxes(log_total, 1, 2),
        jnp.swapaxes(delta, 1, 2),
        pair_wide,
    )
    query_piece = lax.all_gather(sent[0], "blk", axis=1, tiled=True)
    context_piece = lax.all_gather(sent[1], "blk", axis=1, tiled=True)
    total_piece = lax.all_gather(sent[2], "blk", axis=1, tiled=True)
    delta_piece = lax.all_gather(sent[3], "blk", axis=1, tiled=True)
    pair_piece = lax.all_gather(sent[4], "blk", axis=1, tiled=True)
    count = query_piece.shape[1]
    query_part = query_piece.astype(jnp.bfloat16).reshape(row_count, count, HEADS, HD)
    context_part = context_piece.astype(jnp.bfloat16).reshape(row_count, count, HEADS, HD)
    total_part = jnp.swapaxes(total_piece, 1, 2)
    delta_part = jnp.swapaxes(delta_piece, 1, 2)
    allowed = same_passage(pair_piece, pair_wide)
    scores = jnp.where(allowed, product(query_part, key_local, "rqhd,rkhd->rhqk") * scale, NEGATIVE)
    probs = jnp.where(allowed, jnp.exp(scores - total_part[..., None]), 0.0)
    grad_value_acc = product(probs.astype(jnp.bfloat16), context_part, "rhqk,rqhd->rkhd")
    grad_probs = product(context_part, value_local, "rqhd,rkhd->rhqk")
    grad_scores = (probs * (grad_probs - delta_part[..., None])).astype(jnp.bfloat16)
    grad_key_acc = product(grad_scores, query_part, "rhqk,rqhd->rkhd") * scale
    grad_key_acc, grad_value_acc = (grad_key_acc, grad_value_acc)
    grad_keys = grad_key_acc.reshape(token_count, width).astype(jnp.bfloat16)
    grad_values = grad_value_acc.reshape(token_count, width).astype(jnp.bfloat16)
    grad_weight_query = product(flat, grad_queries, "md,me->de")
    grad_bias_query = jnp.sum(grad_queries.astype(jnp.float32), axis=0, keepdims=True)
    grad_weight_key = product(flat, grad_keys, "md,me->de")
    grad_weight_value = product(flat, grad_values, "md,me->de")
    grad_bias_value = jnp.sum(grad_values.astype(jnp.float32), axis=0, keepdims=True)
    grad_tokens = (
        grad_sum_first
        + product(grad_queries, weight_query, "me,de->md")
        + product(grad_keys, weight_key, "me,de->md")
        + product(grad_values, weight_value, "me,de->md")
    )
    contributions = (
        grad_weight_query,
        grad_weight_key,
        grad_weight_value,
        grad_weight_out,
        grad_weight_up,
        grad_weight_down,
        grad_bias_query,
        grad_bias_value,
        grad_bias_out,
        grad_gain_first,
        grad_shift_first,
        grad_bias_up,
        grad_bias_down,
        grad_gain_second,
        grad_shift_second,
    )
    return (
        output.astype(jnp.bfloat16).reshape(row_count, seq_count, width),
        grad_tokens.astype(jnp.bfloat16).reshape(row_count, seq_count, width),
        contributions,
    )


def general(
    inputs,
    segment_ids,
    query_weight,
    query_bias,
    key_weight,
    value_weight,
    value_bias,
    output_weight,
    output_bias,
    first_gain,
    first_shift,
    up_weight,
    up_bias,
    down_weight,
    down_bias,
    second_gain,
    second_shift,
    cotangent,
):
    outputs = []
    input_grads = []
    totals = None
    widened = (
        lax.all_gather(query_weight, "blk", axis=1, tiled=True),
        lax.all_gather(key_weight, "blk", axis=1, tiled=True),
        lax.all_gather(value_weight, "blk", axis=1, tiled=True),
        lax.all_gather(output_weight, "blk", axis=1, tiled=True),
        lax.all_gather(up_weight, "blk", axis=1, tiled=True),
        lax.all_gather(down_weight, "blk", axis=1, tiled=True),
        lax.all_gather(query_bias.reshape(1, -1), "blk", axis=1, tiled=True),
        lax.all_gather(value_bias.reshape(1, -1), "blk", axis=1, tiled=True),
        lax.all_gather(output_bias.reshape(1, -1), "blk", axis=1, tiled=True),
        lax.all_gather(first_gain.reshape(1, -1), "blk", axis=1, tiled=True),
        lax.all_gather(first_shift.reshape(1, -1), "blk", axis=1, tiled=True),
        lax.all_gather(up_bias.reshape(1, -1), "blk", axis=1, tiled=True),
        lax.all_gather(down_bias.reshape(1, -1), "blk", axis=1, tiled=True),
        lax.all_gather(second_gain.reshape(1, -1), "blk", axis=1, tiled=True),
        lax.all_gather(second_shift.reshape(1, -1), "blk", axis=1, tiled=True),
    )
    complete = (
        lax.all_gather(widened[0], "dp", axis=0, tiled=True),
        lax.all_gather(widened[1], "dp", axis=0, tiled=True),
        lax.all_gather(widened[2], "dp", axis=0, tiled=True),
        lax.all_gather(widened[3], "dp", axis=0, tiled=True),
        lax.all_gather(widened[4], "dp", axis=0, tiled=True),
        lax.all_gather(widened[5], "dp", axis=0, tiled=True),
    )
    shared = tuple(complete) + tuple(widened[6:])
    for batch_index in range(inputs.shape[0]):
        layer_out, layer_grad, contributions = micro_step(
            shared, inputs[batch_index], segment_ids[batch_index], cotangent[batch_index]
        )
        outputs.append(layer_out)
        input_grads.append(layer_grad)
        if totals is None:
            totals = contributions
        else:
            totals = tuple((earlier + latest for earlier, latest in zip(totals, contributions)))
    narrowed = (
        lax.psum_scatter(totals[0], "blk", scatter_dimension=1, tiled=True),
        lax.psum_scatter(totals[1], "blk", scatter_dimension=1, tiled=True),
        lax.psum_scatter(totals[2], "blk", scatter_dimension=1, tiled=True),
        lax.psum_scatter(totals[3], "blk", scatter_dimension=1, tiled=True),
        lax.psum_scatter(totals[4], "blk", scatter_dimension=1, tiled=True),
        lax.psum_scatter(totals[5], "blk", scatter_dimension=1, tiled=True),
        lax.psum_scatter(totals[6], "blk", scatter_dimension=1, tiled=True),
        lax.psum_scatter(totals[7], "blk", scatter_dimension=1, tiled=True),
        lax.psum_scatter(totals[8], "blk", scatter_dimension=1, tiled=True),
        lax.psum_scatter(totals[9], "blk", scatter_dimension=1, tiled=True),
        lax.psum_scatter(totals[10], "blk", scatter_dimension=1, tiled=True),
        lax.psum_scatter(totals[11], "blk", scatter_dimension=1, tiled=True),
        lax.psum_scatter(totals[12], "blk", scatter_dimension=1, tiled=True),
        lax.psum_scatter(totals[13], "blk", scatter_dimension=1, tiled=True),
        lax.psum_scatter(totals[14], "blk", scatter_dimension=1, tiled=True),
    )
    matrix_sums = (
        lax.psum_scatter(narrowed[0], "dp", scatter_dimension=0, tiled=True),
        lax.psum_scatter(narrowed[1], "dp", scatter_dimension=0, tiled=True),
        lax.psum_scatter(narrowed[2], "dp", scatter_dimension=0, tiled=True),
        lax.psum_scatter(narrowed[3], "dp", scatter_dimension=0, tiled=True),
        lax.psum_scatter(narrowed[4], "dp", scatter_dimension=0, tiled=True),
        lax.psum_scatter(narrowed[5], "dp", scatter_dimension=0, tiled=True),
    )
    vector_sums = lax.psum(
        (
            narrowed[6],
            narrowed[7],
            narrowed[8],
            narrowed[9],
            narrowed[10],
            narrowed[11],
            narrowed[12],
            narrowed[13],
            narrowed[14],
        ),
        "dp",
    )
    return (
        jnp.stack(outputs),
        jnp.stack(input_grads),
        matrix_sums[0],
        vector_sums[0].reshape(-1),
        matrix_sums[1],
        matrix_sums[2],
        vector_sums[1].reshape(-1),
        matrix_sums[3],
        vector_sums[2].reshape(-1),
        vector_sums[3].reshape(-1),
        vector_sums[4].reshape(-1),
        matrix_sums[4],
        vector_sums[5].reshape(-1),
        matrix_sums[5],
        vector_sums[6].reshape(-1),
        vector_sums[7].reshape(-1),
        vector_sums[8].reshape(-1),
    )


def solution(mesh):
    in_specs = (
        P(None, "dp", "blk", None),
        P(None, "dp", "blk"),
        P("dp", "blk"),
        P("blk"),
        P("dp", "blk"),
        P("dp", "blk"),
        P("blk"),
        P("dp", "blk"),
        P("blk"),
        P("blk"),
        P("blk"),
        P("dp", "blk"),
        P("blk"),
        P("dp", "blk"),
        P("blk"),
        P("blk"),
        P("blk"),
        P(None, "dp", "blk", None),
    )
    out_specs = (
        P(None, "dp", "blk", None),
        P(None, "dp", "blk", None),
        P("dp", "blk"),
        P("blk"),
        P("dp", "blk"),
        P("dp", "blk"),
        P("blk"),
        P("dp", "blk"),
        P("blk"),
        P("blk"),
        P("blk"),
        P("dp", "blk"),
        P("blk"),
        P("dp", "blk"),
        P("blk"),
        P("blk"),
        P("blk"),
    )
    small = mesh.shape["dp"] == 4 and mesh.shape["blk"] == 8

    def on_device(*arrays):
        if small and arrays[0].shape == (4, 1, 128, 768):
            return rows_on_chips(*arrays)
        return general(*arrays)

    return jax.shard_map(
        on_device, mesh=mesh, in_specs=in_specs, out_specs=out_specs, check_vma=False
    )
```

```python
from functools import partial

import jax
import jax.numpy as jnp
from jax import lax
from jax.experimental import pallas as pl
from jax.experimental.pallas import tpu as pltpu
from jax.sharding import PartitionSpec as P

MESH = pl.DeviceIdType.MESH
BF = jnp.bfloat16
F32 = jnp.float32


(BEGIN, RELAY, TOKENS, BLOCK, OTHER, COTANGENT, PAIR, QUERY, KEY, VALUE, HEAD, BRANCH, UP, DOWN) = range(14)
(LAUNCH, ABSORB, HOME, GRAD_U, GRAD_D, GRAD_T, HEAD_BACK, EXCHANGE, MERGE, INPUT_GRAD, VECTORS, VECTORS_LAST) = range(14, 26)


def place():
    dp = lax.axis_index("dp")
    blk = lax.axis_index("blk")
    return dp // 2, dp % 2, blk // 2, blk % 2


def device(y, c, z, x):
    return (y * 2 + c, z * 2 + x)


def greet_all():
    y, c, z, x = place()
    me = (y * 2 + c) * 8 + z * 2 + x
    barrier = pltpu.get_barrier_semaphore()

    def greet(i, carry):
        other = (me + i) % 32
        pl.semaphore_signal(barrier, inc=1, device_id=(other // 8, other % 8), device_id_type=MESH)
        return carry

    lax.fori_loop(1, 32, greet, 0)
    return lambda: pl.semaphore_wait(barrier, 31)


def coords():
    y, c, z, x = place()
    return {"a": z // 2, "b": z % 2, "x": x, "y": y, "c": c}


def to_device(at):
    return device(at["y"], at["c"], 2 * at["a"] + at["b"], at["x"])


def flip(at, dim):
    return {**at, dim: 1 - at[dim]}


def whole(at, dims):
    return {k: (None if k in dims else v) for k, v in at.items()}


def span(v):
    return slice(None) if v is None else v


def each(v):
    return (0, 1) if v is None else (v,)


def lanes(start, size):
    return pl.ds(start if isinstance(start, int) else pl.multiple_of(start, 128), size)


def region(refs, chunk, at):
    wt, wu, wd = refs
    kind, i, _ = chunk
    a, b, x, y, c = (at[k] for k in "abxyc")
    if kind == "t":
        cols = slice(None) if y is None else lanes(384 * y, 384)
        return [wt.at[i, span(a), span(b), span(x), span(c), :, cols]]
    if kind == "u":
        if a is None and b is None and x is None:
            return [wu.at[span(y), span(c), i]]
        return [wu.at[span(y), span(c), i, :, lanes(384 * (4 * p + 2 * q + r), 384)] for p in each(a) for q in each(b) for r in each(x)]
    return [wd.at[span(a), span(b), span(x), i // 2, :, lanes(768 * (2 * p + q) + 384 * (i % 2), 384)] for p in each(y) for q in each(c)]


HEADS, HD = 12, 64
NT = (((1,), (1,)), ((), ()))
NN = (((1,), (0,)), ((), ()))


def dot(l, r, dims=NN):
    return lax.dot_general(l, r, dims, preferred_element_type=F32)


VM = pl.BlockSpec(memory_space=pltpu.VMEM)
ANY = pl.BlockSpec(memory_space=pl.ANY)


def sds(shape, dt=BF):
    return jax.ShapeDtypeStruct(shape, dt)


def norm(h):
    centred = h - jnp.mean(h, axis=-1, keepdims=True)
    inv = lax.rsqrt(jnp.mean(centred * centred, axis=-1, keepdims=True) + 1e-12)
    return centred * inv, inv


def norm_back(g, normed, inv):
    return inv * (g - jnp.mean(g, axis=-1, keepdims=True) - normed * jnp.mean(g * normed, axis=-1, keepdims=True))


FORWARD_CHUNKS = (
    ("t", 0, "abxyc"), ("t", 1, "abxyc"), ("t", 2, "abyxc"), ("t", 3, "abxyc"), ("u", 0, "abxyc"), ("u", 1, "abyxc"), ("u", 2, "abxyc"),
    ("u", 3, "axbyc"), ("d", 0, "abyxc"), ("d", 2, "abxyc"), ("d", 1, "abyxc"), ("d", 3, "abxyc"),
)
FORWARD_PLAN = (
    (TOKENS, 0), (PAIR,), (BEGIN, 0), (BEGIN, 1), (RELAY, 0, 0), (BEGIN, 2), (TOKENS, 1), (RELAY, 1, 0), (BEGIN, 3), (RELAY, 0, 1),
    (RELAY, 2, 0), (BEGIN, 4), (RELAY, 1, 1), (RELAY, 0, 2), (RELAY, 2, 1), (RELAY, 3, 0), (BEGIN, 5), (TOKENS, 2), (RELAY, 4, 0),
    (BEGIN, 6), (RELAY, 1, 2), (RELAY, 3, 1), (RELAY, 0, 3), (RELAY, 5, 0), (BEGIN, 7), (RELAY, 0, 4), (RELAY, 2, 2), (RELAY, 4, 1),
    (RELAY, 3, 2), (RELAY, 1, 3), (RELAY, 5, 1), (RELAY, 6, 0), (BEGIN, 8), (TOKENS, 3), (BLOCK, 0), (BLOCK, 1), (RELAY, 1, 4),
    (RELAY, 2, 3), (OTHER, 0), (BLOCK, 2), (RELAY, 7, 0), (BEGIN, 9), (OTHER, 1), (RELAY, 2, 4), (RELAY, 6, 1), (OTHER, 2), (RELAY, 4, 2),
    (RELAY, 8, 0), (BEGIN, 10), (RELAY, 3, 3), (RELAY, 3, 4), (RELAY, 5, 2), (RELAY, 7, 1), (RELAY, 8, 1), (RELAY, 9, 0), (RELAY, 6, 2),
    (BEGIN, 11), (COTANGENT, 0), (COTANGENT, 1), (COTANGENT, 2), (COTANGENT, 3), (RELAY, 10, 0), (BLOCK, 3), (QUERY,), (RELAY, 4, 3),
    (RELAY, 5, 3), (RELAY, 7, 2), (OTHER, 3), (KEY,), (RELAY, 4, 4), (RELAY, 5, 4), (RELAY, 9, 1), (VALUE,), (RELAY, 8, 2), (RELAY, 11, 0),
    (HEAD, 0), (HEAD, 1), (RELAY, 6, 3), (HEAD, 2), (HEAD, 3), (RELAY, 6, 4), (RELAY, 7, 3), (HEAD, 4), (HEAD, 5), (RELAY, 7, 4),
    (HEAD, 6), (HEAD, 7), (HEAD, 8), (HEAD, 9), (RELAY, 9, 2), (RELAY, 10, 1), (HEAD, 10), (RELAY, 11, 1), (HEAD, 11), (RELAY, 8, 3),
    (BRANCH,), (RELAY, 8, 4), (RELAY, 9, 3), (UP, 0), (RELAY, 9, 4), (UP, 1), (RELAY, 10, 2), (RELAY, 11, 2), (UP, 2), (UP, 3), (DOWN, 0),
    (RELAY, 10, 3), (RELAY, 11, 3), (RELAY, 10, 4), (RELAY, 11, 4), (DOWN, 1),
)
BACKWARD_CHUNKS = (
    ("d", 3, "bxayc"), ("d", 0, "axbyc"), ("u", 3, "axybc"), ("d", 1, "abyxc"), ("d", 2, "aybxc"), ("u", 1, "bxayc"), ("u", 2, "baxyc"),
    ("t", 3, "aybxc"), ("u", 0, "baxyc"), ("t", 0, "abxyc"), ("t", 1, "baxyc"), ("t", 2, "axbyc"),
)
BACKWARD_PLAN = (
    (GRAD_D, 3), (LAUNCH, 0), (GRAD_D, 0), (LAUNCH, 1), (HOME, 0), (HOME, 1), (HOME, 2), (HEAD_BACK, 0), (ABSORB, 0, 0), (GRAD_U, 3),
    (LAUNCH, 2), (ABSORB, 1, 0), (GRAD_D, 1), (LAUNCH, 3), (HOME, 3), (HEAD_BACK, 1), (ABSORB, 2, 0), (GRAD_D, 2), (LAUNCH, 4),
    (ABSORB, 0, 1), (ABSORB, 3, 0), (GRAD_U, 1), (LAUNCH, 5), (HEAD_BACK, 2), (ABSORB, 4, 0), (GRAD_U, 2), (LAUNCH, 6), (ABSORB, 1, 1),
    (ABSORB, 5, 0), (GRAD_T, 3), (LAUNCH, 7), (HEAD_BACK, 3), (ABSORB, 6, 0), (GRAD_U, 0), (LAUNCH, 8), (ABSORB, 3, 1), (ABSORB, 7, 0),
    (ABSORB, 2, 1), (ABSORB, 5, 1), (HEAD_BACK, 4), (ABSORB, 8, 0), (HEAD_BACK, 5), (HEAD_BACK, 6), (ABSORB, 4, 1), (ABSORB, 6, 1),
    (HEAD_BACK, 7), (HEAD_BACK, 8), (ABSORB, 0, 2), (ABSORB, 1, 2), (HEAD_BACK, 9), (ABSORB, 3, 2), (ABSORB, 7, 1), (HEAD_BACK, 10),
    (HEAD_BACK, 11), (EXCHANGE,), (ABSORB, 2, 2), (ABSORB, 4, 2), (ABSORB, 3, 3), (ABSORB, 5, 2), (ABSORB, 6, 2), (ABSORB, 8, 1),
    (ABSORB, 0, 3), (ABSORB, 7, 2), (ABSORB, 1, 3), (MERGE,), (GRAD_T, 0), (LAUNCH, 9), (ABSORB, 2, 3), (ABSORB, 3, 4), (GRAD_T, 1),
    (LAUNCH, 10), (ABSORB, 0, 4), (ABSORB, 4, 3), (ABSORB, 5, 3), (INPUT_GRAD,), (ABSORB, 6, 3), (ABSORB, 1, 4), (ABSORB, 7, 3),
    (ABSORB, 8, 2), (ABSORB, 9, 0), (ABSORB, 10, 0), (ABSORB, 2, 4), (GRAD_T, 2), (LAUNCH, 11), (ABSORB, 5, 4), (ABSORB, 4, 4),
    (ABSORB, 11, 0), (ABSORB, 9, 1), (ABSORB, 10, 1), (ABSORB, 6, 4), (ABSORB, 11, 1), (ABSORB, 9, 2), (ABSORB, 7, 4), (ABSORB, 10, 2),
    (ABSORB, 8, 3), (VECTORS,), (ABSORB, 11, 2), (ABSORB, 9, 3), (ABSORB, 8, 4), (ABSORB, 11, 3), (ABSORB, 10, 3), (ABSORB, 9, 4),
    (ABSORB, 10, 4), (ABSORB, 11, 4), (VECTORS_LAST,),
)
FORWARD = (FORWARD_PLAN, FORWARD_CHUNKS)
BACKWARD = (BACKWARD_PLAN, BACKWARD_CHUNKS)


S = pltpu.SemaphoreType.DMA
FC = 768


def total(v):
    return jnp.sum(v, axis=0, keepdims=True)


class Copies:
    def __init__(self):
        self.sent = []

    def start(self, describe, cond=None):
        def act(method):
            def run():
                src, dst, send, recv, to = describe()
                cp = pltpu.make_async_remote_copy(src_ref=src, dst_ref=dst, send_sem=send, recv_sem=recv, device_id=to, device_id_type=MESH)
                getattr(cp, method)()

            if cond is None:
                run()
            else:
                pl.when(cond())(run)

        act("start")
        self.sent.append(act)

    def start_or_keep(self, mine, describe, local):
        self.start(describe, lambda: jnp.logical_not(mine()))
        src, dst, *_ = describe()
        pl.when(mine())(pltpu.make_async_copy(src, dst, local).start)

    def arrive_or_keep(self, mine, dst, recv, local):
        pl.when(jnp.logical_not(mine))(lambda: arrive(dst, recv))
        pl.when(mine)(pltpu.make_async_copy(dst, dst, local).wait)

    def finish(self):
        for act in self.sent:
            act("wait_send")


def run_plan(plan, work, loops):
    def run(steps):
        for step, *args in steps:
            work[step](*args)

    kinds = [step[0] for step in plan]
    done = 0
    for kind, group in loops:
        first = kinds.index(kind)
        spots = [n for n, other in enumerate(kinds) if other == kind]
        run(plan[done:first])
        between = [plan[n + 1 : m] for n, m in zip(spots, spots[1:])] + [()]

        def body(turn, carry, kind=kind, group=group, between=between):
            for part in range(group):
                work[kind](turn, part)
                for n in range(part, len(between), group):
                    if between[n]:
                        pl.when(turn == n // group)(partial(run, between[n]))
            return carry

        lax.fori_loop(0, len(spots) // group, body, 0)
        done = spots[-1] + 1
    run(plan[done:])


def arrive(dst, recv):
    y, c, z, x = place()
    pltpu.make_async_remote_copy(src_ref=dst, dst_ref=dst, send_sem=recv, recv_sem=recv, device_id=device(y, c, z, x), device_id_type=MESH).wait_recv()


def forward_kernel(
    plan, chunks,
    xs, cot, seg, qw, kw, vw, ow, wup, wdt, small, upb,
    OUT, GF, GC, GST, LOWT, CTX, HID, GI, XO, Q, KT, V, E, CT, RS, WQ, VS,
    wt, wu, wd, pair_src, pair_dst, stage, xbuf, cbuf, sbuf, vec, vbuf, vb, ub,
    qb, kb, ktb, vb_, vtb, mask, ebuf, ctb, rsb, vsb, hid, gib, ctxb, n1, first, acc, rowbuf, outb, gsb, lowb, gcb, gsn,
    ps, pr, ws, wr, ls, xsnd, xrcv, fsnd, frcv, csnd, crcv, ssnd, srcv, vsnd, vrcv, lsem, osem, esem,
):
    y, c, z, x = place()
    j = 2 * z + x
    at = coords()
    partner = device(y, 1 - c, z, x)
    refs = (wt, wu, wd)
    copies = Copies()
    outs = []

    def put(src, dst):
        cp = pltpu.make_async_copy(src, dst, osem.at[len(outs)])
        cp.start()
        outs.append(cp)

    for i, w in enumerate((qw, kw, vw, ow)):
        pair_src[i] = w[...].astype(F32).T.astype(BF)
    vec[...] = jnp.zeros_like(vec)
    vec[0:8, 0:96] = small[...].astype(F32)
    vec[8:11, :] = upb[...].astype(F32)
    greet_all()()
    copies.start(lambda: (pair_src.at[:, pl.ds(48 * (1 - c), 48)], pair_dst, ps, pr, partner))

    def home(b):
        return (b // 2 == z) & (b % 2 == x) & (c == x)

    def send_tokens(src, dst, i, send, recv, local):
        def mine():
            return (z == (z + i) % 4) & (x == c) & (z // 2 == c)

        copies.start_or_keep(mine, lambda: (src.at[(z + i) % 4], dst.at[j % dst.shape[0]], send, recv.at[j % 4], device(y, z // 2, (z + i) % 4, c)), local)

    for i in range(4):
        for k in range(2):
            m = (z + i) % 4
            mine = (z == m) & (x == c) & (k == c)
            copies.start_or_keep(lambda v=mine: v, lambda m=m, i=i, k=k: (seg.at[m], sbuf.at[j], ssnd.at[2 * i + k], srcv.at[j], device(y, k, m, c)), lsem.at[1])
    pltpu.make_async_copy(vec, vbuf.at[j], lsem.at[2]).start()
    for d in range(1, 8):
        o = (j + d) % 8
        copies.start(lambda o=o, d=d: (vec, vbuf.at[j], vsnd.at[d], vrcv.at[d], device(y, c, o // 2, o % 2)))

    def pair_up():
        arrive(pair_dst, pr)
        own = pair_src[:, pl.ds(pl.multiple_of(48 * c, 16), 48), :]
        got = pair_dst[...]
        stage[...] = jnp.concatenate([jnp.where(c == 0, own, got), jnp.where(c == 0, got, own)], axis=-1)

    def source(ch):
        kind, i, _ = ch
        if kind == "t":
            return stage.at[i]
        if kind == "u":
            return wup.at[i]
        return wdt.at[i // 2, :, pl.ds(384 * (i % 2), 384)]

    def begin(u):
        ch = chunks[u]
        here = region(refs, ch, at)[0]
        pltpu.make_async_copy(source(ch), here, ls.at[u]).start()
        copies.start(lambda: (source(ch), region(refs, ch, at)[0], ws.at[u, 0, 0], wr.at[u, 0, 0], to_device(flip(at, ch[2][0]))))

    def relay(u, s):
        ch = chunks[u]
        order = ch[2]
        if s == 0:
            pltpu.make_async_copy(source(ch), region(refs, ch, at)[0], ls.at[u]).wait()

        def parts(at, s):
            if s < 3:
                return [region(refs, ch, whole(at, order[:s]))]
            return [region(refs, ch, whole(v, order[: s - 1])) for v in (at, flip(at, order[s - 1]))]

        def forward(s, h):
            def describe(k):
                part = parts(at, s)[h][k]
                return part, part, ws.at[u, s, 4 * h + k], wr.at[u, s, 4 * h + k], to_device(flip(at, order[s]))

            for k in range(len(parts(at, s)[h])):
                copies.start(partial(describe, k))

        for h, half in enumerate(parts(flip(at, order[s]), s)):
            for k, part in enumerate(half):
                arrive(part, wr.at[u, s, 4 * h + k])
        if s == 0:
            forward(1, 0)
        elif s == 1:
            forward(2, 0)
            forward(3, 0)
        elif s == 2:
            forward(3, 1)
            forward(4, 0)
        elif s == 3:
            forward(4, 1)

    def token_block(i):
        b = 4 * c + i
        copies.arrive_or_keep(home(b), xbuf.at[b], xrcv.at[i], lsem.at[0])
        copies.start(lambda: (xbuf.at[4 * c + i], xbuf.at[4 * c + i], fsnd.at[i], frcv.at[i], partner))

    def weight(i):
        return wt[i].reshape(768, 768)

    ready = []

    def vectors():
        if ready:
            return
        ready.append(True)
        pltpu.make_async_copy(vec, vbuf.at[j], lsem.at[2]).wait()
        for d in range(1, 8):
            arrive(vbuf.at[(j - d) % 8], vrcv.at[d])
        for b in range(8):
            copies.arrive_or_keep(home(b), sbuf.at[b], srcv.at[b], lsem.at[1])
        pieces = [vbuf[b] for b in range(8)]
        vb[...] = jnp.concatenate([p[:8, :96] for p in pieces], axis=-1)
        ub[...] = jnp.concatenate([p[8 + k : 9 + k, :] for p in pieces for k in range(3)], axis=-1)
        row = jnp.concatenate([sbuf[b] for b in range(8)], axis=-1).astype(F32)
        mine = jnp.concatenate([sbuf[4 * c + b] for b in range(4)], axis=-1).astype(F32)
        col = jnp.broadcast_to(row, (8, 1024)).T[:, :1]
        mask[...] = jnp.where(col == mine, 0.0, -1e30)

    def own_rows():
        return xbuf[pl.ds(4 * c, 4)].reshape(512, 768)

    def queries():
        vectors()
        put(xbuf.at[pl.ds(4 * c, 4)], XO)
        q = dot(own_rows(), weight(0), NT) + vb[0:1]
        qb[...] = (q.astype(BF).astype(F32) * 0.125).astype(BF)
        put(qb, Q)

    def keys():
        k = dot(xbuf[...].reshape(1024, 768), weight(1), NT)
        kb[...] = k.astype(BF)
        ktb[...] = k.T.astype(BF)
        put(ktb, KT)

    def values():
        vectors()
        v = dot(xbuf[...].reshape(1024, 768), weight(2), NT) + vb[1:2]
        vb_[...] = v.astype(BF)
        vtb[...] = v.T.astype(BF)
        put(vb_, V)

    def head(p, i):
        h = 2 * p + i
        cols = lanes(128 * p, 128)
        half = lax.broadcasted_iota(jnp.int32, (512, 128), 1) // 64
        qp = qb[:, cols]
        s = dot(kb[:, cols], jnp.where(half == i, qp, jnp.zeros_like(qp)), NT) + mask[...]
        e = jnp.exp(s - jnp.max(s, axis=0, keepdims=True))
        r = 1.0 / jnp.sum(e, axis=0, keepdims=True)
        pl.when(p > 0)(pltpu.make_async_copy(ebuf.at[i], E.at[h], esem.at[i]).wait)
        ebuf[i] = e.astype(BF)
        pltpu.make_async_copy(ebuf.at[i], E.at[h], esem.at[i]).start()
        rsb[pl.ds(h, 1), :] = r
        rows = pl.ds(pl.multiple_of(64 * h, 64), 64)
        ctb[rows, :] = (dot(vtb[rows, :], ebuf[i]) * r).astype(BF)

    def branch():
        put(wt.at[pl.ds(0, 3)], WQ)
        put(ctb, CT)
        put(rsb, RS)
        ctxb[...] = ctb[...].astype(F32).T.astype(BF)
        put(ctxb, CTX)
        normed, inv = norm(own_rows().astype(F32) + dot(ctxb[...], weight(3), NT) + vb[2:3])
        n1[...] = normed
        rowbuf[:, 0:1] = inv
        first[...] = normed * vb[3:4] + vb[4:5]
        lowb[...] = first[...].T.astype(BF)
        put(lowb, LOWT)

    def up(f, _):
        cols = lanes(FC * f, FC)
        inner = dot(first[...].astype(BF), wu[:, :, :, :, cols].reshape(768, FC)) + ub[:, cols]
        cdf = 0.5 * (1.0 + lax.erf(inner * 0.7071067811865476))
        pdf = jnp.exp(-0.5 * inner * inner) * 0.3989422804014327
        hid[:, cols] = (inner * cdf).astype(BF)
        gib[:, cols] = (cdf + inner * pdf).astype(BF)

    downs = []

    def down(b):
        if not downs:
            put(hid, HID)
            acc[...] = first[...] + vb[5:6]

        part = None
        for q in range(4):
            cols = slice(768 * q + 384 * b, 768 * q + 384 * b + 384)
            d = dot(hid[:, cols], wd[:, :, :, :, :, cols].reshape(768, 384), NT)
            part = d if part is None else part + d
        acc[...] += part
        downs.append(b)

    def second_norm():
        normed, inv = norm(acc[...])
        gain = vb[6:7]
        outb[...] = (normed * gain + vb[7:8]).astype(BF)
        put(outb, OUT)
        for b in range(4):
            copies.arrive_or_keep(home(4 * c + b), cbuf.at[b], crcv.at[b], lsem.at[3])
        g = cbuf[...].reshape(512, 768).astype(F32)
        vsb[...] = jnp.zeros_like(vsb)
        vsb[6:7, :768] = total(g * normed)
        vsb[7:8, :768] = total(g)
        gss = norm_back(g * gain, normed, inv)
        gs = gss.astype(BF)
        vsb[5:6, :768] = total(gs.astype(F32))
        acc[...] = gss
        gsb[...] = gss.T.astype(BF)
        put(gsb, GST)
        return gs

    def back(gs):
        gsn[...] = gs

        def step(f, carry):
            cols = lanes(FC * f, FC)
            gi = (dot(gsn[...], wd[:, :, :, :, :, cols].reshape(768, FC)) * gib[:, cols].astype(F32)).astype(BF)
            gib[:, cols] = gi
            vsb[8:9, cols] = total(gi.astype(F32))
            acc[...] += dot(gi, wu[:, :, :, :, cols].reshape(768, FC), NT)
            return carry

        lax.fori_loop(0, 3072 // FC, step, 0)
        put(gib, GI)
        gf = acc[...]
        vsb[3:4, :768] = total(gf * n1[...])
        vsb[4:5, :768] = total(gf)
        gsf = norm_back(gf * vb[3:4], n1[...], rowbuf[:, 0:1])
        first[...] = gsf
        put(first, GF)
        gb = gsf.astype(BF)
        vsb[2:3, :768] = total(gb.astype(F32))
        VS[...] = vsb[...]
        gcb[...] = dot(gb, weight(3)).astype(BF)
        put(gcb, GC)

    def tokens(i):
        send_tokens(xs, xbuf, i, xsnd.at[i], xrcv, lsem.at[0])

    def cotangent(i):
        send_tokens(cot, cbuf, i, csnd.at[i], crcv, lsem.at[3])

    def other_block(i):
        arrive(xbuf.at[4 * (1 - c) + i], frcv.at[i])

    work = {
        BEGIN: begin, RELAY: relay, TOKENS: tokens, BLOCK: token_block, OTHER: other_block, COTANGENT: cotangent, PAIR: pair_up,
        QUERY: queries, KEY: keys, VALUE: values, HEAD: head, BRANCH: branch, UP: up, DOWN: down,
    }
    run_plan(plan, work, ((HEAD, 2), (UP, 1)))
    back(second_norm())
    for i in range(2):
        pltpu.make_async_copy(ebuf.at[i], E.at[10 + i], esem.at[i]).wait()
    for cp in outs:
        cp.wait()
    copies.finish()


def forward_call(plan, chunks, xs, cot, seg, qw, kw, vw, ow, wup, wdt, small, upb):
    n = len(chunks)
    V_ = pltpu.VMEM
    row = (512, 768)
    return pl.pallas_call(
        partial(forward_kernel, plan, chunks),
        out_shape=[
            sds(row), sds(row, F32), sds(row), sds((768, 512)), sds((768, 512)), sds(row), sds((512, 3072)), sds((512, 3072)),
            sds((4, 128, 768)), sds(row), sds((768, 1024)), sds((1024, 768)), sds((12, 1024, 512)), sds((768, 512)), sds((16, 512), F32),
            sds((3, 2, 2, 2, 2, 48, 768)), sds((16, 3072), F32),
        ],
        in_specs=[ANY, ANY] + [VM] * 9,
        out_specs=[ANY] * 16 + [VM],
        scratch_shapes=[
            V_((4, 2, 2, 2, 2, 48, 768), BF), V_((2, 2, 4, 48, 3072), BF), V_((2, 2, 2, 2, 48, 3072), BF),
            V_((4, 96, 192), BF), V_((4, 48, 192), BF), V_((4, 48, 384), BF), V_((8, 128, 768), BF), V_((4, 128, 768), BF),
            V_((8, 1, 128), jnp.int32), V_((16, 128), F32), V_((8, 16, 128), F32), V_((8, 768), F32), V_((1, 3072), F32),
            V_(row, BF), V_((1024, 768), BF), V_((768, 1024), BF), V_((1024, 768), BF), V_((768, 1024), BF), V_((1024, 512), F32),
            V_((2, 1024, 512), BF), V_((768, 512), BF), V_((16, 512), F32), V_((16, 3072), F32), V_((512, 3072), BF), V_((512, 3072), BF),
            V_(row, BF), V_(row, F32), V_(row, F32), V_(row, F32), V_((512, 128), F32), V_(row, BF), V_((768, 512), BF), V_((768, 512), BF), V_(row, BF), V_(row, BF),
            S, S, S((n, 5, 8)), S((n, 5, 8)), S((n,)), S((4,)), S((4,)), S((4,)), S((4,)), S((4,)), S((4,)), S((8,)), S((8,)), S((8,)), S((8,)),
            S((4,)), S((24,)), S((2,)),
        ],
        name="forward",
        compiler_params=pltpu.CompilerParams(collective_id=1, has_side_effects=True, vmem_limit_bytes=59 * 2**20),
    )(xs, cot, seg, qw, kw, vw, ow, wup, wdt, small, upb)


def landing(at, order, s):
    spot = dict(at)
    for d in order[s + 1 :]:
        spot[d] = 1 - at[d]
    return whole(spot, order[:s])


def backward_kernel(
    plan, chunks,
    OUT, GF, GC, GST, LOWT, CTX, HID, GI, XO, Q, KT, V, E, CT, RS, WQ, VS,
    LO, IG, D4, DU, DD, VO,
    gt, gu, gd, rt, ru, rd, hid, gib, gst, lowt, xb, qb, ktb, vb, ctb, gcb, gct, gfb, ebuf,
    dqt, dkb, dvb, dkr, dvr, igb, rcol, vpack, vrecv, vsum, vrecv2, pairs, pairr, fin,
    isem, esem, lsem, ks, kr, os_, or_, gs, gr, vs_, vr, ws, wr, ps, pr,
):
    y, c, z, x = place()
    j = 2 * z + x
    at = coords()
    partner = device(y, 1 - c, z, x)
    G, R = (gt, gu, gd), (rt, ru, rd)
    copies = Copies()
    loads = {}
    for src, dst, name in (
        (GST, gst, "gst"), (HID, hid, "hid"), (LOWT, lowt, "lowt"), (GI, gib, "gi"), (V, vb, "v"), (Q, qb, "q"), (GC, gcb, "gc"), (KT, ktb, "kt"),
        (CT, ctb, "ct"), (CTX, igb, "ctx"), (XO, xb, "x"), (GF, gfb, "gf"),
    ):
        cp = pltpu.make_async_copy(src, dst, isem.at[len(loads)])
        cp.start()
        loads[name] = cp
    for i in range(2):
        pltpu.make_async_copy(E.at[i], ebuf.at[i], esem.at[i]).start()

    def need(*names):
        for n in names:
            if n in loads:
                loads.pop(n).wait()

    all_here = greet_all()

    def send_home(src, out, w, k):
        def mine():
            b = 4 * c + k
            return (x == c) & (b // 2 == z) & (b % 2 == x)

        def describe():
            b = 4 * c + k
            return src.at[pl.ds(128 * k, 128)], out.at[z], os_.at[w, k], or_.at[w, z], device(y, x, b // 2, b % 2)

        copies.start_or_keep(mine, describe, lsem.at[w])

    def send_out(k):
        send_home(OUT, LO, 0, k)

    def send_grad(k):
        send_home(igb, IG, 1, k)

    def halves(order, s, at):
        if s == 3:
            return [flip(at, order[2]), at]
        return [at]

    def stage(ch, s, at, h):
        order = ch[2]
        spot = landing(at, order, s)
        own = whole(at, order[:s])
        if s == 3:
            own[order[2]] = spot[order[2]] = halves(order, s, at)[h][order[2]]
        return region(G, ch, own), region(R, ch, spot)

    def launch(u, s):
        ch = chunks[u]
        to = flip(at, ch[2][s])

        def describe(h, k):
            to = flip(at, ch[2][s])
            src, dst = stage(ch, s, to, h)
            return src[k], dst[k], gs.at[u, s, 4 * h + k], gr.at[u, s, 4 * h + k], to_device(to)

        for h in range(2 if s == 3 else 1):
            for k in range(len(stage(ch, s, to, h)[0])):
                copies.start(partial(describe, h, k))

    def take(u, s, h):
        for k, (own, got) in enumerate(zip(*stage(chunks[u], s, at, h))):
            arrive(got, gr.at[u, s, 4 * h + k])
            own[...] = own[...] + got[...]

    def absorb(u, s):
        kind, i, order = ch = chunks[u]
        if s > 0:
            if s == 2:
                take(u, 3, 1)
            take(u, s, 0)
            launch(u, s - 1)
            return
        (own,), (got,) = stage(ch, 0, at, 0)
        arrive(got, gr.at[u, 0, 0])
        done = own[...].astype(F32) + got[...].astype(F32)
        if kind == "u":
            DU[i] = done
        elif kind == "d":
            DD[i // 2, :, 384 * (i % 2) : 384 * (i % 2) + 384] = done
        else:
            lo, hi = done[:, :192], done[:, 192:]
            fin[i, pl.ds(pl.multiple_of(48 * c, 16), 48), :] = jnp.where(c == 0, lo, hi)
            pairs[i] = jnp.where(c == 0, hi, lo)
            copies.start(lambda: (pairs.at[i], pairr.at[i], ps.at[i], pr.at[i], partner))

    made = []

    def grad_u(i):
        made.append(i)
        need("lowt", "gi")
        rows = lowt[...].reshape(2, 2, 4, 48, 512)[:, :, i].reshape(192, 512)

        def columns(q, carry):
            cols = lanes(768 * q, 768)
            gu[:, :, i, :, cols] = dot(rows, gib[:, cols]).astype(BF).reshape(2, 2, 48, 768)
            return carry

        lax.fori_loop(0, 4, columns, 0)

    def grad_d(i):
        made.append(i)
        need("gst", "hid")
        rows = gst[...].reshape(2, 2, 2, 2, 48, 512)[:, :, :, i // 2].reshape(384, 512)

        def columns(q, carry):
            cols = lanes(768 * q + 384 * (i % 2), 384)
            gd[:, :, :, i // 2, :, cols] = dot(rows, hid[:, cols]).astype(BF).reshape(2, 2, 2, 48, 384)
            return carry

        lax.fori_loop(0, 4, columns, 0)

    shape = (2, 2, 2, 2, 48, 768)

    def grad_t(i):
        if i == 3:
            need("gf", "ctx")
            gt[3] = dot(gfb[...].T.astype(BF), igb[...]).astype(BF).reshape(shape)
        elif i == 0:
            need("x")
            gt[0] = dot(dqt[...], xb[...].reshape(512, 768)).astype(BF).reshape(shape)
        else:
            src = dkr if i == 1 else dvr
            gt[i] = dot(src[...].astype(F32).T.astype(BF), xb[...].reshape(512, 768)).astype(BF).reshape(shape)

    def ready():
        need("gc", "v", "q", "kt", "ct")
        gct[...] = gcb[...].astype(F32).T.astype(BF)
        rcol[...] = RS[...].T

    def head(p, i):
        h = 2 * p + i
        cols = lanes(128 * p, 128)
        rows = pl.ds(pl.multiple_of(64 * h, 64), 64)
        qp = qb[:, cols]
        half = lax.broadcasted_iota(jnp.int32, (512, 128), 1) // 64
        column = lax.broadcasted_iota(jnp.int32, (512, 16), 1)
        scale = jnp.sum(jnp.where(column == h, rcol[...], 0.0), axis=1, keepdims=True)
        gm = jnp.where(half == i, gcb[:, cols].astype(F32) * scale, 0.0).astype(BF)
        qm = jnp.where(half == i, qp, jnp.zeros_like(qp))
        delta = total(ctb[rows, :].astype(F32) * gct[rows, :].astype(F32)) * RS[pl.ds(h, 1), :]
        pltpu.make_async_copy(E.at[h], ebuf.at[i], esem.at[i]).wait()
        ds = (ebuf[i].astype(F32) * (dot(vb[:, cols], gm, NT) - delta)).astype(BF)
        dv = dot(ebuf[i], gm)
        dk = dot(ds, qm)
        dqt[rows, :] = (dot(ktb[rows, :], ds) * 0.125).astype(BF)
        pl.when(p < 5)(pltpu.make_async_copy(E.at[jnp.minimum(h + 2, 11)], ebuf.at[i], esem.at[i]).start)
        dkb[:, cols] = dk.astype(BF) if i == 0 else (dkb[:, cols].astype(F32) + dk).astype(BF)
        dvb[:, cols] = dv.astype(BF) if i == 0 else (dvb[:, cols].astype(F32) + dv).astype(BF)

    theirs = pl.ds(pl.multiple_of(512 * (1 - c), 128), 512)
    ours = pl.ds(pl.multiple_of(512 * c, 128), 512)

    def weight_copies():
        for i in range(3):
            cols = slice(768 * i, 768 * i + 768)
            yield pltpu.make_async_copy(WQ.at[i, pl.ds(0, 512)], hid.at[:, cols], isem.at[13 + 2 * i])
            yield pltpu.make_async_copy(WQ.at[i, pl.ds(512, 256)], gib.at[pl.ds(0, 256), cols], isem.at[14 + 2 * i])

    def exchange():
        assert len(made) == 8
        for cp in weight_copies():
            cp.start()
        copies.start(lambda: (dkb.at[theirs], dkr, ks.at[0], kr.at[0], partner))
        copies.start(lambda: (dvb.at[theirs], dvr, ks.at[1], kr.at[1], partner))

    def merge():
        arrive(dkr, kr.at[0])
        arrive(dvr, kr.at[1])
        dkr[...] = (dkb[ours].astype(F32) + dkr[...].astype(F32)).astype(BF)
        dvr[...] = (dvb[ours].astype(F32) + dvr[...].astype(F32)).astype(BF)

    def token_grads():
        need("gf")
        for cp in weight_copies():
            cp.wait()
        dq = dqt[...].astype(F32).T
        ig = gfb[...]
        for i, g in enumerate((dq.astype(BF), dkr[...], dvr[...])):
            cols = slice(768 * i, 768 * i + 768)
            ig = ig + dot(g[:, :512], hid[:, cols]) + dot(g[:, 512:], gib[:256, cols])
        low = jnp.concatenate([total(dq), total(dvr[...].astype(F32)), VS[2:8, :768]], axis=0)
        vpack[...] = jnp.zeros_like(vpack)
        for b in range(8):
            vpack[b, 0:8, 0:96] = low[:, 96 * b : 96 * b + 96]
            vpack[b, 8:9, :] = VS[8:9, 384 * b : 384 * b + 384]
        for d in range(1, 8):
            o = (j + d) % 8
            copies.start(lambda o=o, d=d: (vpack.at[o], vrecv.at[d], vs_.at[d], vr.at[d], device(y, c, o // 2, o % 2)))
        igb[...] = ig.astype(BF)
        for k in range(4):
            send_grad(k)

    def vectors_first():
        acc = vpack[j]
        for d in range(1, 8):
            arrive(vrecv.at[d], vr.at[d])
            acc = acc + vrecv[d]
        vsum[...] = acc
        me = 2 * y + c
        for d in range(1, 4):
            copies.start(lambda d=d: (vsum, vrecv2.at[d], ws.at[d], wr.at[d], ((me + d) % 4, j)))

    def vectors_last():
        acc = vsum[...]
        for d in range(1, 4):
            arrive(vrecv2.at[d], wr.at[d])
            acc = acc + vrecv2[d]
        VO[...] = acc

    work = {
        LAUNCH: lambda u: launch(u, 4), ABSORB: lambda u, s: absorb(u, 4 - s), HOME: send_out, GRAD_U: grad_u, GRAD_D: grad_d, GRAD_T: grad_t,
        HEAD_BACK: head, EXCHANGE: exchange, MERGE: merge, INPUT_GRAD: token_grads, VECTORS: vectors_first, VECTORS_LAST: vectors_last,
    }
    early = [step for step in plan if step[0] in (GRAD_U, GRAD_D)][:3]
    run_plan(early, work, ())
    all_here()
    plan = [step for step in plan if step not in early]
    loops_at = [step[0] for step in plan].index(HEAD_BACK)
    run_plan(plan[:loops_at], work, ())
    ready()
    run_plan(plan[loops_at:], work, ((HEAD_BACK, 2),))
    for i in range(4):
        arrive(pairr.at[i], pr.at[i])
        fin[i, pl.ds(pl.multiple_of(48 * (1 - c), 16), 48), :] = pairr[i]
        D4[i] = fin[i].T
    for w, out in ((0, LO), (1, IG)):
        for m in range(4):
            copies.arrive_or_keep((m == z) & (x == c) & (z // 2 == c), out.at[m], or_.at[w, m], lsem.at[w])
    copies.finish()


def backward_call(plan, chunks, OUT, GF, GC, GST, LOWT, CTX, HID, GI, XO, Q, KT, V, E, CT, RS, WQ, VS):
    n = len(chunks)
    V_ = pltpu.VMEM
    row = (512, 768)
    col = (768, 512)
    sets = [V_((4, 2, 2, 2, 2, 48, 768), BF), V_((2, 2, 4, 48, 3072), BF), V_((2, 2, 2, 2, 48, 3072), BF)]
    return pl.pallas_call(
        partial(backward_kernel, plan, chunks),
        out_shape=[sds((4, 128, 768)), sds((4, 128, 768))] + [sds((4, 192, 96), F32), sds((4, 48, 384), F32), sds((2, 48, 768), F32), sds((16, 384), F32)],
        in_specs=[ANY] * 14 + [VM, ANY, VM],
        out_specs=[ANY, ANY] + [VM] * 4,
        scratch_shapes=sets + sets + [
            V_((512, 3072), BF), V_((512, 3072), BF), V_(col, BF), V_(col, BF), V_((4, 128, 768), BF), V_(row, BF),
            V_((768, 1024), BF), V_((1024, 768), BF), V_(col, BF), V_(row, BF), V_(col, BF), V_(row, F32), V_((2, 1024, 512), BF),
            V_(col, BF), V_((1024, 768), BF), V_((1024, 768), BF), V_(row, BF), V_(row, BF), V_(row, BF), V_((512, 16), F32),
            V_((8, 16, 384), F32), V_((8, 16, 384), F32), V_((16, 384), F32), V_((4, 16, 384), F32), V_((4, 48, 192), F32), V_((4, 48, 192), F32), V_((4, 96, 192), F32),
            S((19,)), S((2,)), S((2,)), S((2,)), S((2,)), S((2, 4)), S((2, 4)), S((n, 5, 8)), S((n, 5, 8)), S((8,)), S((8,)), S((4,)), S((4,)), S((4,)), S((4,)),
        ],
        name="backward",
        compiler_params=pltpu.CompilerParams(collective_id=2, has_side_effects=True, vmem_limit_bytes=59 * 2**20),
    )(OUT, GF, GC, GST, LOWT, CTX, HID, GI, XO, Q, KT, V, E, CT, RS, WQ.reshape(3, 768, 768), VS)


def rows_on_chips(
    inputs, segment_ids, query_weight, query_bias, key_weight, value_weight, value_bias, output_weight, output_bias,
    first_gain, first_shift, up_weight, up_bias, down_weight, down_bias, second_gain, second_shift, cotangent,
):
    small = jnp.stack([query_bias, value_bias, output_bias, first_gain, first_shift, down_bias, second_gain, second_shift])
    kept = forward_call(
        *FORWARD, inputs.reshape(4, 128, 768), cotangent.reshape(4, 128, 768), segment_ids.reshape(4, 1, 128),
        query_weight, key_weight, value_weight, output_weight, up_weight.reshape(4, 48, 384), down_weight.T.reshape(2, 48, 768),
        small, up_bias.reshape(3, 128),
    )
    LO, IG, D4, DU, DD, VO = backward_call(*BACKWARD, *kept)
    v = VO[:8, :96]
    s = (4, 1, 128, 768)
    return (
        LO.reshape(s), IG.reshape(s), D4[0], v[0], D4[1], D4[2], v[1], D4[3], v[2], v[3], v[4], DU.reshape(192, 384), VO[8], DD.reshape(96, 768).T, v[5], v[6], v[7],
    )


EPSILON = 1e-12
NEGATIVE = -1e30


def product(left, right, form):
    return jnp.einsum(form, left, right, preferred_element_type=jnp.float32)


def normalize(hidden, gain, shift):
    centred = hidden - jnp.mean(hidden, axis=-1, keepdims=True)
    scale_inv = lax.rsqrt(jnp.mean(centred * centred, axis=-1, keepdims=True) + EPSILON)
    normed = centred * scale_inv
    return (normed * gain + shift, normed, scale_inv)


def normalize_back(grad_normed, normed, scale_inv):
    centred_grad = grad_normed - jnp.mean(grad_normed, axis=-1, keepdims=True)
    return scale_inv * (
        centred_grad - normed * jnp.mean(grad_normed * normed, axis=-1, keepdims=True)
    )


def same_passage(query_pair, key_pair):
    return jnp.all(query_pair[:, :, None, :] == key_pair[:, None, :, :], axis=-1)[:, None]


def micro_step(shared, tokens, passage_ids, cotan):
    (
        weight_query,
        weight_key,
        weight_value,
        weight_out,
        weight_up,
        weight_down,
        bias_query,
        bias_value,
        bias_out,
        gain_first,
        shift_first,
        bias_up,
        bias_down,
        gain_second,
        shift_second,
    ) = shared
    bias_query = bias_query.astype(jnp.float32)
    bias_value = bias_value.astype(jnp.float32)
    bias_out = bias_out.astype(jnp.float32)
    gain_first = gain_first.astype(jnp.float32)
    shift_first = shift_first.astype(jnp.float32)
    bias_up = bias_up.astype(jnp.float32)
    bias_down = bias_down.astype(jnp.float32)
    gain_second = gain_second.astype(jnp.float32)
    shift_second = shift_second.astype(jnp.float32)
    row_count, seq_count, width = tokens.shape
    token_count = row_count * seq_count
    scale = HD ** (-0.5)
    flat = tokens.reshape(token_count, width)
    queries = (product(flat, weight_query, "md,de->me") + bias_query).astype(jnp.bfloat16)
    keys = product(flat, weight_key, "md,de->me").astype(jnp.bfloat16)
    values = (product(flat, weight_value, "md,de->me") + bias_value).astype(jnp.bfloat16)
    query_four = queries.reshape(row_count, seq_count, HEADS, HD)
    pair_local = jnp.stack((passage_ids // 256, passage_ids % 256), axis=-1).astype(jnp.bfloat16)
    key_rows = keys.reshape(row_count, seq_count, width)
    value_rows = values.reshape(row_count, seq_count, width)
    key_local = key_rows.reshape(row_count, seq_count, HEADS, HD)
    value_local = value_rows.reshape(row_count, seq_count, HEADS, HD)
    running_max = jnp.full((row_count, HEADS, seq_count), NEGATIVE, jnp.float32)
    running_acc = jnp.zeros((row_count, seq_count, HEADS, HD), jnp.float32)
    key_piece = lax.all_gather(key_rows, "blk", axis=1, tiled=True)
    value_piece = lax.all_gather(value_rows, "blk", axis=1, tiled=True)
    pair_piece = lax.all_gather(pair_local, "blk", axis=1, tiled=True)
    count = key_piece.shape[1]
    key_four = key_piece.reshape(row_count, count, HEADS, HD)
    value_four = value_piece.reshape(row_count, count, HEADS, HD)
    allowed = same_passage(pair_local, pair_piece)
    scores = jnp.where(allowed, product(query_four, key_four, "rqhd,rkhd->rhqk") * scale, NEGATIVE)
    fresh_max = jnp.maximum(running_max, jnp.max(scores, axis=-1))
    weights = jnp.where(allowed, jnp.exp(scores - fresh_max[..., None]), 0.0)
    decay = jnp.exp(running_max - fresh_max)
    running_sum = jnp.sum(weights, axis=-1)
    mixed = product(weights.astype(jnp.bfloat16), value_four, "rhqk,rkhd->rqhd")
    running_acc = running_acc * jnp.swapaxes(decay, 1, 2)[..., None] + mixed
    running_max, running_sum, running_acc = (fresh_max, running_sum, running_acc)
    log_total = running_max + jnp.log(running_sum)
    attended = running_acc / jnp.swapaxes(running_sum, 1, 2)[..., None]
    context = attended.reshape(token_count, width).astype(jnp.bfloat16)
    branch = product(context, weight_out, "md,de->me") + bias_out
    first, normed_first, inv_first = normalize(
        flat.astype(jnp.float32) + branch, gain_first, shift_first
    )
    first_low = first.astype(jnp.bfloat16)
    inner = product(first_low, weight_up, "md,df->mf") + bias_up
    activation, gelu_pull = jax.vjp(partial(jax.nn.gelu, approximate=False), inner)
    hidden = activation.astype(jnp.bfloat16)
    second = product(hidden, weight_down, "mf,fd->md") + bias_down
    output, normed_second, inv_second = normalize(first + second, gain_second, shift_second)
    upstream = cotan.reshape(token_count, width).astype(jnp.float32)
    grad_gain_second = jnp.sum(upstream * normed_second, axis=0, keepdims=True)
    grad_shift_second = jnp.sum(upstream, axis=0, keepdims=True)
    grad_sum_second = normalize_back(upstream * gain_second, normed_second, inv_second)
    grad_second = grad_sum_second.astype(jnp.bfloat16)
    grad_weight_down = product(hidden, grad_second, "mf,md->fd")
    grad_bias_down = jnp.sum(grad_second.astype(jnp.float32), axis=0, keepdims=True)
    grad_inner = gelu_pull(product(grad_second, weight_down, "md,fd->mf"))[0].astype(jnp.bfloat16)
    grad_weight_up = product(first_low, grad_inner, "md,mf->df")
    grad_bias_up = jnp.sum(grad_inner.astype(jnp.float32), axis=0, keepdims=True)
    grad_first = grad_sum_second + product(grad_inner, weight_up, "mf,df->md")
    grad_gain_first = jnp.sum(grad_first * normed_first, axis=0, keepdims=True)
    grad_shift_first = jnp.sum(grad_first, axis=0, keepdims=True)
    grad_sum_first = normalize_back(grad_first * gain_first, normed_first, inv_first)
    grad_branch = grad_sum_first.astype(jnp.bfloat16)
    grad_weight_out = product(context, grad_branch, "md,me->de")
    grad_bias_out = jnp.sum(grad_branch.astype(jnp.float32), axis=0, keepdims=True)
    grad_context = product(grad_branch, weight_out, "me,de->md").astype(jnp.bfloat16)
    grad_context_four = grad_context.reshape(row_count, seq_count, HEADS, HD)
    delta = jnp.swapaxes(jnp.sum(grad_context_four.astype(jnp.float32) * attended, axis=-1), 1, 2)
    key_piece = lax.all_gather(key_rows, "blk", axis=1, tiled=True)
    value_piece = lax.all_gather(value_rows, "blk", axis=1, tiled=True)
    pair_piece = lax.all_gather(pair_local, "blk", axis=1, tiled=True)
    count = key_piece.shape[1]
    key_four = key_piece.reshape(row_count, count, HEADS, HD)
    value_four = value_piece.reshape(row_count, count, HEADS, HD)
    allowed = same_passage(pair_local, pair_piece)
    scores = jnp.where(allowed, product(query_four, key_four, "rqhd,rkhd->rhqk") * scale, NEGATIVE)
    probs = jnp.where(allowed, jnp.exp(scores - log_total[..., None]), 0.0)
    grad_probs = product(grad_context_four, value_four, "rqhd,rkhd->rhqk")
    grad_scores = (probs * (grad_probs - delta[..., None])).astype(jnp.bfloat16)
    grad_query_acc = product(grad_scores, key_four, "rhqk,rkhd->rqhd") * scale
    grad_queries = grad_query_acc.reshape(token_count, width).astype(jnp.bfloat16)
    pair_wide = pair_local.astype(jnp.float32)
    sent = (
        queries.reshape(row_count, seq_count, width).astype(jnp.float32),
        grad_context.reshape(row_count, seq_count, width).astype(jnp.float32),
        jnp.swapaxes(log_total, 1, 2),
        jnp.swapaxes(delta, 1, 2),
        pair_wide,
    )
    query_piece = lax.all_gather(sent[0], "blk", axis=1, tiled=True)
    context_piece = lax.all_gather(sent[1], "blk", axis=1, tiled=True)
    total_piece = lax.all_gather(sent[2], "blk", axis=1, tiled=True)
    delta_piece = lax.all_gather(sent[3], "blk", axis=1, tiled=True)
    pair_piece = lax.all_gather(sent[4], "blk", axis=1, tiled=True)
    count = query_piece.shape[1]
    query_part = query_piece.astype(jnp.bfloat16).reshape(row_count, count, HEADS, HD)
    context_part = context_piece.astype(jnp.bfloat16).reshape(row_count, count, HEADS, HD)
    total_part = jnp.swapaxes(total_piece, 1, 2)
    delta_part = jnp.swapaxes(delta_piece, 1, 2)
    allowed = same_passage(pair_piece, pair_wide)
    scores = jnp.where(allowed, product(query_part, key_local, "rqhd,rkhd->rhqk") * scale, NEGATIVE)
    probs = jnp.where(allowed, jnp.exp(scores - total_part[..., None]), 0.0)
    grad_value_acc = product(probs.astype(jnp.bfloat16), context_part, "rhqk,rqhd->rkhd")
    grad_probs = product(context_part, value_local, "rqhd,rkhd->rhqk")
    grad_scores = (probs * (grad_probs - delta_part[..., None])).astype(jnp.bfloat16)
    grad_key_acc = product(grad_scores, query_part, "rhqk,rqhd->rkhd") * scale
    grad_key_acc, grad_value_acc = (grad_key_acc, grad_value_acc)
    grad_keys = grad_key_acc.reshape(token_count, width).astype(jnp.bfloat16)
    grad_values = grad_value_acc.reshape(token_count, width).astype(jnp.bfloat16)
    grad_weight_query = product(flat, grad_queries, "md,me->de")
    grad_bias_query = jnp.sum(grad_queries.astype(jnp.float32), axis=0, keepdims=True)
    grad_weight_key = product(flat, grad_keys, "md,me->de")
    grad_weight_value = product(flat, grad_values, "md,me->de")
    grad_bias_value = jnp.sum(grad_values.astype(jnp.float32), axis=0, keepdims=True)
    grad_tokens = (
        grad_sum_first
        + product(grad_queries, weight_query, "me,de->md")
        + product(grad_keys, weight_key, "me,de->md")
        + product(grad_values, weight_value, "me,de->md")
    )
    contributions = (
        grad_weight_query,
        grad_weight_key,
        grad_weight_value,
        grad_weight_out,
        grad_weight_up,
        grad_weight_down,
        grad_bias_query,
        grad_bias_value,
        grad_bias_out,
        grad_gain_first,
        grad_shift_first,
        grad_bias_up,
        grad_bias_down,
        grad_gain_second,
        grad_shift_second,
    )
    return (
        output.astype(jnp.bfloat16).reshape(row_count, seq_count, width),
        grad_tokens.astype(jnp.bfloat16).reshape(row_count, seq_count, width),
        contributions,
    )


def general(
    inputs,
    segment_ids,
    query_weight,
    query_bias,
    key_weight,
    value_weight,
    value_bias,
    output_weight,
    output_bias,
    first_gain,
    first_shift,
    up_weight,
    up_bias,
    down_weight,
    down_bias,
    second_gain,
    second_shift,
    cotangent,
):
    outputs = []
    input_grads = []
    totals = None
    widened = (
        lax.all_gather(query_weight, "blk", axis=1, tiled=True),
        lax.all_gather(key_weight, "blk", axis=1, tiled=True),
        lax.all_gather(value_weight, "blk", axis=1, tiled=True),
        lax.all_gather(output_weight, "blk", axis=1, tiled=True),
        lax.all_gather(up_weight, "blk", axis=1, tiled=True),
        lax.all_gather(down_weight, "blk", axis=1, tiled=True),
        lax.all_gather(query_bias.reshape(1, -1), "blk", axis=1, tiled=True),
        lax.all_gather(value_bias.reshape(1, -1), "blk", axis=1, tiled=True),
        lax.all_gather(output_bias.reshape(1, -1), "blk", axis=1, tiled=True),
        lax.all_gather(first_gain.reshape(1, -1), "blk", axis=1, tiled=True),
        lax.all_gather(first_shift.reshape(1, -1), "blk", axis=1, tiled=True),
        lax.all_gather(up_bias.reshape(1, -1), "blk", axis=1, tiled=True),
        lax.all_gather(down_bias.reshape(1, -1), "blk", axis=1, tiled=True),
        lax.all_gather(second_gain.reshape(1, -1), "blk", axis=1, tiled=True),
        lax.all_gather(second_shift.reshape(1, -1), "blk", axis=1, tiled=True),
    )
    complete = (
        lax.all_gather(widened[0], "dp", axis=0, tiled=True),
        lax.all_gather(widened[1], "dp", axis=0, tiled=True),
        lax.all_gather(widened[2], "dp", axis=0, tiled=True),
        lax.all_gather(widened[3], "dp", axis=0, tiled=True),
        lax.all_gather(widened[4], "dp", axis=0, tiled=True),
        lax.all_gather(widened[5], "dp", axis=0, tiled=True),
    )
    shared = tuple(complete) + tuple(widened[6:])
    for batch_index in range(inputs.shape[0]):
        layer_out, layer_grad, contributions = micro_step(
            shared, inputs[batch_index], segment_ids[batch_index], cotangent[batch_index]
        )
        outputs.append(layer_out)
        input_grads.append(layer_grad)
        if totals is None:
            totals = contributions
        else:
            totals = tuple((earlier + latest for earlier, latest in zip(totals, contributions)))
    narrowed = (
        lax.psum_scatter(totals[0], "blk", scatter_dimension=1, tiled=True),
        lax.psum_scatter(totals[1], "blk", scatter_dimension=1, tiled=True),
        lax.psum_scatter(totals[2], "blk", scatter_dimension=1, tiled=True),
        lax.psum_scatter(totals[3], "blk", scatter_dimension=1, tiled=True),
        lax.psum_scatter(totals[4], "blk", scatter_dimension=1, tiled=True),
        lax.psum_scatter(totals[5], "blk", scatter_dimension=1, tiled=True),
        lax.psum_scatter(totals[6], "blk", scatter_dimension=1, tiled=True),
        lax.psum_scatter(totals[7], "blk", scatter_dimension=1, tiled=True),
        lax.psum_scatter(totals[8], "blk", scatter_dimension=1, tiled=True),
        lax.psum_scatter(totals[9], "blk", scatter_dimension=1, tiled=True),
        lax.psum_scatter(totals[10], "blk", scatter_dimension=1, tiled=True),
        lax.psum_scatter(totals[11], "blk", scatter_dimension=1, tiled=True),
        lax.psum_scatter(totals[12], "blk", scatter_dimension=1, tiled=True),
        lax.psum_scatter(totals[13], "blk", scatter_dimension=1, tiled=True),
        lax.psum_scatter(totals[14], "blk", scatter_dimension=1, tiled=True),
    )
    matrix_sums = (
        lax.psum_scatter(narrowed[0], "dp", scatter_dimension=0, tiled=True),
        lax.psum_scatter(narrowed[1], "dp", scatter_dimension=0, tiled=True),
        lax.psum_scatter(narrowed[2], "dp", scatter_dimension=0, tiled=True),
        lax.psum_scatter(narrowed[3], "dp", scatter_dimension=0, tiled=True),
        lax.psum_scatter(narrowed[4], "dp", scatter_dimension=0, tiled=True),
        lax.psum_scatter(narrowed[5], "dp", scatter_dimension=0, tiled=True),
    )
    vector_sums = lax.psum(
        (
            narrowed[6],
            narrowed[7],
            narrowed[8],
            narrowed[9],
            narrowed[10],
            narrowed[11],
            narrowed[12],
            narrowed[13],
            narrowed[14],
        ),
        "dp",
    )
    return (
        jnp.stack(outputs),
        jnp.stack(input_grads),
        matrix_sums[0],
        vector_sums[0].reshape(-1),
        matrix_sums[1],
        matrix_sums[2],
        vector_sums[1].reshape(-1),
        matrix_sums[3],
        vector_sums[2].reshape(-1),
        vector_sums[3].reshape(-1),
        vector_sums[4].reshape(-1),
        matrix_sums[4],
        vector_sums[5].reshape(-1),
        matrix_sums[5],
        vector_sums[6].reshape(-1),
        vector_sums[7].reshape(-1),
        vector_sums[8].reshape(-1),
    )


def solution(mesh):
    in_specs = (
        P(None, "dp", "blk", None),
        P(None, "dp", "blk"),
        P("dp", "blk"),
        P("blk"),
        P("dp", "blk"),
        P("dp", "blk"),
        P("blk"),
        P("dp", "blk"),
        P("blk"),
        P("blk"),
        P("blk"),
        P("dp", "blk"),
        P("blk"),
        P("dp", "blk"),
        P("blk"),
        P("blk"),
        P("blk"),
        P(None, "dp", "blk", None),
    )
    out_specs = (
        P(None, "dp", "blk", None),
        P(None, "dp", "blk", None),
        P("dp", "blk"),
        P("blk"),
        P("dp", "blk"),
        P("dp", "blk"),
        P("blk"),
        P("dp", "blk"),
        P("blk"),
        P("blk"),
        P("blk"),
        P("dp", "blk"),
        P("blk"),
        P("dp", "blk"),
        P("blk"),
        P("blk"),
        P("blk"),
    )
    small = mesh.shape["dp"] == 4 and mesh.shape["blk"] == 8

    def on_device(*arrays):
        if small and arrays[0].shape == (4, 1, 128, 768):
            return rows_on_chips(*arrays)
        return general(*arrays)

    return jax.shard_map(
        on_device, mesh=mesh, in_specs=in_specs, out_specs=out_specs, check_vma=False
    )
```

```python
from functools import partial

import jax
import jax.numpy as jnp
from jax import lax
from jax.experimental import pallas as pl
from jax.experimental.pallas import tpu as pltpu
from jax.sharding import PartitionSpec as P

MESH = pl.DeviceIdType.MESH
BF = jnp.bfloat16
F32 = jnp.float32


(BEGIN, RELAY, TOKENS, BLOCK, OTHER, COTANGENT, PAIR, QUERY, KEY, VALUE, HEAD, BRANCH, UP, DOWN) = range(14)
(LAUNCH, ABSORB, HOME, GRAD_U, GRAD_D, GRAD_T, HEAD_BACK, EXCHANGE, MERGE, INPUT_GRAD, VECTORS, VECTORS_LAST) = range(14, 26)


def place():
    dp = lax.axis_index("dp")
    blk = lax.axis_index("blk")
    return dp // 2, dp % 2, blk // 2, blk % 2


def device(y, c, z, x):
    return (y * 2 + c, z * 2 + x)


def greet_all():
    y, c, z, x = place()
    me = (y * 2 + c) * 8 + z * 2 + x
    barrier = pltpu.get_barrier_semaphore()

    def greet(i, carry):
        other = (me + i) % 32
        pl.semaphore_signal(barrier, inc=1, device_id=(other // 8, other % 8), device_id_type=MESH)
        return carry

    lax.fori_loop(1, 32, greet, 0)
    return lambda: pl.semaphore_wait(barrier, 31)


def coords():
    y, c, z, x = place()
    return {"a": z // 2, "b": z % 2, "x": x, "y": y, "c": c}


def to_device(at):
    return device(at["y"], at["c"], 2 * at["a"] + at["b"], at["x"])


def flip(at, dim):
    return {**at, dim: 1 - at[dim]}


def whole(at, dims):
    return {k: (None if k in dims else v) for k, v in at.items()}


def span(v):
    return slice(None) if v is None else v


def each(v):
    return (0, 1) if v is None else (v,)


def lanes(start, size):
    return pl.ds(start if isinstance(start, int) else pl.multiple_of(start, 128), size)


def region(refs, chunk, at):
    wt, wu, wd = refs
    kind, i, _ = chunk
    a, b, x, y, c = (at[k] for k in "abxyc")
    if kind == "t":
        cols = slice(None) if y is None else lanes(384 * y, 384)
        return [wt.at[i, span(a), span(b), span(x), span(c), :, cols]]
    if kind == "u":
        if a is None and b is None and x is None:
            return [wu.at[span(y), span(c), i]]
        return [wu.at[span(y), span(c), i, :, lanes(384 * (4 * p + 2 * q + r), 384)] for p in each(a) for q in each(b) for r in each(x)]
    return [wd.at[span(a), span(b), span(x), i // 2, :, lanes(768 * (2 * p + q) + 384 * (i % 2), 384)] for p in each(y) for q in each(c)]


HEADS, HD = 12, 64
NT = (((1,), (1,)), ((), ()))
NN = (((1,), (0,)), ((), ()))


def dot(l, r, dims=NN):
    return lax.dot_general(l, r, dims, preferred_element_type=F32)


VM = pl.BlockSpec(memory_space=pltpu.VMEM)
ANY = pl.BlockSpec(memory_space=pl.ANY)


def sds(shape, dt=BF):
    return jax.ShapeDtypeStruct(shape, dt)


def norm(h):
    centred = h - jnp.mean(h, axis=-1, keepdims=True)
    inv = lax.rsqrt(jnp.mean(centred * centred, axis=-1, keepdims=True) + 1e-12)
    return centred * inv, inv


def norm_back(g, normed, inv):
    return inv * (g - jnp.mean(g, axis=-1, keepdims=True) - normed * jnp.mean(g * normed, axis=-1, keepdims=True))


FORWARD_CHUNKS = (
    ("t", 0, "abxyc"), ("t", 1, "abxyc"), ("t", 2, "abyxc"), ("t", 3, "abxyc"), ("u", 0, "abxyc"), ("u", 1, "abyxc"), ("u", 2, "abxyc"),
    ("u", 3, "axbyc"), ("d", 0, "abyxc"), ("d", 2, "abxyc"), ("d", 1, "abyxc"), ("d", 3, "abxyc"),
)
FORWARD_PLAN = (
    (TOKENS, 0), (PAIR,), (BEGIN, 0), (BEGIN, 1), (RELAY, 0, 0), (BEGIN, 2), (TOKENS, 1), (RELAY, 1, 0), (BEGIN, 3), (RELAY, 0, 1),
    (RELAY, 2, 0), (BEGIN, 4), (RELAY, 1, 1), (RELAY, 0, 2), (RELAY, 2, 1), (RELAY, 3, 0), (BEGIN, 5), (TOKENS, 2), (RELAY, 4, 0),
    (BEGIN, 6), (RELAY, 1, 2), (RELAY, 3, 1), (RELAY, 0, 3), (RELAY, 5, 0), (BEGIN, 7), (RELAY, 0, 4), (RELAY, 2, 2), (RELAY, 4, 1),
    (RELAY, 3, 2), (RELAY, 1, 3), (RELAY, 5, 1), (RELAY, 6, 0), (BEGIN, 8), (TOKENS, 3), (BLOCK, 0), (BLOCK, 1), (RELAY, 1, 4),
    (RELAY, 2, 3), (OTHER, 0), (BLOCK, 2), (RELAY, 7, 0), (BEGIN, 9), (OTHER, 1), (RELAY, 2, 4), (RELAY, 6, 1), (OTHER, 2), (RELAY, 4, 2),
    (RELAY, 8, 0), (BEGIN, 10), (RELAY, 3, 3), (RELAY, 3, 4), (RELAY, 5, 2), (RELAY, 7, 1), (RELAY, 8, 1), (RELAY, 9, 0), (RELAY, 6, 2),
    (BEGIN, 11), (COTANGENT, 0), (COTANGENT, 1), (COTANGENT, 2), (COTANGENT, 3), (RELAY, 10, 0), (BLOCK, 3), (QUERY,), (RELAY, 4, 3),
    (RELAY, 5, 3), (RELAY, 7, 2), (OTHER, 3), (KEY,), (RELAY, 4, 4), (RELAY, 5, 4), (RELAY, 9, 1), (VALUE,), (RELAY, 8, 2), (RELAY, 11, 0),
    (HEAD, 0), (HEAD, 1), (RELAY, 6, 3), (HEAD, 2), (HEAD, 3), (RELAY, 6, 4), (RELAY, 7, 3), (HEAD, 4), (HEAD, 5), (RELAY, 7, 4),
    (HEAD, 6), (HEAD, 7), (HEAD, 8), (HEAD, 9), (RELAY, 9, 2), (RELAY, 10, 1), (HEAD, 10), (RELAY, 11, 1), (HEAD, 11), (RELAY, 8, 3),
    (BRANCH,), (RELAY, 8, 4), (RELAY, 9, 3), (UP, 0), (RELAY, 9, 4), (UP, 1), (RELAY, 10, 2), (RELAY, 11, 2), (UP, 2), (UP, 3), (DOWN, 0),
    (RELAY, 10, 3), (RELAY, 11, 3), (RELAY, 10, 4), (RELAY, 11, 4), (DOWN, 1),
)
BACKWARD_CHUNKS = (
    ("d", 2, "axbyc"), ("d", 0, "abxyc"), ("d", 3, "byaxc"), ("u", 0, "axbyc"), ("u", 3, "bxayc"), ("t", 3, "yabxc"), ("u", 2, "axbyc"),
    ("u", 1, "abyxc"), ("d", 1, "axbyc"), ("t", 2, "axbyc"), ("t", 0, "baxyc"), ("t", 1, "abxyc"),
)
BACKWARD_PLAN = (
    (GRAD_D, 2), (LAUNCH, 0), (GRAD_D, 0), (LAUNCH, 1), (HOME, 0), (HOME, 1), (HEAD_BACK, 0), (ABSORB, 0, 0), (GRAD_D, 3), (LAUNCH, 2),
    (ABSORB, 1, 0), (GRAD_U, 0), (LAUNCH, 3), (HOME, 2), (HOME, 3), (HEAD_BACK, 1), (ABSORB, 2, 0), (GRAD_U, 3), (LAUNCH, 4),
    (ABSORB, 0, 1), (ABSORB, 3, 0), (GRAD_T, 3), (LAUNCH, 5), (HEAD_BACK, 2), (ABSORB, 4, 0), (GRAD_U, 2), (LAUNCH, 6), (ABSORB, 1, 1),
    (ABSORB, 5, 0), (GRAD_U, 1), (LAUNCH, 7), (HEAD_BACK, 3), (ABSORB, 6, 0), (GRAD_D, 1), (LAUNCH, 8), (ABSORB, 2, 1), (ABSORB, 3, 1),
    (ABSORB, 0, 2), (ABSORB, 7, 0), (HEAD_BACK, 4), (ABSORB, 8, 0), (HEAD_BACK, 5), (HEAD_BACK, 6), (ABSORB, 1, 2), (ABSORB, 4, 1),
    (HEAD_BACK, 7), (ABSORB, 3, 2), (ABSORB, 5, 1), (HEAD_BACK, 8), (ABSORB, 1, 3), (ABSORB, 2, 2), (HEAD_BACK, 9), (ABSORB, 0, 3),
    (ABSORB, 6, 1), (HEAD_BACK, 10), (HEAD_BACK, 11), (EXCHANGE,), (ABSORB, 7, 1), (ABSORB, 5, 2), (ABSORB, 8, 1), (ABSORB, 4, 2),
    (ABSORB, 1, 4), (ABSORB, 3, 3), (ABSORB, 0, 4), (MERGE,), (GRAD_T, 2), (LAUNCH, 9), (ABSORB, 2, 3), (ABSORB, 4, 3), (ABSORB, 6, 2),
    (GRAD_T, 0), (LAUNCH, 10), (INPUT_GRAD,), (ABSORB, 5, 3), (ABSORB, 7, 2), (ABSORB, 6, 3), (ABSORB, 8, 2), (ABSORB, 9, 0),
    (ABSORB, 2, 4), (ABSORB, 10, 0), (ABSORB, 4, 4), (ABSORB, 3, 4), (GRAD_T, 1), (LAUNCH, 11), (ABSORB, 5, 4), (ABSORB, 11, 0),
    (ABSORB, 9, 1), (ABSORB, 10, 1), (ABSORB, 8, 3), (ABSORB, 11, 1), (ABSORB, 7, 3), (ABSORB, 10, 2), (ABSORB, 6, 4), (ABSORB, 9, 2),
    (ABSORB, 11, 2), (VECTORS,), (ABSORB, 8, 4), (ABSORB, 7, 4), (ABSORB, 9, 3), (ABSORB, 11, 3), (ABSORB, 10, 3), (ABSORB, 9, 4),
    (ABSORB, 10, 4), (ABSORB, 11, 4), (VECTORS_LAST,),
)
FORWARD = (FORWARD_PLAN, FORWARD_CHUNKS)
BACKWARD = (BACKWARD_PLAN, BACKWARD_CHUNKS)


S = pltpu.SemaphoreType.DMA
FC = 768


def total(v):
    return jnp.sum(v, axis=0, keepdims=True)


class Copies:
    def __init__(self):
        self.sent = []

    def start(self, describe, cond=None):
        def act(method):
            def run():
                src, dst, send, recv, to = describe()
                cp = pltpu.make_async_remote_copy(src_ref=src, dst_ref=dst, send_sem=send, recv_sem=recv, device_id=to, device_id_type=MESH)
                getattr(cp, method)()

            if cond is None:
                run()
            else:
                pl.when(cond())(run)

        act("start")
        self.sent.append(act)

    def start_or_keep(self, mine, describe, local):
        self.start(describe, lambda: jnp.logical_not(mine()))
        src, dst, *_ = describe()
        pl.when(mine())(pltpu.make_async_copy(src, dst, local).start)

    def arrive_or_keep(self, mine, dst, recv, local):
        pl.when(jnp.logical_not(mine))(lambda: arrive(dst, recv))
        pl.when(mine)(pltpu.make_async_copy(dst, dst, local).wait)

    def finish(self):
        for act in self.sent:
            act("wait_send")


def run_plan(plan, work, loops):
    def run(steps):
        for step, *args in steps:
            work[step](*args)

    kinds = [step[0] for step in plan]
    done = 0
    for kind, group in loops:
        first = kinds.index(kind)
        spots = [n for n, other in enumerate(kinds) if other == kind]
        run(plan[done:first])
        between = [plan[n + 1 : m] for n, m in zip(spots, spots[1:])] + [()]

        def body(turn, carry, kind=kind, group=group, between=between):
            for part in range(group):
                work[kind](turn, part)
                for n in range(part, len(between), group):
                    if between[n]:
                        pl.when(turn == n // group)(partial(run, between[n]))
            return carry

        lax.fori_loop(0, len(spots) // group, body, 0)
        done = spots[-1] + 1
    run(plan[done:])


def arrive(dst, recv):
    y, c, z, x = place()
    pltpu.make_async_remote_copy(src_ref=dst, dst_ref=dst, send_sem=recv, recv_sem=recv, device_id=device(y, c, z, x), device_id_type=MESH).wait_recv()


def forward_kernel(
    plan, chunks,
    xs, cot, seg, qw, kw, vw, ow, wup, wdt, upb, s0, s1, s2, s3, s4, s5, s6, s7,
    OUT, GF, GC, GST, LOWT, CTX, HID, GI, XO, Q, KT, V, E, CT, RS, WQ, VS,
    wt, wu, wd, pair_src, pair_dst, stage, xbuf, cbuf, sbuf, vec, vbuf, vb, ub,
    qb, kb, ktb, vb_, vtb, mask, ebuf, ctb, rsb, vsb, hid, gib, ctxb, n1, first, acc, rowbuf, outb, gsb, lowb, gcb, gsn,
    ps, pr, ws, wr, ls, xsnd, xrcv, fsnd, frcv, csnd, crcv, ssnd, srcv, vsnd, vrcv, lsem, osem, esem,
):
    y, c, z, x = place()
    j = 2 * z + x
    at = coords()
    partner = device(y, 1 - c, z, x)
    refs = (wt, wu, wd)
    copies = Copies()
    outs = []

    def put(src, dst):
        cp = pltpu.make_async_copy(src, dst, osem.at[len(outs)])
        cp.start()
        outs.append(cp)

    for i, w in enumerate((qw, kw, vw, ow)):
        pair_src[i] = w[...].astype(F32).T.astype(BF)
    vec[...] = jnp.zeros_like(vec)
    for i, v in enumerate((s0, s1, s2, s3, s4, s5, s6, s7)):
        vec[i : i + 1, 0:96] = v[...].astype(F32)
    vec[8:11, :] = upb[...].astype(F32)
    greet_all()()
    copies.start(lambda: (pair_src.at[:, pl.ds(48 * (1 - c), 48)], pair_dst, ps, pr, partner))

    def home(b):
        return (b // 2 == z) & (b % 2 == x) & (c == x)

    def send_tokens(src, dst, i, send, recv, local):
        def mine():
            return (z == (z + i) % 4) & (x == c) & (z // 2 == c)

        copies.start_or_keep(mine, lambda: (src.at[(z + i) % 4], dst.at[j % dst.shape[0]], send, recv.at[j % 4], device(y, z // 2, (z + i) % 4, c)), local)

    for i in range(4):
        for k in range(2):
            m = (z + i) % 4
            mine = (z == m) & (x == c) & (k == c)
            copies.start_or_keep(lambda v=mine: v, lambda m=m, i=i, k=k: (seg.at[m], sbuf.at[j], ssnd.at[2 * i + k], srcv.at[j], device(y, k, m, c)), lsem.at[1])
    pltpu.make_async_copy(vec, vbuf.at[j], lsem.at[2]).start()
    for d in range(1, 8):
        o = (j + d) % 8
        copies.start(lambda o=o, d=d: (vec, vbuf.at[j], vsnd.at[d], vrcv.at[d], device(y, c, o // 2, o % 2)))

    def pair_up():
        arrive(pair_dst, pr)
        own = pair_src[:, pl.ds(pl.multiple_of(48 * c, 16), 48), :]
        got = pair_dst[...]
        stage[...] = jnp.concatenate([jnp.where(c == 0, own, got), jnp.where(c == 0, got, own)], axis=-1)

    def source(ch):
        kind, i, _ = ch
        if kind == "t":
            return stage.at[i]
        if kind == "u":
            return wup.at[i]
        return wdt.at[i // 2, :, pl.ds(384 * (i % 2), 384)]

    def begin(u):
        ch = chunks[u]
        here = region(refs, ch, at)[0]
        pltpu.make_async_copy(source(ch), here, ls.at[u]).start()
        copies.start(lambda: (source(ch), region(refs, ch, at)[0], ws.at[u, 0, 0], wr.at[u, 0, 0], to_device(flip(at, ch[2][0]))))

    def relay(u, s):
        ch = chunks[u]
        order = ch[2]
        if s == 0:
            pltpu.make_async_copy(source(ch), region(refs, ch, at)[0], ls.at[u]).wait()

        def parts(at, s):
            if s < 3:
                return [region(refs, ch, whole(at, order[:s]))]
            return [region(refs, ch, whole(v, order[: s - 1])) for v in (at, flip(at, order[s - 1]))]

        def forward(s, h):
            def describe(k):
                part = parts(at, s)[h][k]
                return part, part, ws.at[u, s, 4 * h + k], wr.at[u, s, 4 * h + k], to_device(flip(at, order[s]))

            for k in range(len(parts(at, s)[h])):
                copies.start(partial(describe, k))

        for h, half in enumerate(parts(flip(at, order[s]), s)):
            for k, part in enumerate(half):
                arrive(part, wr.at[u, s, 4 * h + k])
        if s == 0:
            forward(1, 0)
        elif s == 1:
            forward(2, 0)
            forward(3, 0)
        elif s == 2:
            forward(3, 1)
            forward(4, 0)
        elif s == 3:
            forward(4, 1)

    def token_block(i):
        b = 4 * c + i
        copies.arrive_or_keep(home(b), xbuf.at[b], xrcv.at[i], lsem.at[0])
        copies.start(lambda: (xbuf.at[4 * c + i], xbuf.at[4 * c + i], fsnd.at[i], frcv.at[i], partner))

    def weight(i):
        return wt[i].reshape(768, 768)

    ready = []

    def vectors():
        if ready:
            return
        ready.append(True)
        pltpu.make_async_copy(vec, vbuf.at[j], lsem.at[2]).wait()
        for d in range(1, 8):
            arrive(vbuf.at[(j - d) % 8], vrcv.at[d])
        for b in range(8):
            copies.arrive_or_keep(home(b), sbuf.at[b], srcv.at[b], lsem.at[1])
        pieces = [vbuf[b] for b in range(8)]
        vb[...] = jnp.concatenate([p[:8, :96] for p in pieces], axis=-1)
        ub[...] = jnp.concatenate([p[8 + k : 9 + k, :] for p in pieces for k in range(3)], axis=-1)
        row = jnp.concatenate([sbuf[b] for b in range(8)], axis=-1).astype(F32)
        mine = jnp.concatenate([sbuf[4 * c + b] for b in range(4)], axis=-1).astype(F32)
        col = jnp.broadcast_to(row, (8, 1024)).T[:, :1]
        mask[...] = jnp.where(col == mine, 0.0, -1e30)

    def own_rows():
        return xbuf[pl.ds(4 * c, 4)].reshape(512, 768)

    def queries():
        vectors()
        put(xbuf.at[pl.ds(4 * c, 4)], XO)
        q = dot(own_rows(), weight(0), NT) + vb[0:1]
        qb[...] = (q.astype(BF).astype(F32) * 0.125).astype(BF)
        put(qb, Q)

    def keys():
        k = dot(xbuf[...].reshape(1024, 768), weight(1), NT)
        kb[...] = k.astype(BF)
        ktb[...] = k.T.astype(BF)
        put(ktb, KT)

    def values():
        vectors()
        v = dot(xbuf[...].reshape(1024, 768), weight(2), NT) + vb[1:2]
        vb_[...] = v.astype(BF)
        vtb[...] = v.T.astype(BF)
        put(vb_, V)

    def head(p, i):
        h = 2 * p + i
        cols = lanes(128 * p, 128)
        half = lax.broadcasted_iota(jnp.int32, (512, 128), 1) // 64
        qp = qb[:, cols]
        s = dot(kb[:, cols], jnp.where(half == i, qp, jnp.zeros_like(qp)), NT) + mask[...]
        e = jnp.exp(s - jnp.max(s, axis=0, keepdims=True))
        r = 1.0 / jnp.sum(e, axis=0, keepdims=True)
        pl.when(p > 0)(pltpu.make_async_copy(ebuf.at[i], E.at[h], esem.at[i]).wait)
        ebuf[i] = e.astype(BF)
        pltpu.make_async_copy(ebuf.at[i], E.at[h], esem.at[i]).start()
        rsb[pl.ds(h, 1), :] = r
        rows = pl.ds(pl.multiple_of(64 * h, 64), 64)
        ctb[rows, :] = (dot(vtb[rows, :], ebuf[i]) * r).astype(BF)

    def branch():
        put(wt.at[pl.ds(0, 3)], WQ)
        put(ctb, CT)
        put(rsb, RS)
        ctxb[...] = ctb[...].astype(F32).T.astype(BF)
        put(ctxb, CTX)
        normed, inv = norm(own_rows().astype(F32) + dot(ctxb[...], weight(3), NT) + vb[2:3])
        n1[...] = normed
        rowbuf[:, 0:1] = inv
        first[...] = normed * vb[3:4] + vb[4:5]
        lowb[...] = first[...].T.astype(BF)
        put(lowb, LOWT)

    def up(f, _):
        cols = lanes(FC * f, FC)
        inner = dot(first[...].astype(BF), wu[:, :, :, :, cols].reshape(768, FC)) + ub[:, cols]
        cdf = 0.5 * (1.0 + lax.erf(inner * 0.7071067811865476))
        pdf = jnp.exp(-0.5 * inner * inner) * 0.3989422804014327
        hid[:, cols] = (inner * cdf).astype(BF)
        gib[:, cols] = (cdf + inner * pdf).astype(BF)

    downs = []

    def down(b):
        if not downs:
            put(hid, HID)
            acc[...] = first[...] + vb[5:6]

        part = None
        for q in range(4):
            cols = slice(768 * q + 384 * b, 768 * q + 384 * b + 384)
            d = dot(hid[:, cols], wd[:, :, :, :, :, cols].reshape(768, 384), NT)
            part = d if part is None else part + d
        acc[...] += part
        downs.append(b)

    def second_norm():
        normed, inv = norm(acc[...])
        gain = vb[6:7]
        outb[...] = (normed * gain + vb[7:8]).astype(BF)
        put(outb, OUT)
        for b in range(4):
            copies.arrive_or_keep(home(4 * c + b), cbuf.at[b], crcv.at[b], lsem.at[3])
        g = cbuf[...].reshape(512, 768).astype(F32)
        vsb[...] = jnp.zeros_like(vsb)
        vsb[6:7, :768] = total(g * normed)
        vsb[7:8, :768] = total(g)
        gss = norm_back(g * gain, normed, inv)
        gs = gss.astype(BF)
        vsb[5:6, :768] = total(gs.astype(F32))
        acc[...] = gss
        gsb[...] = gss.T.astype(BF)
        put(gsb, GST)
        return gs

    def back(gs):
        gsn[...] = gs

        def step(f, carry):
            cols = lanes(FC * f, FC)
            gi = (dot(gsn[...], wd[:, :, :, :, :, cols].reshape(768, FC)) * gib[:, cols].astype(F32)).astype(BF)
            gib[:, cols] = gi
            vsb[8:9, cols] = total(gi.astype(F32))
            acc[...] += dot(gi, wu[:, :, :, :, cols].reshape(768, FC), NT)
            return carry

        lax.fori_loop(0, 3072 // FC, step, 0)
        put(gib, GI)
        gf = acc[...]
        vsb[3:4, :768] = total(gf * n1[...])
        vsb[4:5, :768] = total(gf)
        gsf = norm_back(gf * vb[3:4], n1[...], rowbuf[:, 0:1])
        first[...] = gsf
        put(first, GF)
        gb = gsf.astype(BF)
        vsb[2:3, :768] = total(gb.astype(F32))
        VS[...] = vsb[...]
        gcb[...] = dot(gb, weight(3)).astype(BF)
        put(gcb, GC)

    def tokens(i):
        send_tokens(xs, xbuf, i, xsnd.at[i], xrcv, lsem.at[0])

    def cotangent(i):
        send_tokens(cot, cbuf, i, csnd.at[i], crcv, lsem.at[3])

    def other_block(i):
        arrive(xbuf.at[4 * (1 - c) + i], frcv.at[i])

    work = {
        BEGIN: begin, RELAY: relay, TOKENS: tokens, BLOCK: token_block, OTHER: other_block, COTANGENT: cotangent, PAIR: pair_up,
        QUERY: queries, KEY: keys, VALUE: values, HEAD: head, BRANCH: branch, UP: up, DOWN: down,
    }
    run_plan(plan, work, ((HEAD, 2), (UP, 1)))
    back(second_norm())
    for i in range(2):
        pltpu.make_async_copy(ebuf.at[i], E.at[10 + i], esem.at[i]).wait()
    for cp in outs:
        cp.wait()
    copies.finish()


def forward_call(plan, chunks, xs, cot, seg, qw, kw, vw, ow, wup, wdt, small, upb):
    n = len(chunks)
    V_ = pltpu.VMEM
    row = (512, 768)
    return pl.pallas_call(
        partial(forward_kernel, plan, chunks),
        out_shape=[
            sds(row), sds(row, F32), sds(row), sds((768, 512)), sds((768, 512)), sds(row), sds((512, 3072)), sds((512, 3072)),
            sds((4, 128, 768)), sds(row), sds((768, 1024)), sds((1024, 768)), sds((12, 1024, 512)), sds((768, 512)), sds((16, 512), F32),
            sds((3, 2, 2, 2, 2, 48, 768)), sds((16, 3072), F32),
        ],
        in_specs=[ANY, ANY] + [VM] * 16,
        out_specs=[ANY] * 16 + [VM],
        scratch_shapes=[
            V_((4, 2, 2, 2, 2, 48, 768), BF), V_((2, 2, 4, 48, 3072), BF), V_((2, 2, 2, 2, 48, 3072), BF),
            V_((4, 96, 192), BF), V_((4, 48, 192), BF), V_((4, 48, 384), BF), V_((8, 128, 768), BF), V_((4, 128, 768), BF),
            V_((8, 1, 128), jnp.int32), V_((16, 128), F32), V_((8, 16, 128), F32), V_((8, 768), F32), V_((1, 3072), F32),
            V_(row, BF), V_((1024, 768), BF), V_((768, 1024), BF), V_((1024, 768), BF), V_((768, 1024), BF), V_((1024, 512), F32),
            V_((2, 1024, 512), BF), V_((768, 512), BF), V_((16, 512), F32), V_((16, 3072), F32), V_((512, 3072), BF), V_((512, 3072), BF),
            V_(row, BF), V_(row, F32), V_(row, F32), V_(row, F32), V_((512, 128), F32), V_(row, BF), V_((768, 512), BF), V_((768, 512), BF), V_(row, BF), V_(row, BF),
            S, S, S((n, 5, 8)), S((n, 5, 8)), S((n,)), S((4,)), S((4,)), S((4,)), S((4,)), S((4,)), S((4,)), S((8,)), S((8,)), S((8,)), S((8,)),
            S((4,)), S((24,)), S((2,)),
        ],
        name="forward",
        compiler_params=pltpu.CompilerParams(collective_id=1, has_side_effects=True, vmem_limit_bytes=59 * 2**20),
    )(xs, cot, seg, qw, kw, vw, ow, wup, wdt, upb, *small)


def landing(at, order, s):
    spot = dict(at)
    for d in order[s + 1 :]:
        spot[d] = 1 - at[d]
    return whole(spot, order[:s])


def backward_kernel(
    plan, chunks,
    OUT, GF, GC, GST, LOWT, CTX, HID, GI, XO, Q, KT, V, E, CT, RS, WQ, VS,
    LO, IG, D4, DU, DD, VO,
    gt, gu, gd, rt, ru, rd, hid, gib, gst, lowt, xb, qb, ktb, vb, ctb, gcb, gct, gfb, ebuf,
    dqt, dkb, dvb, dkr, dvr, igb, rcol, vpack, vrecv, vsum, vrecv2, pairs, pairr, fin,
    isem, esem, lsem, ks, kr, os_, or_, gs, gr, vs_, vr, ws, wr, ps, pr,
):
    y, c, z, x = place()
    j = 2 * z + x
    at = coords()
    partner = device(y, 1 - c, z, x)
    G, R = (gt, gu, gd), (rt, ru, rd)
    copies = Copies()
    loads = {}
    for src, dst, name in (
        (GST, gst, "gst"), (HID, hid, "hid"), (LOWT, lowt, "lowt"), (GI, gib, "gi"), (V, vb, "v"), (Q, qb, "q"), (GC, gcb, "gc"), (KT, ktb, "kt"),
        (CT, ctb, "ct"), (CTX, igb, "ctx"), (XO, xb, "x"), (GF, gfb, "gf"),
    ):
        cp = pltpu.make_async_copy(src, dst, isem.at[len(loads)])
        cp.start()
        loads[name] = cp
    for i in range(2):
        pltpu.make_async_copy(E.at[i], ebuf.at[i], esem.at[i]).start()

    def need(*names):
        for n in names:
            if n in loads:
                loads.pop(n).wait()

    all_here = greet_all()

    def send_home(src, out, w, k):
        def mine():
            b = 4 * c + k
            return (x == c) & (b // 2 == z) & (b % 2 == x)

        def describe():
            b = 4 * c + k
            return src.at[pl.ds(128 * k, 128)], out.at[z], os_.at[w, k], or_.at[w, z], device(y, x, b // 2, b % 2)

        copies.start_or_keep(mine, describe, lsem.at[w])

    def send_out(k):
        send_home(OUT, LO, 0, k)

    def send_grad(k):
        send_home(igb, IG, 1, k)

    def halves(order, s, at):
        if s == 3:
            return [flip(at, order[2]), at]
        return [at]

    def stage(ch, s, at, h):
        order = ch[2]
        spot = landing(at, order, s)
        own = whole(at, order[:s])
        if s == 3:
            own[order[2]] = spot[order[2]] = halves(order, s, at)[h][order[2]]
        return region(G, ch, own), region(R, ch, spot)

    def launch(u, s):
        ch = chunks[u]
        to = flip(at, ch[2][s])

        def describe(h, k):
            to = flip(at, ch[2][s])
            src, dst = stage(ch, s, to, h)
            return src[k], dst[k], gs.at[u, s, 4 * h + k], gr.at[u, s, 4 * h + k], to_device(to)

        for h in range(2 if s == 3 else 1):
            for k in range(len(stage(ch, s, to, h)[0])):
                copies.start(partial(describe, h, k))

    def take(u, s, h):
        for k, (own, got) in enumerate(zip(*stage(chunks[u], s, at, h))):
            arrive(got, gr.at[u, s, 4 * h + k])
            own[...] = own[...] + got[...]

    def absorb(u, s):
        kind, i, order = ch = chunks[u]
        if s > 0:
            if s == 2:
                take(u, 3, 1)
            take(u, s, 0)
            launch(u, s - 1)
            return
        (own,), (got,) = stage(ch, 0, at, 0)
        arrive(got, gr.at[u, 0, 0])
        done = own[...].astype(F32) + got[...].astype(F32)
        if kind == "u":
            DU[i] = done
        elif kind == "d":
            DD[i // 2, :, 384 * (i % 2) : 384 * (i % 2) + 384] = done
        else:
            lo, hi = done[:, :192], done[:, 192:]
            fin[i, pl.ds(pl.multiple_of(48 * c, 16), 48), :] = jnp.where(c == 0, lo, hi)
            pairs[i] = jnp.where(c == 0, hi, lo)
            copies.start(lambda: (pairs.at[i], pairr.at[i], ps.at[i], pr.at[i], partner))

    made = []

    def grad_u(i):
        made.append(i)
        need("lowt", "gi")
        rows = lowt[...].reshape(2, 2, 4, 48, 512)[:, :, i].reshape(192, 512)

        def columns(q, carry):
            cols = lanes(768 * q, 768)
            gu[:, :, i, :, cols] = dot(rows, gib[:, cols]).astype(BF).reshape(2, 2, 48, 768)
            return carry

        lax.fori_loop(0, 4, columns, 0)

    def grad_d(i):
        made.append(i)
        need("gst", "hid")
        rows = gst[...].reshape(2, 2, 2, 2, 48, 512)[:, :, :, i // 2].reshape(384, 512)

        def columns(q, carry):
            cols = lanes(768 * q + 384 * (i % 2), 384)
            gd[:, :, :, i // 2, :, cols] = dot(rows, hid[:, cols]).astype(BF).reshape(2, 2, 2, 48, 384)
            return carry

        lax.fori_loop(0, 4, columns, 0)

    shape = (2, 2, 2, 2, 48, 768)

    def grad_t(i):
        if i == 3:
            need("gf", "ctx")
            gt[3] = dot(gfb[...].T.astype(BF), igb[...]).astype(BF).reshape(shape)
            return
        need("x")
        if i == 0:
            left = dqt[...]
        else:
            left = (dkr if i == 1 else dvr)[...].astype(F32).T.astype(BF)
        gt[i] = dot(left, xb[...].reshape(512, 768)).astype(BF).reshape(shape)

    def ready():
        need("gc", "v", "q", "kt", "ct")
        gct[...] = gcb[...].astype(F32).T.astype(BF)
        rcol[...] = RS[...].T

    def head(p, i):
        h = 2 * p + i
        cols = lanes(128 * p, 128)
        rows = pl.ds(pl.multiple_of(64 * h, 64), 64)
        qp = qb[:, cols]
        half = lax.broadcasted_iota(jnp.int32, (512, 128), 1) // 64
        column = lax.broadcasted_iota(jnp.int32, (512, 16), 1)
        scale = jnp.sum(jnp.where(column == h, rcol[...], 0.0), axis=1, keepdims=True)
        gm = jnp.where(half == i, gcb[:, cols].astype(F32) * scale, 0.0).astype(BF)
        qm = jnp.where(half == i, qp, jnp.zeros_like(qp))
        delta = total(ctb[rows, :].astype(F32) * gct[rows, :].astype(F32)) * RS[pl.ds(h, 1), :]
        pltpu.make_async_copy(E.at[h], ebuf.at[i], esem.at[i]).wait()
        ds = (ebuf[i].astype(F32) * (dot(vb[:, cols], gm, NT) - delta)).astype(BF)
        dv = dot(ebuf[i], gm)
        dk = dot(ds, qm)
        dqt[rows, :] = (dot(ktb[rows, :], ds) * 0.125).astype(BF)
        pl.when(p < 5)(pltpu.make_async_copy(E.at[jnp.minimum(h + 2, 11)], ebuf.at[i], esem.at[i]).start)
        dkb[:, cols] = dk.astype(BF) if i == 0 else (dkb[:, cols].astype(F32) + dk).astype(BF)
        dvb[:, cols] = dv.astype(BF) if i == 0 else (dvb[:, cols].astype(F32) + dv).astype(BF)

    theirs = pl.ds(pl.multiple_of(512 * (1 - c), 128), 512)
    ours = pl.ds(pl.multiple_of(512 * c, 128), 512)

    def weight_copies():
        for i in range(3):
            cols = slice(768 * i, 768 * i + 768)
            yield pltpu.make_async_copy(WQ.at[i, pl.ds(0, 512)], hid.at[:, cols], isem.at[13 + 2 * i])
            yield pltpu.make_async_copy(WQ.at[i, pl.ds(512, 256)], gib.at[pl.ds(0, 256), cols], isem.at[14 + 2 * i])

    def exchange():
        assert len(made) == 8
        for cp in weight_copies():
            cp.start()
        copies.start(lambda: (dkb.at[theirs], dkr, ks.at[0], kr.at[0], partner))
        copies.start(lambda: (dvb.at[theirs], dvr, ks.at[1], kr.at[1], partner))

    def merge():
        arrive(dkr, kr.at[0])
        arrive(dvr, kr.at[1])
        dkr[...] = (dkb[ours].astype(F32) + dkr[...].astype(F32)).astype(BF)
        dvr[...] = (dvb[ours].astype(F32) + dvr[...].astype(F32)).astype(BF)

    def token_grads():
        need("gf")
        for cp in weight_copies():
            cp.wait()
        dq = dqt[...].astype(F32).T
        ig = gfb[...]
        for i, g in enumerate((dq.astype(BF), dkr[...], dvr[...])):
            cols = slice(768 * i, 768 * i + 768)
            ig = ig + dot(g[:, :512], hid[:, cols]) + dot(g[:, 512:], gib[:256, cols])
        low = jnp.concatenate([total(dq), total(dvr[...].astype(F32)), VS[2:8, :768]], axis=0)
        vpack[...] = jnp.zeros_like(vpack)
        for b in range(8):
            vpack[b, 0:8, 0:96] = low[:, 96 * b : 96 * b + 96]
            vpack[b, 8:9, :] = VS[8:9, 384 * b : 384 * b + 384]
        for d in range(1, 8):
            o = (j + d) % 8
            copies.start(lambda o=o, d=d: (vpack.at[o], vrecv.at[d], vs_.at[d], vr.at[d], device(y, c, o // 2, o % 2)))
        igb[...] = ig.astype(BF)
        for k in range(4):
            send_grad(k)

    def vectors_first():
        acc = vpack[j]
        for d in range(1, 8):
            arrive(vrecv.at[d], vr.at[d])
            acc = acc + vrecv[d]
        vsum[...] = acc
        me = 2 * y + c
        for d in range(1, 4):
            copies.start(lambda d=d: (vsum, vrecv2.at[d], ws.at[d], wr.at[d], ((me + d) % 4, j)))

    def vectors_last():
        acc = vsum[...]
        for d in range(1, 4):
            arrive(vrecv2.at[d], wr.at[d])
            acc = acc + vrecv2[d]
        VO[...] = acc

    work = {
        LAUNCH: lambda u: launch(u, 4), ABSORB: lambda u, s: absorb(u, 4 - s), HOME: send_out, GRAD_U: grad_u, GRAD_D: grad_d, GRAD_T: grad_t,
        HEAD_BACK: head, EXCHANGE: exchange, MERGE: merge, INPUT_GRAD: token_grads, VECTORS: vectors_first, VECTORS_LAST: vectors_last,
    }
    early = [step for step in plan if step[0] in (GRAD_U, GRAD_D)][:3]
    run_plan(early, work, ())
    all_here()
    plan = [step for step in plan if step not in early]
    loops_at = [step[0] for step in plan].index(HEAD_BACK)
    run_plan(plan[:loops_at], work, ())
    ready()
    run_plan(plan[loops_at:], work, ((HEAD_BACK, 2),))
    for i in range(4):
        arrive(pairr.at[i], pr.at[i])
        fin[i, pl.ds(pl.multiple_of(48 * (1 - c), 16), 48), :] = pairr[i]
        D4[i] = fin[i].T
    for w, out in ((0, LO), (1, IG)):
        for m in range(4):
            copies.arrive_or_keep((m == z) & (x == c) & (z // 2 == c), out.at[m], or_.at[w, m], lsem.at[w])
    copies.finish()


def backward_call(plan, chunks, OUT, GF, GC, GST, LOWT, CTX, HID, GI, XO, Q, KT, V, E, CT, RS, WQ, VS):
    n = len(chunks)
    V_ = pltpu.VMEM
    row = (512, 768)
    col = (768, 512)
    sets = [V_((4, 2, 2, 2, 2, 48, 768), BF), V_((2, 2, 4, 48, 3072), BF), V_((2, 2, 2, 2, 48, 3072), BF)]
    return pl.pallas_call(
        partial(backward_kernel, plan, chunks),
        out_shape=[sds((4, 128, 768)), sds((4, 128, 768))] + [sds((4, 192, 96), F32), sds((4, 48, 384), F32), sds((2, 48, 768), F32), sds((16, 384), F32)],
        in_specs=[ANY] * 14 + [VM, ANY, VM],
        out_specs=[ANY, ANY] + [VM] * 4,
        scratch_shapes=sets + sets + [
            V_((512, 3072), BF), V_((512, 3072), BF), V_(col, BF), V_(col, BF), V_((4, 128, 768), BF), V_(row, BF),
            V_((768, 1024), BF), V_((1024, 768), BF), V_(col, BF), V_(row, BF), V_(col, BF), V_(row, F32), V_((2, 1024, 512), BF),
            V_(col, BF), V_((1024, 768), BF), V_((1024, 768), BF), V_(row, BF), V_(row, BF), V_(row, BF), V_((512, 16), F32),
            V_((8, 16, 384), F32), V_((8, 16, 384), F32), V_((16, 384), F32), V_((4, 16, 384), F32), V_((4, 48, 192), F32), V_((4, 48, 192), F32), V_((4, 96, 192), F32),
            S((19,)), S((2,)), S((2,)), S((2,)), S((2,)), S((2, 4)), S((2, 4)), S((n, 5, 8)), S((n, 5, 8)), S((8,)), S((8,)), S((4,)), S((4,)), S((4,)), S((4,)),
        ],
        name="backward",
        compiler_params=pltpu.CompilerParams(collective_id=2, has_side_effects=True, vmem_limit_bytes=59 * 2**20),
    )(OUT, GF, GC, GST, LOWT, CTX, HID, GI, XO, Q, KT, V, E, CT, RS, WQ.reshape(3, 768, 768), VS)


def finish_kernel(lo, ig, d4, du, dd, vo, LO, IG, DQ, DK, DV, DO, DU, DD, *rest):
    rows, held, (sem_in, sem_out) = rest[:9], rest[9:17], rest[17:]
    pairs = [(lo, LO), (ig, IG), (du, DU), (dd, DD)] + [(d4.at[i], out) for i, out in enumerate((DQ, DK, DV, DO))]
    taken = [pltpu.make_async_copy(src, buf, sem_in.at[i]) for i, ((src, _), buf) in enumerate(zip(pairs, held))]
    given = [pltpu.make_async_copy(buf, dst, sem_out.at[i]) for i, ((_, dst), buf) in enumerate(zip(pairs, held))]
    for cp in taken:
        cp.start()
    for i, row in enumerate(rows):
        row[...] = vo[i : i + 1, : row.shape[1]]
    for one, other in zip(taken, given):
        one.wait()
        other.start()
    for cp in given:
        cp.wait()


def finish_call(lo, ig, d4, du, dd, vo):
    return pl.pallas_call(
        finish_kernel,
        out_shape=[sds((4, 128, 768)), sds((4, 128, 768))] + [sds((192, 96), F32)] * 4 + [sds((4, 48, 384), F32), sds((2, 48, 768), F32)]
        + [sds((1, 96), F32)] * 8 + [sds((1, 384), F32)],
        in_specs=[ANY] * 5 + [VM],
        out_specs=[ANY] * 8 + [VM] * 9,
        scratch_shapes=[pltpu.VMEM((4, 128, 768), BF)] * 2 + [pltpu.VMEM((4, 48, 384), F32), pltpu.VMEM((2, 48, 768), F32)] + [pltpu.VMEM((192, 96), F32)] * 4
        + [pltpu.SemaphoreType.DMA((8,))] * 2,
        name="finish",
    )(lo, ig, d4, du, dd, vo)


def rows_on_chips(
    inputs, segment_ids, query_weight, query_bias, key_weight, value_weight, value_bias, output_weight, output_bias,
    first_gain, first_shift, up_weight, up_bias, down_weight, down_bias, second_gain, second_shift, cotangent,
):
    small = [v.reshape(1, 96) for v in (query_bias, value_bias, output_bias, first_gain, first_shift, down_bias, second_gain, second_shift)]
    kept = forward_call(
        *FORWARD, inputs.reshape(4, 128, 768), cotangent.reshape(4, 128, 768), segment_ids.reshape(4, 1, 128),
        query_weight, key_weight, value_weight, output_weight, up_weight.reshape(4, 48, 384), down_weight.T.reshape(2, 48, 768),
        small, up_bias.reshape(3, 128),
    )
    LO, IG, DQ, DK, DV, DO, DU, DD, *v = finish_call(*backward_call(*BACKWARD, *kept))
    v = [row.reshape(-1) for row in v]
    s = (4, 1, 128, 768)
    return (
        LO.reshape(s), IG.reshape(s), DQ, v[0], DK, DV, v[1], DO, v[2], v[3], v[4], DU.reshape(192, 384), v[8], DD.reshape(96, 768).T, v[5], v[6], v[7],
    )


EPSILON = 1e-12
NEGATIVE = -1e30


def product(left, right, form):
    return jnp.einsum(form, left, right, preferred_element_type=jnp.float32)


def normalize(hidden, gain, shift):
    centred = hidden - jnp.mean(hidden, axis=-1, keepdims=True)
    scale_inv = lax.rsqrt(jnp.mean(centred * centred, axis=-1, keepdims=True) + EPSILON)
    normed = centred * scale_inv
    return (normed * gain + shift, normed, scale_inv)


def normalize_back(grad_normed, normed, scale_inv):
    centred_grad = grad_normed - jnp.mean(grad_normed, axis=-1, keepdims=True)
    return scale_inv * (
        centred_grad - normed * jnp.mean(grad_normed * normed, axis=-1, keepdims=True)
    )


def same_passage(query_pair, key_pair):
    return jnp.all(query_pair[:, :, None, :] == key_pair[:, None, :, :], axis=-1)[:, None]


def micro_step(shared, tokens, passage_ids, cotan):
    (
        weight_query,
        weight_key,
        weight_value,
        weight_out,
        weight_up,
        weight_down,
        bias_query,
        bias_value,
        bias_out,
        gain_first,
        shift_first,
        bias_up,
        bias_down,
        gain_second,
        shift_second,
    ) = shared
    bias_query = bias_query.astype(jnp.float32)
    bias_value = bias_value.astype(jnp.float32)
    bias_out = bias_out.astype(jnp.float32)
    gain_first = gain_first.astype(jnp.float32)
    shift_first = shift_first.astype(jnp.float32)
    bias_up = bias_up.astype(jnp.float32)
    bias_down = bias_down.astype(jnp.float32)
    gain_second = gain_second.astype(jnp.float32)
    shift_second = shift_second.astype(jnp.float32)
    row_count, seq_count, width = tokens.shape
    token_count = row_count * seq_count
    scale = HD ** (-0.5)
    flat = tokens.reshape(token_count, width)
    queries = (product(flat, weight_query, "md,de->me") + bias_query).astype(jnp.bfloat16)
    keys = product(flat, weight_key, "md,de->me").astype(jnp.bfloat16)
    values = (product(flat, weight_value, "md,de->me") + bias_value).astype(jnp.bfloat16)
    query_four = queries.reshape(row_count, seq_count, HEADS, HD)
    pair_local = jnp.stack((passage_ids // 256, passage_ids % 256), axis=-1).astype(jnp.bfloat16)
    key_rows = keys.reshape(row_count, seq_count, width)
    value_rows = values.reshape(row_count, seq_count, width)
    key_local = key_rows.reshape(row_count, seq_count, HEADS, HD)
    value_local = value_rows.reshape(row_count, seq_count, HEADS, HD)
    running_max = jnp.full((row_count, HEADS, seq_count), NEGATIVE, jnp.float32)
    running_acc = jnp.zeros((row_count, seq_count, HEADS, HD), jnp.float32)
    key_piece = lax.all_gather(key_rows, "blk", axis=1, tiled=True)
    value_piece = lax.all_gather(value_rows, "blk", axis=1, tiled=True)
    pair_piece = lax.all_gather(pair_local, "blk", axis=1, tiled=True)
    count = key_piece.shape[1]
    key_four = key_piece.reshape(row_count, count, HEADS, HD)
    value_four = value_piece.reshape(row_count, count, HEADS, HD)
    allowed = same_passage(pair_local, pair_piece)
    scores = jnp.where(allowed, product(query_four, key_four, "rqhd,rkhd->rhqk") * scale, NEGATIVE)
    fresh_max = jnp.maximum(running_max, jnp.max(scores, axis=-1))
    weights = jnp.where(allowed, jnp.exp(scores - fresh_max[..., None]), 0.0)
    decay = jnp.exp(running_max - fresh_max)
    running_sum = jnp.sum(weights, axis=-1)
    mixed = product(weights.astype(jnp.bfloat16), value_four, "rhqk,rkhd->rqhd")
    running_acc = running_acc * jnp.swapaxes(decay, 1, 2)[..., None] + mixed
    running_max, running_sum, running_acc = (fresh_max, running_sum, running_acc)
    log_total = running_max + jnp.log(running_sum)
    attended = running_acc / jnp.swapaxes(running_sum, 1, 2)[..., None]
    context = attended.reshape(token_count, width).astype(jnp.bfloat16)
    branch = product(context, weight_out, "md,de->me") + bias_out
    first, normed_first, inv_first = normalize(
        flat.astype(jnp.float32) + branch, gain_first, shift_first
    )
    first_low = first.astype(jnp.bfloat16)
    inner = product(first_low, weight_up, "md,df->mf") + bias_up
    activation, gelu_pull = jax.vjp(partial(jax.nn.gelu, approximate=False), inner)
    hidden = activation.astype(jnp.bfloat16)
    second = product(hidden, weight_down, "mf,fd->md") + bias_down
    output, normed_second, inv_second = normalize(first + second, gain_second, shift_second)
    upstream = cotan.reshape(token_count, width).astype(jnp.float32)
    grad_gain_second = jnp.sum(upstream * normed_second, axis=0, keepdims=True)
    grad_shift_second = jnp.sum(upstream, axis=0, keepdims=True)
    grad_sum_second = normalize_back(upstream * gain_second, normed_second, inv_second)
    grad_second = grad_sum_second.astype(jnp.bfloat16)
    grad_weight_down = product(hidden, grad_second, "mf,md->fd")
    grad_bias_down = jnp.sum(grad_second.astype(jnp.float32), axis=0, keepdims=True)
    grad_inner = gelu_pull(product(grad_second, weight_down, "md,fd->mf"))[0].astype(jnp.bfloat16)
    grad_weight_up = product(first_low, grad_inner, "md,mf->df")
    grad_bias_up = jnp.sum(grad_inner.astype(jnp.float32), axis=0, keepdims=True)
    grad_first = grad_sum_second + product(grad_inner, weight_up, "mf,df->md")
    grad_gain_first = jnp.sum(grad_first * normed_first, axis=0, keepdims=True)
    grad_shift_first = jnp.sum(grad_first, axis=0, keepdims=True)
    grad_sum_first = normalize_back(grad_first * gain_first, normed_first, inv_first)
    grad_branch = grad_sum_first.astype(jnp.bfloat16)
    grad_weight_out = product(context, grad_branch, "md,me->de")
    grad_bias_out = jnp.sum(grad_branch.astype(jnp.float32), axis=0, keepdims=True)
    grad_context = product(grad_branch, weight_out, "me,de->md").astype(jnp.bfloat16)
    grad_context_four = grad_context.reshape(row_count, seq_count, HEADS, HD)
    delta = jnp.swapaxes(jnp.sum(grad_context_four.astype(jnp.float32) * attended, axis=-1), 1, 2)
    key_piece = lax.all_gather(key_rows, "blk", axis=1, tiled=True)
    value_piece = lax.all_gather(value_rows, "blk", axis=1, tiled=True)
    pair_piece = lax.all_gather(pair_local, "blk", axis=1, tiled=True)
    count = key_piece.shape[1]
    key_four = key_piece.reshape(row_count, count, HEADS, HD)
    value_four = value_piece.reshape(row_count, count, HEADS, HD)
    allowed = same_passage(pair_local, pair_piece)
    scores = jnp.where(allowed, product(query_four, key_four, "rqhd,rkhd->rhqk") * scale, NEGATIVE)
    probs = jnp.where(allowed, jnp.exp(scores - log_total[..., None]), 0.0)
    grad_probs = product(grad_context_four, value_four, "rqhd,rkhd->rhqk")
    grad_scores = (probs * (grad_probs - delta[..., None])).astype(jnp.bfloat16)
    grad_query_acc = product(grad_scores, key_four, "rhqk,rkhd->rqhd") * scale
    grad_queries = grad_query_acc.reshape(token_count, width).astype(jnp.bfloat16)
    pair_wide = pair_local.astype(jnp.float32)
    sent = (
        queries.reshape(row_count, seq_count, width).astype(jnp.float32),
        grad_context.reshape(row_count, seq_count, width).astype(jnp.float32),
        jnp.swapaxes(log_total, 1, 2),
        jnp.swapaxes(delta, 1, 2),
        pair_wide,
    )
    query_piece = lax.all_gather(sent[0], "blk", axis=1, tiled=True)
    context_piece = lax.all_gather(sent[1], "blk", axis=1, tiled=True)
    total_piece = lax.all_gather(sent[2], "blk", axis=1, tiled=True)
    delta_piece = lax.all_gather(sent[3], "blk", axis=1, tiled=True)
    pair_piece = lax.all_gather(sent[4], "blk", axis=1, tiled=True)
    count = query_piece.shape[1]
    query_part = query_piece.astype(jnp.bfloat16).reshape(row_count, count, HEADS, HD)
    context_part = context_piece.astype(jnp.bfloat16).reshape(row_count, count, HEADS, HD)
    total_part = jnp.swapaxes(total_piece, 1, 2)
    delta_part = jnp.swapaxes(delta_piece, 1, 2)
    allowed = same_passage(pair_piece, pair_wide)
    scores = jnp.where(allowed, product(query_part, key_local, "rqhd,rkhd->rhqk") * scale, NEGATIVE)
    probs = jnp.where(allowed, jnp.exp(scores - total_part[..., None]), 0.0)
    grad_value_acc = product(probs.astype(jnp.bfloat16), context_part, "rhqk,rqhd->rkhd")
    grad_probs = product(context_part, value_local, "rqhd,rkhd->rhqk")
    grad_scores = (probs * (grad_probs - delta_part[..., None])).astype(jnp.bfloat16)
    grad_key_acc = product(grad_scores, query_part, "rhqk,rqhd->rkhd") * scale
    grad_key_acc, grad_value_acc = (grad_key_acc, grad_value_acc)
    grad_keys = grad_key_acc.reshape(token_count, width).astype(jnp.bfloat16)
    grad_values = grad_value_acc.reshape(token_count, width).astype(jnp.bfloat16)
    grad_weight_query = product(flat, grad_queries, "md,me->de")
    grad_bias_query = jnp.sum(grad_queries.astype(jnp.float32), axis=0, keepdims=True)
    grad_weight_key = product(flat, grad_keys, "md,me->de")
    grad_weight_value = product(flat, grad_values, "md,me->de")
    grad_bias_value = jnp.sum(grad_values.astype(jnp.float32), axis=0, keepdims=True)
    grad_tokens = (
        grad_sum_first
        + product(grad_queries, weight_query, "me,de->md")
        + product(grad_keys, weight_key, "me,de->md")
        + product(grad_values, weight_value, "me,de->md")
    )
    contributions = (
        grad_weight_query,
        grad_weight_key,
        grad_weight_value,
        grad_weight_out,
        grad_weight_up,
        grad_weight_down,
        grad_bias_query,
        grad_bias_value,
        grad_bias_out,
        grad_gain_first,
        grad_shift_first,
        grad_bias_up,
        grad_bias_down,
        grad_gain_second,
        grad_shift_second,
    )
    return (
        output.astype(jnp.bfloat16).reshape(row_count, seq_count, width),
        grad_tokens.astype(jnp.bfloat16).reshape(row_count, seq_count, width),
        contributions,
    )


def general(
    inputs,
    segment_ids,
    query_weight,
    query_bias,
    key_weight,
    value_weight,
    value_bias,
    output_weight,
    output_bias,
    first_gain,
    first_shift,
    up_weight,
    up_bias,
    down_weight,
    down_bias,
    second_gain,
    second_shift,
    cotangent,
):
    outputs = []
    input_grads = []
    totals = None
    widened = (
        lax.all_gather(query_weight, "blk", axis=1, tiled=True),
        lax.all_gather(key_weight, "blk", axis=1, tiled=True),
        lax.all_gather(value_weight, "blk", axis=1, tiled=True),
        lax.all_gather(output_weight, "blk", axis=1, tiled=True),
        lax.all_gather(up_weight, "blk", axis=1, tiled=True),
        lax.all_gather(down_weight, "blk", axis=1, tiled=True),
        lax.all_gather(query_bias.reshape(1, -1), "blk", axis=1, tiled=True),
        lax.all_gather(value_bias.reshape(1, -1), "blk", axis=1, tiled=True),
        lax.all_gather(output_bias.reshape(1, -1), "blk", axis=1, tiled=True),
        lax.all_gather(first_gain.reshape(1, -1), "blk", axis=1, tiled=True),
        lax.all_gather(first_shift.reshape(1, -1), "blk", axis=1, tiled=True),
        lax.all_gather(up_bias.reshape(1, -1), "blk", axis=1, tiled=True),
        lax.all_gather(down_bias.reshape(1, -1), "blk", axis=1, tiled=True),
        lax.all_gather(second_gain.reshape(1, -1), "blk", axis=1, tiled=True),
        lax.all_gather(second_shift.reshape(1, -1), "blk", axis=1, tiled=True),
    )
    complete = (
        lax.all_gather(widened[0], "dp", axis=0, tiled=True),
        lax.all_gather(widened[1], "dp", axis=0, tiled=True),
        lax.all_gather(widened[2], "dp", axis=0, tiled=True),
        lax.all_gather(widened[3], "dp", axis=0, tiled=True),
        lax.all_gather(widened[4], "dp", axis=0, tiled=True),
        lax.all_gather(widened[5], "dp", axis=0, tiled=True),
    )
    shared = tuple(complete) + tuple(widened[6:])
    for batch_index in range(inputs.shape[0]):
        layer_out, layer_grad, contributions = micro_step(
            shared, inputs[batch_index], segment_ids[batch_index], cotangent[batch_index]
        )
        outputs.append(layer_out)
        input_grads.append(layer_grad)
        if totals is None:
            totals = contributions
        else:
            totals = tuple((earlier + latest for earlier, latest in zip(totals, contributions)))
    narrowed = (
        lax.psum_scatter(totals[0], "blk", scatter_dimension=1, tiled=True),
        lax.psum_scatter(totals[1], "blk", scatter_dimension=1, tiled=True),
        lax.psum_scatter(totals[2], "blk", scatter_dimension=1, tiled=True),
        lax.psum_scatter(totals[3], "blk", scatter_dimension=1, tiled=True),
        lax.psum_scatter(totals[4], "blk", scatter_dimension=1, tiled=True),
        lax.psum_scatter(totals[5], "blk", scatter_dimension=1, tiled=True),
        lax.psum_scatter(totals[6], "blk", scatter_dimension=1, tiled=True),
        lax.psum_scatter(totals[7], "blk", scatter_dimension=1, tiled=True),
        lax.psum_scatter(totals[8], "blk", scatter_dimension=1, tiled=True),
        lax.psum_scatter(totals[9], "blk", scatter_dimension=1, tiled=True),
        lax.psum_scatter(totals[10], "blk", scatter_dimension=1, tiled=True),
        lax.psum_scatter(totals[11], "blk", scatter_dimension=1, tiled=True),
        lax.psum_scatter(totals[12], "blk", scatter_dimension=1, tiled=True),
        lax.psum_scatter(totals[13], "blk", scatter_dimension=1, tiled=True),
        lax.psum_scatter(totals[14], "blk", scatter_dimension=1, tiled=True),
    )
    matrix_sums = (
        lax.psum_scatter(narrowed[0], "dp", scatter_dimension=0, tiled=True),
        lax.psum_scatter(narrowed[1], "dp", scatter_dimension=0, tiled=True),
        lax.psum_scatter(narrowed[2], "dp", scatter_dimension=0, tiled=True),
        lax.psum_scatter(narrowed[3], "dp", scatter_dimension=0, tiled=True),
        lax.psum_scatter(narrowed[4], "dp", scatter_dimension=0, tiled=True),
        lax.psum_scatter(narrowed[5], "dp", scatter_dimension=0, tiled=True),
    )
    vector_sums = lax.psum(
        (
            narrowed[6],
            narrowed[7],
            narrowed[8],
            narrowed[9],
            narrowed[10],
            narrowed[11],
            narrowed[12],
            narrowed[13],
            narrowed[14],
        ),
        "dp",
    )
    return (
        jnp.stack(outputs),
        jnp.stack(input_grads),
        matrix_sums[0],
        vector_sums[0].reshape(-1),
        matrix_sums[1],
        matrix_sums[2],
        vector_sums[1].reshape(-1),
        matrix_sums[3],
        vector_sums[2].reshape(-1),
        vector_sums[3].reshape(-1),
        vector_sums[4].reshape(-1),
        matrix_sums[4],
        vector_sums[5].reshape(-1),
        matrix_sums[5],
        vector_sums[6].reshape(-1),
        vector_sums[7].reshape(-1),
        vector_sums[8].reshape(-1),
    )


def solution(mesh):
    in_specs = (
        P(None, "dp", "blk", None),
        P(None, "dp", "blk"),
        P("dp", "blk"),
        P("blk"),
        P("dp", "blk"),
        P("dp", "blk"),
        P("blk"),
        P("dp", "blk"),
        P("blk"),
        P("blk"),
        P("blk"),
        P("dp", "blk"),
        P("blk"),
        P("dp", "blk"),
        P("blk"),
        P("blk"),
        P("blk"),
        P(None, "dp", "blk", None),
    )
    out_specs = (
        P(None, "dp", "blk", None),
        P(None, "dp", "blk", None),
        P("dp", "blk"),
        P("blk"),
        P("dp", "blk"),
        P("dp", "blk"),
        P("blk"),
        P("dp", "blk"),
        P("blk"),
        P("blk"),
        P("blk"),
        P("dp", "blk"),
        P("blk"),
        P("dp", "blk"),
        P("blk"),
        P("blk"),
        P("blk"),
    )
    small = mesh.shape["dp"] == 4 and mesh.shape["blk"] == 8

    def on_device(*arrays):
        if small and arrays[0].shape == (4, 1, 128, 768):
            return rows_on_chips(*arrays)
        return general(*arrays)

    return jax.shard_map(
        on_device, mesh=mesh, in_specs=in_specs, out_specs=out_specs, check_vma=False
    )
```
